32 devices in a mesh: batch: 4 (over z), seq: 8 (over y, x, core).
Axes of the slice: x: 2, y: 2, z: 4, core: 2. Of those that a mesh axis runs over, the one named last changes fastest.
Arguments:
- tokens: bfloat16 [8, 4096, 768], P('batch', 'seq'), may hold values from -6 to 6
- sequence_lengths: int32 [8, 4], P('batch'), may hold values from 0 to 4096, as said below
- norm_gains: bfloat16 [2, 768], P(None, ('batch', 'seq')), may hold values from 0.099609375 to 1.8984375
- norm_shifts: bfloat16 [2, 768], P(None, ('batch', 'seq')), may hold values from -4 to 4
- mixing_weight: bfloat16 [768, 2304], P(('batch', 'seq')), may hold values from -0.21875 to 0.21875
- mixing_offset: bfloat16 [2304], P(('batch', 'seq')), may hold values from -1.5 to 1.5
- feature_maps: bfloat16 [768, 128], P(('batch', 'seq')), may hold values from -4 to 4
- output_weight: bfloat16 [768, 768], P(('batch', 'seq')), may hold values from -0.875 to 0.875
- branch_offsets: bfloat16 [2, 768], P(None, ('batch', 'seq')), may hold values from -4 to 4
- expand_weight: bfloat16 [768, 3072], P(('batch', 'seq')), may hold values from -0.21875 to 0.21875
- hidden_offset: bfloat16 [3072], P(('batch', 'seq')), may hold values from -4 to 4
- shrink_weight: bfloat16 [3072, 768], P(('batch', 'seq')), may hold values from -0.109375 to 0.109375
- cotangent: bfloat16 [8, 4096, 768], P('batch', 'seq'), may hold values from -6 to 6
Outputs:
- layer_output: bfloat16 [8, 4096, 768], P('batch', 'seq')
- input_gradient: bfloat16 [8, 4096, 768], P('batch', 'seq')
- gains_gradient: float32 [2, 768], P(None, ('batch', 'seq'))
- shifts_gradient: float32 [2, 768], P(None, ('batch', 'seq'))
- mixing_gradient: float32 [768, 2304], P(('batch', 'seq'))
- offset_gradient: float32 [2304], P(('batch', 'seq'))
- feature_gradient: float32 [768, 128], P(('batch', 'seq'))
- output_gradient: float32 [768, 768], P(('batch', 'seq'))
- branch_gradient: float32 [2, 768], P(None, ('batch', 'seq'))
- expand_gradient: float32 [768, 3072], P(('batch', 'seq'))
- hidden_gradient: float32 [3072], P(('batch', 'seq'))
- shrink_gradient: float32 [3072, 768], P(('batch', 'seq'))
The draws below stay inside these ranges and needn't reach their ends.
Inputs may be any that keep to these rules, and one draw needn't show every extreme that they name: `sequence_lengths`: each row lists its sequences' lengths in order, then zeros; the lengths sum to 4096 and each is 1024 or more and under 3 * 1024, except that among the 2 rows of each index of batch one row is a single sequence of 4096.
All inputs are finite; a program needn't handle non-finite values.
Results may differ from the reference program's by a relative error of at most 0.015.
Values may be sent and summed in bfloat16 or wider, within the bound.
No kernel may reach another device: no remote copies, remote signals or barrier semaphores. Data moves between devices by JAX's collectives and lax.ppermute only.
A program may use at most 256 MiB of HBM per device.

```python
import jax
import jax.numpy as jnp
from jax import lax

D = 768
H = 12
HD = 64
FF = 3072
TOK_DEV = 512
ROWS_DEV = 2
SEQLEN = 4096
BROWS = 8
SHORTEST = 1024
NSEQ = 4


def draw_sequence_lengths(key, part):
    key = jax.random.fold_in(key, 11)
    length_key = jax.random.fold_in(key, 1)
    row_key = jax.random.fold_in(key, 2)
    raw_lengths = jax.random.randint(length_key, (BROWS, NSEQ), SHORTEST, 2 * SHORTEST + 1)
    endings = jnp.cumsum(raw_lengths, axis=1)
    inside = endings <= SEQLEN - SHORTEST
    kept_count = jnp.sum(inside.astype(jnp.int32), axis=1, keepdims=True)
    slot_ids = jnp.arange(NSEQ, dtype=jnp.int32)[None, :]
    covered = jnp.sum(jnp.where(inside, raw_lengths, 0), axis=1, keepdims=True)
    packed = jnp.where(inside, raw_lengths, jnp.where(slot_ids == kept_count, SEQLEN - covered, 0))
    chosen = jax.random.randint(row_key, (BROWS // ROWS_DEV,), 0, ROWS_DEV)
    rows_index = jnp.arange(BROWS, dtype=jnp.int32)
    single = rows_index % ROWS_DEV == jnp.repeat(chosen, ROWS_DEV)
    whole_row = jnp.where(slot_ids == 0, SEQLEN, 0)
    return jnp.where(single[:, None], whole_row, packed).astype(jnp.int32)


def raised(array, stream_key, source, target, blocks, factor):
    def block_of(position):
        return (jnp.arange(array.shape[position]) // (array.shape[position] // blocks)).reshape((-1,) + (1,) * (array.ndim - 1 - position))

    near = jax.random.permutation(stream_key, blocks)[block_of(target)]
    other_side = (block_of(target) + blocks // 2) % blocks
    return jnp.where((block_of(source) == near) | (block_of(source) == other_side), factor * array, array)


def levels(own_key, dims, cuts, least, largest):
    def one(axis_at, shards_of):
        heights = jax.random.uniform(jax.random.fold_in(jax.random.fold_in(own_key, 6), axis_at), (shards_of,), jnp.float32, least / len(cuts), largest / len(cuts))
        return jnp.repeat(jnp.exp(heights), dims[axis_at] // shards_of).reshape((-1,) + (1,) * (len(dims) - axis_at - 1))

    loudness = one(*cuts[0])
    for cut in cuts[1:]:
        loudness = loudness * one(*cut)
    return loudness


def bell_draw(key, dims, deviation, reach, cuts=(), kind=jnp.bfloat16):
    entries = jax.random.normal(key, dims, jnp.float32) * deviation
    if len(cuts) > 0:
        entries = levels(key, dims, cuts, -0.22, 0.18) * entries
    return jnp.clip(entries, min=-reach, max=reach).astype(kind)


def bell_draw_with(stream_key, dims, scale, limit, cuts, heavy, held_as=jnp.bfloat16):
    entries = scale * jax.random.normal(stream_key, dims, jnp.float32)
    if cuts:
        entries = entries * levels(stream_key, dims, cuts, -0.22, 0.18)
    return jnp.clip(raised(entries, jax.random.fold_in(stream_key, 3), *heavy), -limit, limit).astype(held_as)


def setup_inputs(seed: int = 0) -> dict:
    streams_of = jax.random.split(jax.random.key(seed), 14)
    return {
        "tokens": bell_draw(streams_of[0], (BROWS, SEQLEN, D), 1.0, 6.0, ((0, 4), (1, 8))),
        "sequence_lengths": draw_sequence_lengths(jax.random.fold_in(streams_of[13], 71), 0),
        "norm_gains": jnp.clip(1.0 + 0.18 * jax.random.normal(streams_of[2], (2, D), jnp.float32), 0.099609375, 1.8984375).astype(jnp.bfloat16),
        "norm_shifts": bell_draw(streams_of[3], (2, D), 0.3, 4.0, ((1, 32),)),
        "mixing_weight": bell_draw(streams_of[4], (D, 3 * D), D ** -0.5, 0.21875, ((0, 32),)),
        "mixing_offset": bell_draw(streams_of[5], (3 * D,), 0.1, 1.5, ((0, 32),)),
        "feature_maps": bell_draw(streams_of[6], (D, 2 * HD), 0.3, 4.0, ((0, 32),)),
        "output_weight": bell_draw(streams_of[7], (D, D), (D // 16) ** -0.5, 0.875, ((0, 32),)),
        "branch_offsets": bell_draw(streams_of[8], (2, D), 0.3, 4.0, ((1, 32),)),
        "expand_weight": bell_draw(streams_of[9], (D, FF), D ** -0.5, 0.21875, ((0, 32),)),
        "hidden_offset": bell_draw(streams_of[10], (FF,), 0.3, 4.0, ((0, 32),)),
        "shrink_weight": bell_draw(streams_of[11], (FF, D), FF ** -0.5, 0.109375, ((0, 32),)),
        "cotangent": bell_draw_with(streams_of[12], (BROWS, SEQLEN, D), 1.0, 6.0, ((0, 4), (1, 8)), (1, 2, 8, 2.0)),
    }


EPSILON = 1e-05
PRECISE = lax.Precision.HIGHEST

@jax.custom_vjp
def low(v):
    return lax.optimization_barrier(v.astype(jnp.bfloat16)).astype(jnp.float32)

@jax.custom_vjp
def low_back(v):
    return v

def low_keep(v):
    return (low(v), None)

def low_pass(kept, grad):
    return (grad,)

def back_keep(v):
    return (v, None)

def back_low(kept, grad):
    return (low(grad),)
low.defvjp(low_keep, low_pass)
low_back.defvjp(back_keep, back_low)

def layer_norm(values, gain_row, shift_row):
    center = lax.optimization_barrier(jnp.mean(values, axis=-1, keepdims=True))
    centered = values - center
    spread = lax.optimization_barrier(jnp.mean(centered * centered, axis=-1, keepdims=True))
    return centered * lax.rsqrt(spread + EPSILON) * gain_row + shift_row

def feature_map(logits):
    return jnp.concatenate([jax.nn.softmax(logits, axis=-1), jax.nn.softmax(-logits, axis=-1)], axis=-1)

def reference(tokens, sequence_lengths, norm_gains, norm_shifts, mixing_weight, mixing_offset, feature_maps, output_weight, branch_offsets, expand_weight, hidden_offset, shrink_weight, cotangent):
    starts = jnp.cumsum(sequence_lengths, axis=1) - sequence_lengths
    places = jnp.arange(SEQLEN, dtype=jnp.int32)
    doc_ids = lax.optimization_barrier(jnp.sum((starts[:, None, :] <= places[None, :, None]).astype(jnp.int32), axis=2))
    block_count = SEQLEN // TOK_DEV
    block_edges = jnp.arange(block_count, dtype=jnp.int32) * TOK_DEV - 1
    before = lax.optimization_barrier(jnp.sum((starts[:, None, :] <= block_edges[None, :, None]).astype(jnp.int32), axis=2))
    causal = jnp.arange(TOK_DEV)[None, :] <= jnp.arange(TOK_DEV)[:, None]

    def blocked(tensor):
        return jnp.moveaxis(tensor.reshape((BROWS, block_count, TOK_DEV) + tensor.shape[2:]), 1, 0)

    @jax.checkpoint
    def block_step(carried, pieces):
        memory, key_memory = carried
        query_block, key_block, value_block, doc_block, doc_before = pieces
        allowed = ((doc_block[:, :, None] == doc_block[:, None, :]) & causal[None]).astype(jnp.float32)
        scores = low_back(jnp.einsum('bihf,bjhf->bhij', query_block, key_block, precision=PRECISE) * allowed[:, None])
        carry_mask = (doc_block == doc_before[:, None]).astype(jnp.float32)
        numerator = low_back(jnp.einsum('bhij,bjhe->bihe', low(scores), value_block, precision=PRECISE) + carry_mask[:, :, None, None] * jnp.einsum('bihf,bhfe->bihe', query_block, memory, precision=PRECISE))
        denominator = jnp.moveaxis(lax.optimization_barrier(jnp.sum(scores, axis=3)), 1, 2) + carry_mask[:, :, None] * jnp.einsum('bihf,bhf->bih', query_block, key_memory, precision=PRECISE)
        last_mask = (doc_block == doc_block[:, -1:]).astype(jnp.float32)
        state_sum = jnp.einsum('bjhf,bjhe->bhfe', key_block * last_mask[:, :, None, None], value_block, precision=PRECISE)
        key_sum = jnp.einsum('bjhf,bj->bhf', key_block, last_mask, precision=PRECISE)
        retained = 1.0 - (doc_block[:, -1] != doc_before).astype(jnp.float32)
        updated = (state_sum + retained[:, None, None, None] * memory, key_sum + retained[:, None, None] * key_memory)
        return (updated, numerator / denominator[:, :, :, None])

    def linear_attention(phi_query, phi_key, values):
        initial = (jnp.zeros((BROWS, H, 2 * HD, HD), jnp.float32), jnp.zeros((BROWS, H, 2 * HD), jnp.float32))
        pieces = (blocked(phi_query), blocked(phi_key), blocked(values), blocked(doc_ids), jnp.moveaxis(before, 1, 0))
        _, outputs = lax.scan(block_step, initial, pieces)
        return jnp.moveaxis(outputs, 0, 1).reshape(BROWS, SEQLEN, H, HD)

    def forward(inputs, gain_rows, shift_rows, mixing, offset_mix, maps, out_weight, branch_rows, expand, hidden_bias, shrink):
        normed_in = low(layer_norm(inputs, gain_rows[0], shift_rows[0]))
        projected = low(low_back(jnp.einsum('btd,de->bte', normed_in, mixing, precision=PRECISE) + offset_mix))
        separated = projected.reshape(BROWS, SEQLEN, 3, H, HD)
        queries = separated[:, :, 0]
        keys_all = separated[:, :, 1]
        values = separated[:, :, 2]
        layout = maps.reshape(H, HD, 2, HD)
        query_logits = low_back(jnp.einsum('bthd,hde->bthe', queries, layout[:, :, 0], precision=PRECISE))
        key_logits = low_back(jnp.einsum('bthd,hde->bthe', keys_all, layout[:, :, 1], precision=PRECISE))
        phi_query = low(feature_map(query_logits))
        phi_key = low(feature_map(key_logits))
        attended = low(linear_attention(phi_query, phi_key, values).reshape(BROWS, SEQLEN, D))
        branch = low_back(jnp.einsum('bti,io->bto', attended, out_weight, precision=PRECISE) + branch_rows[0])
        middle = inputs + branch
        normed_mid = low(layer_norm(middle, gain_rows[1], shift_rows[1]))
        preact = low_back(jnp.einsum('btd,df->btf', normed_mid, expand, precision=PRECISE) + hidden_bias)
        hidden = low(jax.nn.gelu(preact, approximate=True))
        return middle + jnp.einsum('btf,fd->btd', hidden, shrink, precision=PRECISE) + branch_rows[1]
    primal = (tokens, norm_gains, norm_shifts, mixing_weight, mixing_offset, feature_maps, output_weight, branch_offsets, expand_weight, hidden_offset, shrink_weight)
    primal = tuple((entry.astype(jnp.float32) for entry in primal))
    layer_output, pullback = jax.vjp(forward, *primal)
    gradients = pullback(cotangent.astype(jnp.float32))
    return (layer_output.astype(jnp.bfloat16), gradients[0].astype(jnp.bfloat16), gradients[1], gradients[2], gradients[3], gradients[4], gradients[5], gradients[6], gradients[7], gradients[8], gradients[9], gradients[10])
```

```python
import functools

import jax
import jax.numpy as jnp
from jax import lax
from jax.experimental import pallas as pl
from jax.experimental.pallas import tpu as pltpu
from jax.sharding import PartitionSpec as P

HD = 64
F = 2 * HD
PAIR = 2 * HD
SUB = 256
WIRE = F + 16
EPSILON = 1e-05
AXES = ("batch", "seq")
VMEM = 56 * 1024 * 1024
bf16 = jnp.bfloat16
f32 = jnp.float32


def dot(a, b, left, right):
    return lax.dot_general(a, b, (((left,), (right,)), ((), ())), preferred_element_type=f32)


def nn(a, b):
    return dot(a, b, 1, 0)


def nt(a, b):
    return dot(a, b, 1, 1)


def tn(a, b):
    return dot(a, b, 0, 0)


def lane(shape):
    return lax.broadcasted_iota(jnp.int32, shape, len(shape) - 1)


def sublane(shape):
    return lax.broadcasted_iota(jnp.int32, shape, len(shape) - 2)


def normalize(values):
    center = jnp.mean(values, axis=-1, keepdims=True)
    centered = values - center
    spread = jnp.mean(centered * centered, axis=-1, keepdims=True)
    scale = lax.rsqrt(spread + EPSILON)
    return centered * scale, scale


def normalize_back(upstream, xhat, scale, gain):
    entry = upstream * gain
    first = jnp.mean(entry, axis=-1, keepdims=True)
    second = jnp.mean(entry * xhat, axis=-1, keepdims=True)
    return scale * (entry - first - xhat * second)


def map_weight(rows, keys):
    rows = rows.astype(f32)
    turned = pltpu.roll(rows, HD, 1)
    low = lane(rows.shape) < HD
    signed = jnp.where(low, turned, -rows) if keys else jnp.where(low, rows, -turned)
    top = sublane(rows.shape) < HD
    return jnp.concatenate(
        [jnp.where(top, signed, 0.0), jnp.where(top, 0.0, signed)], axis=1
    ).astype(bf16)


def segment_ones(width):
    shape = (width, width)
    return (lane(shape) // HD == sublane(shape) // HD).astype(bf16)


def segment_sum(values, ones):
    high = values.astype(bf16)
    low = (values - high.astype(f32)).astype(bf16)
    return nn(high, ones) + nn(low, ones)


def features(logits, ones):
    parts = []
    for at in range(0, logits.shape[1], F):
        part = logits[:, at : at + F]
        low = lane(part.shape) < HD
        first = jnp.max(jnp.where(low, part, -jnp.inf), axis=1, keepdims=True)
        second = jnp.max(jnp.where(low, -jnp.inf, part), axis=1, keepdims=True)
        parts.append(jnp.exp(part - jnp.where(low, first, second)))
    powers = jnp.concatenate(parts, axis=1)
    return powers / nn(powers.astype(bf16), ones)


def features_back(phi, upstream, ones):
    phi = phi.astype(f32)
    return phi * (upstream - segment_sum(phi * upstream, ones))


def with_aux(pair, head, aux):
    own = (lane(pair.shape) < HD) if head == 0 else (lane(pair.shape) >= HD)
    return jnp.where(own, pair, aux)


def pair_rows(first, second):
    top = sublane(first.shape) < HD
    return jnp.where(top, first, second)


def put_wire(ref, at, first, second, aux_rows):
    ref[0, at, 0:F, :] = pair_rows(first, second).astype(bf16)
    sums = [sum(x[a : a + 1] for a in rows) for x, rows in zip((first, second), aux_rows)]
    row = sublane((16, F))
    ref[0, at, F:WIRE, :] = jnp.where(
        row == 0, sums[0], jnp.where(row == 1, sums[1], 0.0)
    ).astype(bf16)


def take_wire(ref, at):
    state = ref[0, at, 0:F, :]
    sums = ref[0, at, F:WIRE, :]
    top = sublane(state.shape) < HD
    return jnp.where(top, state, sums[0:1]), jnp.where(top, sums[1:2], state)


def block_masks(split, count, flipped):
    masks = {}
    for ib in range(count):
        for jb in range(ib + 1):
            shape = (SUB, SUB)
            i = (lane(shape) if flipped else sublane(shape)) + ib * SUB
            j = (sublane(shape) if flipped else lane(shape)) + jb * SUB
            mask = (i < split) | (j >= split)
            if ib == jb:
                mask = mask & (j <= i)
            masks[ib, jb] = mask
    return masks


def keys_kernel(
    split_ref, tok, gain, shift, wk, wv, ok, ov, maps, normed_o, k_o, v_o, phi_o, wire_o, kept
):
    row, quad = pl.program_id(0), pl.program_id(1)

    @pl.when(quad == 0)
    def _():
        xhat, _ = normalize(tok[...].astype(f32))
        normed = (xhat * gain[...] + shift[...]).astype(bf16)
        kept[...] = normed
        normed_o[...] = normed

    normed = kept[...]
    keys = (nn(normed, wk[...]) + ok[...]).astype(bf16)
    values = (nn(normed, wv[...]) + ov[...]).astype(bf16)
    k_o[...] = keys
    v_o[...] = values
    count = keys.shape[0]
    split = split_ref[row]
    begin = jnp.where(split < count, split, 0)
    last = sublane((count, PAIR)) >= begin
    ones = segment_ones(2 * F)
    for p in range(2):
        at = slice(p * PAIR, (p + 1) * PAIR)
        phi = features(nn(keys[:, at], map_weight(maps[at, :], True)), ones).astype(bf16)
        phi_o[:, 2 * p * F : 2 * (p + 1) * F] = phi
        pair = values[:, at].astype(f32)
        sums = [
            tn(
                jnp.where(last, with_aux(pair, h, 1.0), 0.0).astype(bf16),
                phi[:, h * F : (h + 1) * F],
            )
            for h in range(2)
        ]
        put_wire(wire_o, p, sums[0], sums[1], ((HD,), (0,)))


def local_kernel(split_ref, normed, wq, oq, maps, phi_key, val, q_o, phi_o, num_o):
    row = pl.program_id(0)
    queries = (nn(normed[...], wq[...]) + oq[...]).astype(bf16)
    q_o[...] = queries
    count = queries.shape[0]
    split = split_ref[row]
    blocks = count // SUB
    masks = block_masks(split, blocks, False)
    ones = segment_ones(2 * F)
    for p in range(2):
        at = slice(p * PAIR, (p + 1) * PAIR)
        phi = features(nn(queries[:, at], map_weight(maps[at, :], False)), ones).astype(bf16)
        phi_o[:, 2 * p * F : 2 * (p + 1) * F] = phi
        pair = val[:, at].astype(f32)
        for h in range(2):
            column = slice((2 * p + h) * F, (2 * p + h + 1) * F)
            query = phi[:, h * F : (h + 1) * F]
            key = phi_key[:, column]
            extended = with_aux(pair, h, 1.0).astype(bf16)
            for ib in range(blocks):
                rows = slice(ib * SUB, (ib + 1) * SUB)
                total = None
                for jb in range(ib + 1):
                    others = slice(jb * SUB, (jb + 1) * SUB)
                    scores = nt(query[rows], key[others])
                    scores = jnp.where(masks[ib, jb], scores, 0.0).astype(bf16)
                    part = nn(scores, extended[others])
                    total = part if total is None else total + part
                num_o[rows, column] = total


def middle_kernel(
    split_ref, num, phi_query, wire, tok, wo, bias, gain, shift, att_o, rden_o, mid_o, normed_o
):
    row = pl.program_id(0)
    count = num.shape[0]
    carry = sublane((count, F)) < split_ref[row]
    for p in range(wire.shape[1]):
        sums = []
        for h, memory in enumerate(take_wire(wire, p)):
            column = slice((2 * p + h) * F, (2 * p + h + 1) * F)
            sums.append(
                num[:, column] + jnp.where(carry, nt(phi_query[:, column], memory), 0.0)
            )
        low = lane((count, PAIR)) < HD
        numerator = jnp.where(low, sums[0], sums[1])
        denominator = pltpu.roll(jnp.where(low, sums[1], sums[0]), HD, 1)
        inverse = 1.0 / denominator
        at = slice(p * PAIR, (p + 1) * PAIR)
        rden_o[:, at] = inverse
        att_o[:, at] = (numerator * inverse).astype(bf16)
    middle = tok[...].astype(f32) + nn(att_o[...], wo[...]) + bias[...]
    mid_o[...] = middle
    xhat, _ = normalize(middle)
    normed_o[...] = (xhat * gain[...] + shift[...]).astype(bf16)


def mlp_kernel(normed, cot, ex, sh, bias, y_o, back_o, eg_o, sg_o, bg_o, turned):
    step = pl.program_id(0)

    @pl.when(step == 0)
    def _():
        turned[...] = normed[...].T
        y_o[...] = jnp.zeros_like(y_o)
        back_o[...] = jnp.zeros_like(back_o)

    slope = 0.7978845608028654
    cubic = 0.044715
    pre = nn(normed[...], ex[...]) + bias[...]
    square = pre * pre
    bend = jnp.tanh(slope * (pre + cubic * pre * square))
    hidden = (0.5 * pre * (1.0 + bend)).astype(bf16)
    rise = 0.5 * (1.0 + bend) + 0.5 * pre * (1.0 - bend * bend) * slope * (
        1.0 + 3.0 * cubic * square
    )
    back = (nt(cot[...], sh[...]) * rise).astype(bf16)
    bg_o[...] = jnp.sum(back.astype(f32), axis=0, keepdims=True)
    y_o[...] += nn(hidden, sh[...])
    back_o[...] += nt(back, ex[...])
    sg_o[...] = tn(hidden, cot[...])
    eg_o[...] = nn(turned[...], back)


def column_sum(values):
    return jnp.sum(values, axis=0, keepdims=True)


def middle_back_kernel(
    split_ref,
    mid,
    y,
    back,
    cot,
    att,
    rden,
    phi_query,
    wo,
    gain,
    bias,
    out_o,
    mb_o,
    ext_o,
    wire_o,
    og_o,
    small_o,
):
    row = pl.program_id(0)

    @pl.when(row == 0)
    def _():
        og_o[...] = jnp.zeros_like(og_o)
        small_o[...] = jnp.zeros_like(small_o)

    middle = mid[...]
    upstream = cot[...].astype(f32)
    out_o[...] = (middle + y[...] + bias[...]).astype(bf16)
    xhat, scale = normalize(middle)
    from_norm = back[...]
    middle_back = upstream + normalize_back(from_norm, xhat, scale, gain[...])
    mb_o[...] = middle_back
    branch_back = middle_back.astype(bf16)
    small_o[0:1, :] += column_sum(from_norm * xhat)
    small_o[1:2, :] += column_sum(from_norm)
    small_o[2:3, :] += column_sum(branch_back.astype(f32))
    small_o[3:4, :] += column_sum(upstream)
    og_o[...] += tn(att[...], branch_back)
    attended_back = nt(branch_back, wo[...])
    count = middle.shape[0]
    carry = sublane((count, F)) < split_ref[row]
    ones = segment_ones(PAIR)
    spot = lane((count, PAIR))
    for p in range(wire_o.shape[1]):
        at = slice(p * PAIR, (p + 1) * PAIR)
        given = attended_back[:, at]
        inverse = rden[:, at]
        numerator_back = given * inverse
        denominator_back = -segment_sum(given * att[:, at].astype(f32), ones) * inverse
        aux = pltpu.roll(denominator_back, HD, 1)
        high = aux.astype(bf16).astype(f32)
        rest = aux - high
        sums = []
        for h in range(2):
            first = HD if h == 0 else 0
            extended = with_aux(
                numerator_back,
                h,
                jnp.where(spot == first, high, jnp.where(spot == first + 1, rest, 0.0)),
            ).astype(bf16)
            column = slice((2 * p + h) * F, (2 * p + h + 1) * F)
            ext_o[:, column] = extended
            query = jnp.where(carry, phi_query[:, column].astype(f32), 0.0).astype(bf16)
            sums.append(tn(extended, query))
        put_wire(wire_o, p, sums[0], sums[1], ((HD, HD + 1), (0, 1)))


def map_gradient(pair, logits_back):
    both = tn(pair, logits_back)
    rows = pair_rows(both[:, :F], both[:, F:])
    return rows - pltpu.roll(rows, HD, 1)


def local_back_kernel(
    split_ref, phi_query, phi_key, val, ext, wire, queries, maps, pq_o, mg_o, kg_o, vg_o
):
    row = pl.program_id(1)
    count = val.shape[0]
    split = split_ref[row]
    blocks = count // SUB
    masks = block_masks(split, blocks, False)
    flipped = block_masks(split, blocks, True)
    carry = sublane((count, F)) < split
    ones = segment_ones(2 * F)
    pair = val[...].astype(f32)
    memories = take_wire(wire, 0)
    grads, tops = [], []
    for h in range(2):
        column = slice(h * F, (h + 1) * F)
        query, key, given = phi_query[:, column], phi_key[:, column], ext[:, column]
        extended = with_aux(pair, h, 1.0).astype(bf16)
        query_grad = [None] * blocks
        key_grad = [None] * blocks
        value_grad = [None] * blocks

        def add(into, at, part):
            into[at] = part if into[at] is None else into[at] + part

        for ib in range(blocks):
            rows = slice(ib * SUB, (ib + 1) * SUB)
            for jb in range(ib + 1):
                others = slice(jb * SUB, (jb + 1) * SUB)
                turned = jnp.where(flipped[ib, jb], nt(key[others], query[rows]), 0.0)
                add(value_grad, jb, nn(turned.astype(bf16), given[rows]))
                turned = jnp.where(flipped[ib, jb], nt(extended[others], given[rows]), 0.0)
                add(key_grad, jb, nn(turned.astype(bf16), query[rows]))
                straight = jnp.where(masks[ib, jb], nt(given[rows], extended[others]), 0.0)
                add(query_grad, ib, nn(straight.astype(bf16), key[others]))
        kg_o[:, column] = jnp.concatenate(key_grad, axis=0)
        tops.append(jnp.concatenate(value_grad, axis=0))
        grads.append(
            jnp.concatenate(query_grad, axis=0)
            + jnp.where(carry, nn(given, memories[h]), 0.0)
        )
    vg_o[...] = jnp.where(lane(pair.shape) < HD, tops[0], tops[1])
    logits_back = features_back(phi_query[...], jnp.concatenate(grads, axis=1), ones).astype(bf16)
    pq_o[...] = nt(logits_back, map_weight(maps[...], False)).astype(bf16)
    gradient = map_gradient(queries[...], logits_back)

    @pl.when(row == 0)
    def _():
        mg_o[...] = gradient

    @pl.when(row > 0)
    def _():
        mg_o[...] += gradient


def keys_back_kernel(
    split_ref, kg, vg, phi_key, val, wire, keys, maps, from_queries, pk_o, pv_o, mg_o
):
    row = pl.program_id(1)
    count = val.shape[0]
    split = split_ref[row]
    begin = jnp.where(split < count, split, 0)
    last = sublane((count, F)) >= begin
    ones = segment_ones(2 * F)
    pair = val[...].astype(f32)
    state = wire[0, 0, 0:F, :]
    spot = sublane(state.shape)
    grads, tops = [], []
    for h, memory in enumerate(take_wire(wire, 0)):
        column = slice(h * F, (h + 1) * F)
        first = HD if h == 0 else 0
        own = (spot < HD) if h == 0 else (spot >= HD)
        memory = jnp.where(own | (spot == first), memory.astype(f32), 0.0).astype(bf16)
        extended = with_aux(pair, h, 1.0).astype(bf16)
        grads.append(kg[:, column] + jnp.where(last, nn(extended, memory), 0.0))
        tops.append(nt(phi_key[:, column], state))
    low = lane(pair.shape) < HD
    pv_o[...] = (vg[...] + jnp.where(last, jnp.where(low, tops[0], tops[1]), 0.0)).astype(bf16)
    logits_back = features_back(phi_key[...], jnp.concatenate(grads, axis=1), ones).astype(bf16)
    pk_o[...] = nt(logits_back, map_weight(maps[...], True)).astype(bf16)
    gradient = pltpu.roll(map_gradient(keys[...], logits_back), HD, 1)

    @pl.when(row == 0)
    def _():
        mg_o[...] = jnp.where(lane(gradient.shape) < HD, from_queries[...], gradient)

    @pl.when(row > 0)
    def _():
        mg_o[...] += jnp.where(lane(gradient.shape) < HD, 0.0, gradient)


def weight_back_kernel(normed, pb, wg_o, bg_o, turned):
    @pl.when(pl.program_id(0) == 0)
    def _():
        turned[...] = normed[...].T

    wg_o[...] = nn(turned[...], pb[...])
    bg_o[...] = column_sum(pb[...].astype(f32))


def input_back_kernel(pq, pk, pv, wq, wk, wv, tok, mb, gain, out_o, small_o):
    @pl.when(pl.program_id(0) == 0)
    def _():
        small_o[...] = jnp.zeros_like(small_o)

    from_norm = nt(pq[...], wq[...]) + nt(pk[...], wk[...]) + nt(pv[...], wv[...])
    xhat, scale = normalize(tok[...].astype(f32))
    small_o[0:1, :] += column_sum(from_norm * xhat)
    small_o[1:2, :] += column_sum(from_norm)
    out_o[...] = (mb[...] + normalize_back(from_norm, xhat, scale, gain[...])).astype(bf16)


def spec(shape, index):
    return pl.BlockSpec(shape, index)


def call(kernel, grid, ins, outs, scratch=(), scalars=0, name=None):
    arrays = [entry[0] for entry in ins[scalars:]]
    fetched = [entry[0] for entry in ins[:scalars]]
    return pl.pallas_call(
        kernel,
        out_shape=[jax.ShapeDtypeStruct(shape, kind) for shape, kind, _, _ in outs],
        grid_spec=pltpu.PrefetchScalarGridSpec(
            num_scalar_prefetch=scalars,
            grid=grid,
            in_specs=[spec(block, index) for _, block, index in ins[scalars:]],
            out_specs=[spec(block, index) for _, _, block, index in outs],
            scratch_shapes=list(scratch),
        ),
        compiler_params=pltpu.CompilerParams(vmem_limit_bytes=VMEM),
        name=name,
    )(*fetched, *arrays)


def gather_rows(part):
    return lax.all_gather(part, AXES, axis=0, tiled=True)


def scatter_rows(whole):
    return lax.psum_scatter(whole, AXES, scatter_dimension=0, tiled=True)


def any_start(starts, low, high):
    return jnp.any((starts >= low) & (starts <= high), axis=1)


def carried(wire, starts, tok_count, reverse):
    size, mine = lax.axis_size("seq"), lax.axis_index("seq")
    total, reached = wire, jnp.zeros_like(wire)
    span = 1
    while span < size:
        other = lax.ppermute(total, "seq", [(i, i ^ span) for i in range(size)])
        group = mine // span
        upper = group % 2 == 1
        begin = group * span
        if reverse:
            receives = jnp.logical_not(upper)
            closed = any_start(starts, (mine + 1) * tok_count, (begin + span) * tok_count - 1)
            own_closed = any_start(starts, begin * tok_count, (begin + span) * tok_count - 1)
            other_begin = (begin - span) * tok_count
            other_closed = any_start(starts, other_begin, begin * tok_count - 1)
        else:
            receives = upper
            closed = any_start(starts, begin * tok_count, mine * tok_count - 1)
            own_closed = any_start(starts, begin * tok_count, (begin + span) * tok_count - 1)
            other_begin = (begin + span) * tok_count
            other_closed = any_start(starts, other_begin, other_begin + span * tok_count - 1)
        open_here = (receives & jnp.logical_not(closed))[:, None, None, None]
        reached = reached + jnp.where(open_here, other, 0)
        own_on = jnp.where(receives, True, jnp.logical_not(other_closed))[:, None, None, None]
        other_on = jnp.where(receives, jnp.logical_not(own_closed), True)[:, None, None, None]
        total = jnp.where(own_on, total, 0) + jnp.where(other_on, other, 0)
        span *= 2
    return reached


def local(
    tokens,
    sequence_lengths,
    norm_gains,
    norm_shifts,
    mixing_weight,
    mixing_offset,
    feature_maps,
    output_weight,
    branch_offsets,
    expand_weight,
    hidden_offset,
    shrink_weight,
    cotangent,
):
    row_count, tok_count, width = tokens.shape
    count = row_count * tok_count
    heads = width // HD
    pairs, quads = heads // 2, heads // 4
    quad = 2 * PAIR
    hidden_width = expand_weight.shape[1]

    gains = lax.all_gather(norm_gains, AXES, axis=1, tiled=True).astype(f32)
    shifts = lax.all_gather(norm_shifts, AXES, axis=1, tiled=True).astype(f32)
    branches = lax.all_gather(branch_offsets, AXES, axis=1, tiled=True).astype(f32)
    offset = gather_rows(mixing_offset).astype(f32)[None]
    hidden_bias = gather_rows(hidden_offset).astype(f32)[None]
    maps = gather_rows(feature_maps)
    mixing = gather_rows(mixing_weight)
    out_weight = gather_rows(output_weight)
    expand = gather_rows(expand_weight)
    shrink = gather_rows(shrink_weight)

    place = lax.axis_index("seq") * tok_count
    starts = jnp.cumsum(sequence_lengths, axis=1) - sequence_lengths
    inside = (starts >= place) & (starts < place + tok_count)
    split = jnp.min(jnp.where(inside, starts - place, tok_count), axis=1).astype(jnp.int32)

    tok = tokens.reshape(count, width)
    cot = cotangent.reshape(count, width)
    full = lambda r, q, s: (0, 0)
    rows_ = lambda r, q, s: (r, 0)
    both = lambda r, q, s: (r, q)

    def columns(first):
        return lambda r, q, s: (0, first + q)

    normed, keys, values, phi_key, wire = call(
        keys_kernel,
        (row_count, quads),
        [
            (split, None, None),
            (tok, (tok_count, width), rows_),
            (gains[0:1], (1, width), full),
            (shifts[0:1], (1, width), full),
            (mixing, (width, quad), columns(quads)),
            (mixing, (width, quad), columns(2 * quads)),
            (offset, (1, quad), columns(quads)),
            (offset, (1, quad), columns(2 * quads)),
            (maps, (quad, F), lambda r, q, s: (q, 0)),
        ],
        [
            ((count, width), bf16, (tok_count, width), rows_),
            ((count, width), bf16, (tok_count, quad), both),
            ((count, width), bf16, (tok_count, quad), both),
            ((count, heads * F), bf16, (tok_count, 4 * F), both),
            ((row_count, pairs, WIRE, F), bf16, (1, 2, WIRE, F), lambda r, q, s: (r, q, 0, 0)),
        ],
        [pltpu.VMEM((tok_count, width), bf16)],
        1,
        "keys",
    )
    memory = carried(wire, starts, tok_count, False)
    queries, phi_query, numerator = call(
        local_kernel,
        (row_count, quads),
        [
            (split, None, None),
            (normed, (tok_count, width), rows_),
            (mixing, (width, quad), columns(0)),
            (offset, (1, quad), columns(0)),
            (maps, (quad, F), lambda r, q, s: (q, 0)),
            (phi_key, (tok_count, 4 * F), both),
            (values, (tok_count, quad), both),
        ],
        [
            ((count, width), bf16, (tok_count, quad), both),
            ((count, heads * F), bf16, (tok_count, 4 * F), both),
            ((count, heads * F), f32, (tok_count, 4 * F), both),
        ],
        [],
        1,
        "local_attention",
    )
    one = lambda r, s: (r, 0)
    whole = lambda r, s: (0, 0)
    attended, inverse, middle, normed_mid = call(
        middle_kernel,
        (row_count,),
        [
            (split, None, None),
            (numerator, (tok_count, heads * F), one),
            (phi_query, (tok_count, heads * F), one),
            (memory, (1, pairs, WIRE, F), lambda r, s: (r, 0, 0, 0)),
            (tok, (tok_count, width), one),
            (out_weight, (width, width), whole),
            (branches[0:1], (1, width), whole),
            (gains[1:2], (1, width), whole),
            (shifts[1:2], (1, width), whole),
        ],
        [
            ((count, width), bf16, (tok_count, width), one),
            ((count, width), f32, (tok_count, width), one),
            ((count, width), f32, (tok_count, width), one),
            ((count, width), bf16, (tok_count, width), one),
        ],
        [],
        1,
        "middle",
    )
    tile = 512
    y, normed_mid_back, expand_grad, shrink_grad, hidden_grad = call(
        mlp_kernel,
        (hidden_width // tile,),
        [
            (normed_mid, (count, width), lambda f: (0, 0)),
            (cot, (count, width), lambda f: (0, 0)),
            (expand, (width, tile), lambda f: (0, f)),
            (shrink, (tile, width), lambda f: (f, 0)),
            (hidden_bias, (1, tile), lambda f: (0, f)),
        ],
        [
            ((count, width), f32, (count, width), lambda f: (0, 0)),
            ((count, width), f32, (count, width), lambda f: (0, 0)),
            ((width, hidden_width), f32, (width, tile), lambda f: (0, f)),
            ((hidden_width, width), f32, (tile, width), lambda f: (f, 0)),
            ((1, hidden_width), f32, (1, tile), lambda f: (0, f)),
        ],
        [pltpu.VMEM((width, count), bf16)],
        0,
        "mlp",
    )
    layer_output, middle_back, extended, wire_back, output_grad, small_mid = call(
        middle_back_kernel,
        (row_count,),
        [
            (split, None, None),
            (middle, (tok_count, width), one),
            (y, (tok_count, width), one),
            (normed_mid_back, (tok_count, width), one),
            (cot, (tok_count, width), one),
            (attended, (tok_count, width), one),
            (inverse, (tok_count, width), one),
            (phi_query, (tok_count, heads * F), one),
            (out_weight, (width, width), whole),
            (gains[1:2], (1, width), whole),
            (branches[1:2], (1, width), whole),
        ],
        [
            ((count, width), bf16, (tok_count, width), one),
            ((count, width), f32, (tok_count, width), one),
            ((count, heads * F), bf16, (tok_count, heads * F), one),
            ((row_count, pairs, WIRE, F), bf16, (1, pairs, WIRE, F), lambda r, s: (r, 0, 0, 0)),
            ((width, width), f32, (width, width), whole),
            ((8, width), f32, (8, width), whole),
        ],
        [],
        1,
        "middle_back",
    )
    memory_back = carried(wire_back, starts, tok_count, True)
    cell = lambda p, r, s: (r, p)
    mine = lambda p, r, s: (p, 0)
    from_wire = lambda p, r, s: (r, p, 0, 0)
    queries_back, map_query, key_feat, value_feat = call(
        local_back_kernel,
        (pairs, row_count),
        [
            (split, None, None),
            (phi_query, (tok_count, 2 * F), cell),
            (phi_key, (tok_count, 2 * F), cell),
            (values, (tok_count, PAIR), cell),
            (extended, (tok_count, 2 * F), cell),
            (memory, (1, 1, WIRE, F), from_wire),
            (queries, (tok_count, PAIR), cell),
            (maps, (PAIR, F), mine),
        ],
        [
            ((count, width), bf16, (tok_count, PAIR), cell),
            ((width, F), f32, (PAIR, F), mine),
            ((count, heads * F), f32, (tok_count, 2 * F), cell),
            ((count, width), f32, (tok_count, PAIR), cell),
        ],
        [],
        1,
        "local_back",
    )
    keys_back, values_back, map_grad = call(
        keys_back_kernel,
        (pairs, row_count),
        [
            (split, None, None),
            (key_feat, (tok_count, 2 * F), cell),
            (value_feat, (tok_count, PAIR), cell),
            (phi_key, (tok_count, 2 * F), cell),
            (values, (tok_count, PAIR), cell),
            (memory_back, (1, 1, WIRE, F), from_wire),
            (keys, (tok_count, PAIR), cell),
            (maps, (PAIR, F), mine),
            (map_query, (PAIR, F), mine),
        ],
        [
            ((count, width), bf16, (tok_count, PAIR), cell),
            ((count, width), bf16, (tok_count, PAIR), cell),
            ((width, F), f32, (PAIR, F), mine),
        ],
        [],
        1,
        "keys_back",
    )

    def weight_back(pb):
        return call(
            weight_back_kernel,
            (quads,),
            [
                (normed, (count, width), lambda q: (0, 0)),
                (pb, (count, quad), lambda q: (0, q)),
            ],
            [
                ((width, width), f32, (width, quad), lambda q: (0, q)),
                ((1, width), f32, (1, quad), lambda q: (0, q)),
            ],
            [pltpu.VMEM((width, count), bf16)],
            0,
            "weight_back",
        )

    parts = [weight_back(pb) for pb in (queries_back, keys_back, values_back)]
    mixing_grad = jnp.concatenate([p[0] for p in parts], axis=1)
    offset_grad = jnp.concatenate([p[1] for p in parts], axis=1)[0]
    row = lambda r: (r, 0)
    fixed = lambda r: (0, 0)
    input_gradient, small_in = call(
        input_back_kernel,
        (row_count,),
        [
            (queries_back, (tok_count, width), row),
            (keys_back, (tok_count, width), row),
            (values_back, (tok_count, width), row),
            (mixing, (width, width), lambda r: (0, 0)),
            (mixing, (width, width), lambda r: (0, 1)),
            (mixing, (width, width), lambda r: (0, 2)),
            (tok, (tok_count, width), row),
            (middle_back, (tok_count, width), row),
            (gains[0:1], (1, width), fixed),
        ],
        [
            ((count, width), bf16, (tok_count, width), row),
            ((8, width), f32, (8, width), fixed),
        ],
        [],
        0,
        "input_back",
    )
    gains_sum = jnp.stack([small_in[0], small_mid[0]])
    shifts_sum = jnp.stack([small_in[1], small_mid[1]])
    branch_sum = small_mid[2:4]

    def scatter_columns(rows):
        return lax.psum_scatter(rows, AXES, scatter_dimension=1, tiled=True)

    return (
        layer_output.reshape(tokens.shape),
        input_gradient.reshape(tokens.shape),
        scatter_columns(gains_sum),
        scatter_columns(shifts_sum),
        scatter_rows(mixing_grad),
        scatter_rows(offset_grad),
        scatter_rows(map_grad),
        scatter_rows(output_grad),
        scatter_columns(branch_sum),
        scatter_rows(expand_grad),
        scatter_rows(hidden_grad[0]),
        scatter_rows(shrink_grad),
    )


def solution(mesh):
    rows = P("batch", "seq", None)
    split_rows = P(AXES, None)
    split_columns = P(None, AXES)
    split_vector = P(AXES)
    return jax.shard_map(
        local,
        mesh=mesh,
        in_specs=(
            rows,
            P("batch", None),
            split_columns,
            split_columns,
            split_rows,
            split_vector,
            split_rows,
            split_rows,
            split_columns,
            split_rows,
            split_vector,
            split_rows,
            rows,
        ),
        out_specs=(
            rows,
            rows,
            split_columns,
            split_columns,
            split_rows,
            split_vector,
            split_rows,
            split_rows,
            split_columns,
            split_rows,
            split_vector,
            split_rows,
        ),
        check_vma=False,
    )
```

```python
import functools

import jax
import jax.numpy as jnp
from jax import lax
from jax.experimental import pallas as pl
from jax.experimental.pallas import tpu as pltpu
from jax.sharding import PartitionSpec as P

HD = 64
F = 2 * HD
PAIR = 2 * HD
SUB = 256
WIRE = F + 16
EPSILON = 1e-05
AXES = ("batch", "seq")
VMEM = 60 * 1024 * 1024
PACE = 0.01
bf16 = jnp.bfloat16
f32 = jnp.float32


def dot(a, b, left, right):
    return lax.dot_general(a, b, (((left,), (right,)), ((), ())), preferred_element_type=f32)


def nn(a, b):
    return dot(a, b, 1, 0)


def nt(a, b):
    return dot(a, b, 1, 1)


def tn(a, b):
    return dot(a, b, 0, 0)


def lane(shape):
    return lax.broadcasted_iota(jnp.int32, shape, len(shape) - 1)


def sublane(shape):
    return lax.broadcasted_iota(jnp.int32, shape, len(shape) - 2)


def normalize(values):
    center = jnp.mean(values, axis=-1, keepdims=True)
    centered = values - center
    spread = jnp.mean(centered * centered, axis=-1, keepdims=True)
    scale = lax.rsqrt(spread + EPSILON)
    return centered * scale, scale


def normalize_back(upstream, xhat, scale, gain):
    entry = upstream * gain
    first = jnp.mean(entry, axis=-1, keepdims=True)
    second = jnp.mean(entry * xhat, axis=-1, keepdims=True)
    return scale * (entry - first - xhat * second)


def map_weight(rows, keys):
    rows = rows.astype(f32)
    turned = pltpu.roll(rows, HD, 1)
    low = lane(rows.shape) < HD
    signed = jnp.where(low, turned, -rows) if keys else jnp.where(low, rows, -turned)
    top = sublane(rows.shape) < HD
    return jnp.concatenate(
        [jnp.where(top, signed, 0.0), jnp.where(top, 0.0, signed)], axis=1
    ).astype(bf16)


def segment_ones(width):
    shape = (width, width)
    return (lane(shape) // HD == sublane(shape) // HD).astype(bf16)


def segment_sum(values, ones):
    high = values.astype(bf16)
    low = (values - high.astype(f32)).astype(bf16)
    return nn(high, ones) + nn(low, ones)


def features(logits, ones):
    parts = []
    for at in range(0, logits.shape[1], F):
        part = logits[:, at : at + F]
        low = lane(part.shape) < HD
        first = jnp.max(jnp.where(low, part, -jnp.inf), axis=1, keepdims=True)
        second = jnp.max(jnp.where(low, -jnp.inf, part), axis=1, keepdims=True)
        parts.append(jnp.exp(part - jnp.where(low, first, second)))
    powers = jnp.concatenate(parts, axis=1)
    return powers / nn(powers.astype(bf16), ones)


def features_back(phi, upstream, ones):
    phi = phi.astype(f32)
    return phi * (upstream - segment_sum(phi * upstream, ones))


def split_of(ids, lens, row, count):
    first = ids[1] * count
    start, split = 0, count
    for n in range(lens.shape[1]):
        inside = (start >= first) & (start < first + count)
        split = jnp.where(inside, start - first, split)
        start = start + lens[row, n]
    return split


def starts_within(lens, row, low, high):
    start, found = 0, 0
    for n in range(lens.shape[1]):
        found = found | jnp.where((start >= low) & (start < high), 1, 0)
        start = start + lens[row, n]
    return found == 1


def matrix(ref):
    value = ref[...]
    return value if value.ndim == 2 else value.reshape(-1, value.shape[-1])


def with_aux(pair, head, aux):
    own = (lane(pair.shape) < HD) if head == 0 else (lane(pair.shape) >= HD)
    return jnp.where(own, pair, aux)


def pair_rows(first, second):
    top = sublane(first.shape) < HD
    return jnp.where(top, first, second)


def put_wire(ref, at, first, second, aux_rows):
    ref[0, at, 0:F, :] = pair_rows(first, second).astype(bf16)
    sums = [sum(x[a : a + 1] for a in rows) for x, rows in zip((first, second), aux_rows)]
    row = sublane((16, F))
    ref[0, at, F:WIRE, :] = jnp.where(
        row == 0, sums[0], jnp.where(row == 1, sums[1], 0.0)
    ).astype(bf16)


def take_wire(ref, at):
    state = ref[0, at, 0:F, :]
    sums = ref[0, at, F:WIRE, :]
    top = sublane(state.shape) < HD
    return jnp.where(top, state, sums[0:1]), jnp.where(top, sums[1:2], state)


def block_masks(split, count, flipped):
    masks = {}
    for ib in range(count):
        for jb in range(ib + 1):
            shape = (SUB, SUB)
            i = (lane(shape) if flipped else sublane(shape)) + ib * SUB
            j = (sublane(shape) if flipped else lane(shape)) + jb * SUB
            mask = (i < split) | (j >= split)
            if ib == jb:
                mask = mask & (j <= i)
            masks[ib, jb] = mask
    return masks


def keys_kernel(
    first, ids, lens, tok, gain, shift, wk, wv, ok, ov, maps, normed_o, k_o, v_o, phi_o, wire_o, kept
):
    row, quad = pl.program_id(0) + first, pl.program_id(1)

    @pl.when(quad == 0)
    def _():
        xhat, _ = normalize(tok[...].astype(f32))
        normed = (xhat * gain[...] + shift[...]).astype(bf16)
        kept[...] = normed
        normed_o[...] = normed

    normed = kept[...]
    keys = (nn(normed, wk[...]) + ok[...]).astype(bf16)
    values = (nn(normed, wv[...]) + ov[...]).astype(bf16)
    k_o[...] = keys
    v_o[...] = values
    count = keys.shape[0]
    split = split_of(ids, lens, row, count)
    begin = jnp.where(split < count, split, 0)
    last = sublane((count, PAIR)) >= begin
    ones = segment_ones(2 * F)
    for p in range(2):
        at = slice(p * PAIR, (p + 1) * PAIR)
        phi = features(nn(keys[:, at], map_weight(maps[at, :], True)), ones).astype(bf16)
        phi_o[:, 2 * p * F : 2 * (p + 1) * F] = phi
        pair = values[:, at].astype(f32)
        sums = [
            tn(
                jnp.where(last, with_aux(pair, h, 1.0), 0.0).astype(bf16),
                phi[:, h * F : (h + 1) * F],
            )
            for h in range(2)
        ]
        put_wire(wire_o, p, sums[0], sums[1], ((HD,), (0,)))


def local_kernel(first, ids, lens, normed, wq, oq, maps, phi_key, val, q_o, phi_o, num_o):
    row = pl.program_id(0) + first
    queries = (nn(normed[...], wq[...]) + oq[...]).astype(bf16)
    q_o[...] = queries
    count = queries.shape[0]
    split = split_of(ids, lens, row, count)
    blocks = count // SUB
    masks = block_masks(split, blocks, False)
    ones = segment_ones(2 * F)
    for p in range(2):
        at = slice(p * PAIR, (p + 1) * PAIR)
        phi = features(nn(queries[:, at], map_weight(maps[at, :], False)), ones).astype(bf16)
        phi_o[:, 2 * p * F : 2 * (p + 1) * F] = phi
        pair = val[:, at].astype(f32)
        for h in range(2):
            column = slice((2 * p + h) * F, (2 * p + h + 1) * F)
            query = phi[:, h * F : (h + 1) * F]
            key = phi_key[:, column]
            extended = with_aux(pair, h, 1.0).astype(bf16)
            for ib in range(blocks):
                rows = slice(ib * SUB, (ib + 1) * SUB)
                total = None
                for jb in range(ib + 1):
                    others = slice(jb * SUB, (jb + 1) * SUB)
                    scores = nt(query[rows], key[others])
                    scores = jnp.where(masks[ib, jb], scores, 0.0).astype(bf16)
                    part = nn(scores, extended[others])
                    total = part if total is None else total + part
                num_o[rows, column] = total


def middle_kernel(
    ids, lens, num, phi_query, wire, tok, wo, bias, gain, shift, att_o, rden_o, mid_o, normed_o
):
    row = pl.program_id(0)
    count = num.shape[0]
    carry = sublane((count, F)) < split_of(ids, lens, row, count)
    for p in range(wire.shape[1]):
        sums = []
        for h, memory in enumerate(take_wire(wire, p)):
            column = slice((2 * p + h) * F, (2 * p + h + 1) * F)
            sums.append(
                num[:, column] + jnp.where(carry, nt(phi_query[:, column], memory), 0.0)
            )
        low = lane((count, PAIR)) < HD
        numerator = jnp.where(low, sums[0], sums[1])
        denominator = pltpu.roll(jnp.where(low, sums[1], sums[0]), HD, 1)
        inverse = 1.0 / denominator
        at = slice(p * PAIR, (p + 1) * PAIR)
        rden_o[:, at] = inverse
        att_o[:, at] = (numerator * inverse).astype(bf16)
    middle = tok[...].astype(f32) + nn(att_o[...], matrix(wo)) + bias[...]
    mid_o[...] = middle
    xhat, _ = normalize(middle)
    normed_o[...] = (xhat * gain[...] + shift[...]).astype(bf16)


def put_halves(refs, value, core, at):
    if len(refs) == 1:
        refs[0][:, at] = value
        return
    mine_o, other_o = refs
    chips, rows, _ = mine_o.shape
    parted = value.reshape(chips, 2, rows, value.shape[1])
    even, odd = parted[:, 0], parted[:, 1]
    first = core == 0
    mine_o[:, :, at] = jnp.where(first, even, odd).astype(bf16)
    other_o[:, :, at] = jnp.where(first, odd, even).astype(bf16)


def mlp_kernel(plain, ids, lens, normed, cot, ex, sh, bias, *rest):
    if plain:
        y_o, back_o, bg_o, eg_o, sg_o, turned = rest
    else:
        y_o, back_o, bg_o, em_o, eo_o, sm_o, so_o, turned = rest
    step = pl.program_id(0)

    @pl.when(step == 0)
    def _():
        turned[...] = normed[...].T
        y_o[...] = jnp.zeros_like(y_o)
        back_o[...] = jnp.zeros_like(back_o)

    slope = 0.7978845608028654
    cubic = 0.044715
    expand, shrink = matrix(ex), matrix(sh)
    pre = nn(normed[...], expand) + bias[...]
    square = pre * pre
    bend = jnp.tanh(slope * (pre + cubic * pre * square))
    hidden = (0.5 * pre * (1.0 + bend)).astype(bf16)
    rise = 0.5 * (1.0 + bend) + 0.5 * pre * (1.0 - bend * bend) * slope * (
        1.0 + 3.0 * cubic * square
    )
    back = (nt(cot[...], shrink) * rise).astype(bf16)
    bg_o[...] = jnp.sum(back.astype(f32), axis=0, keepdims=True)
    y_o[...] += nn(hidden, shrink)
    back_o[...] += nt(back, expand)
    shrink_grad = tn(hidden, cot[...])
    expand_grad = nn(turned[...], back)
    if plain:
        sg_o[...] = shrink_grad
        eg_o[...] = expand_grad
        return
    core = ids[1] % 2
    first = core == 0
    put_halves((em_o, eo_o), expand_grad, core, slice(None))
    chips, rows, lanes = sm_o.shape
    width = shrink_grad.shape[1]
    subs = lanes // width
    parted = shrink_grad.reshape(chips, 2, subs, rows, width)
    for sub in range(subs):
        even, odd = parted[:, 0, sub], parted[:, 1, sub]
        at = slice(sub * width, (sub + 1) * width)
        sm_o[:, :, at] = jnp.where(first, even, odd).astype(bf16)
        so_o[:, :, at] = jnp.where(first, odd, even).astype(bf16)


def column_sum(values):
    return jnp.sum(values, axis=0, keepdims=True)


def middle_back_kernel(
    ids,
    lens,
    mid,
    y,
    back,
    cot,
    att,
    rden,
    phi_query,
    wo,
    gain,
    bias,
    out_o,
    mb_o,
    ext_o,
    wire_o,
    small_o,
    *rest,
):
    *og_refs, og_s = rest
    row = pl.program_id(0)

    @pl.when(row == 0)
    def _():
        og_s[...] = jnp.zeros_like(og_s)
        small_o[...] = jnp.zeros_like(small_o)

    middle = mid[...]
    upstream = cot[...].astype(f32)
    out_o[...] = (middle + y[...] + bias[...]).astype(bf16)
    xhat, scale = normalize(middle)
    from_norm = back[...]
    middle_back = upstream + normalize_back(from_norm, xhat, scale, gain[...])
    mb_o[...] = middle_back
    branch_back = middle_back.astype(bf16)
    small_o[0:1, :] += column_sum(from_norm * xhat)
    small_o[1:2, :] += column_sum(from_norm)
    small_o[2:3, :] += column_sum(branch_back.astype(f32))
    small_o[3:4, :] += column_sum(upstream)
    og_s[...] += tn(att[...], branch_back)

    @pl.when(row == pl.num_programs(0) - 1)
    def _():
        put_halves(og_refs, og_s[...], ids[1] % 2, slice(None))

    attended_back = nt(branch_back, matrix(wo))
    count = middle.shape[0]
    carry = sublane((count, F)) < split_of(ids, lens, row, count)
    ones = segment_ones(PAIR)
    spot = lane((count, PAIR))
    for p in range(wire_o.shape[1]):
        at = slice(p * PAIR, (p + 1) * PAIR)
        given = attended_back[:, at]
        inverse = rden[:, at]
        numerator_back = given * inverse
        denominator_back = -segment_sum(given * att[:, at].astype(f32), ones) * inverse
        aux = pltpu.roll(denominator_back, HD, 1)
        high = aux.astype(bf16).astype(f32)
        rest = aux - high
        sums = []
        for h in range(2):
            first = HD if h == 0 else 0
            extended = with_aux(
                numerator_back,
                h,
                jnp.where(spot == first, high, jnp.where(spot == first + 1, rest, 0.0)),
            ).astype(bf16)
            column = slice((2 * p + h) * F, (2 * p + h + 1) * F)
            ext_o[:, column] = extended
            query = jnp.where(carry, phi_query[:, column].astype(f32), 0.0).astype(bf16)
            sums.append(tn(extended, query))
        put_wire(wire_o, p, sums[0], sums[1], ((HD, HD + 1), (0, 1)))


def map_gradient(pair, logits_back):
    both = tn(pair, logits_back)
    rows = pair_rows(both[:, :F], both[:, F:])
    return rows - pltpu.roll(rows, HD, 1)


def local_back_kernel(
    ids, lens, phi_query, phi_key, val, ext, wire, queries, maps, pq_o, mg_o, kg_o, vg_o
):
    row = pl.program_id(1)
    count = val.shape[0]
    split = split_of(ids, lens, row, count)
    blocks = count // SUB
    masks = block_masks(split, blocks, False)
    flipped = block_masks(split, blocks, True)
    carry = sublane((count, F)) < split
    ones = segment_ones(2 * F)
    pair = val[...].astype(f32)
    memories = take_wire(wire, 0)
    grads, tops = [], []
    for h in range(2):
        column = slice(h * F, (h + 1) * F)
        query, key, given = phi_query[:, column], phi_key[:, column], ext[:, column]
        extended = with_aux(pair, h, 1.0).astype(bf16)
        query_grad = [None] * blocks
        key_grad = [None] * blocks
        value_grad = [None] * blocks

        def add(into, at, part):
            into[at] = part if into[at] is None else into[at] + part

        for ib in range(blocks):
            rows = slice(ib * SUB, (ib + 1) * SUB)
            for jb in range(ib + 1):
                others = slice(jb * SUB, (jb + 1) * SUB)
                turned = jnp.where(flipped[ib, jb], nt(key[others], query[rows]), 0.0)
                add(value_grad, jb, nn(turned.astype(bf16), given[rows]))
                turned = jnp.where(flipped[ib, jb], nt(extended[others], given[rows]), 0.0)
                add(key_grad, jb, nn(turned.astype(bf16), query[rows]))
                straight = jnp.where(masks[ib, jb], nt(given[rows], extended[others]), 0.0)
                add(query_grad, ib, nn(straight.astype(bf16), key[others]))
        kg_o[:, column] = jnp.concatenate(key_grad, axis=0)
        tops.append(jnp.concatenate(value_grad, axis=0))
        grads.append(
            jnp.concatenate(query_grad, axis=0)
            + jnp.where(carry, nn(given, memories[h]), 0.0)
        )
    vg_o[...] = jnp.where(lane(pair.shape) < HD, tops[0], tops[1])
    logits_back = features_back(phi_query[...], jnp.concatenate(grads, axis=1), ones).astype(bf16)
    pq_o[...] = nt(logits_back, map_weight(maps[...], False)).astype(bf16)
    gradient = map_gradient(queries[...], logits_back)

    @pl.when(row == 0)
    def _():
        mg_o[...] = gradient

    @pl.when(row > 0)
    def _():
        mg_o[...] += gradient


def keys_back_kernel(
    ids, lens, kg, vg, phi_key, val, wire, keys, maps, from_queries, pk_o, pv_o, mg_o
):
    row = pl.program_id(1)
    count = val.shape[0]
    split = split_of(ids, lens, row, count)
    begin = jnp.where(split < count, split, 0)
    last = sublane((count, F)) >= begin
    ones = segment_ones(2 * F)
    pair = val[...].astype(f32)
    state = wire[0, 0, 0:F, :]
    spot = sublane(state.shape)
    grads, tops = [], []
    for h, memory in enumerate(take_wire(wire, 0)):
        column = slice(h * F, (h + 1) * F)
        first = HD if h == 0 else 0
        own = (spot < HD) if h == 0 else (spot >= HD)
        memory = jnp.where(own | (spot == first), memory.astype(f32), 0.0).astype(bf16)
        extended = with_aux(pair, h, 1.0).astype(bf16)
        grads.append(kg[:, column] + jnp.where(last, nn(extended, memory), 0.0))
        tops.append(nt(phi_key[:, column], state))
    low = lane(pair.shape) < HD
    pv_o[...] = (vg[...] + jnp.where(last, jnp.where(low, tops[0], tops[1]), 0.0)).astype(bf16)
    logits_back = features_back(phi_key[...], jnp.concatenate(grads, axis=1), ones).astype(bf16)
    pk_o[...] = nt(logits_back, map_weight(maps[...], True)).astype(bf16)
    gradient = pltpu.roll(map_gradient(keys[...], logits_back), HD, 1)

    @pl.when(row == 0)
    def _():
        mg_o[...] = jnp.where(lane(gradient.shape) < HD, from_queries[...], gradient)

    @pl.when(row > 0)
    def _():
        mg_o[...] += jnp.where(lane(gradient.shape) < HD, 0.0, gradient)


def weight_back_kernel(ids, lens, normed, pb, *rest):
    *refs, turned = rest

    @pl.when(pl.program_id(0) == 0)
    def _():
        turned[...] = normed[...].T

    put_halves(refs, nn(turned[...], pb[...]), ids[1] % 2, slice(None))


def key_weight_back_kernel(half, ids, lens, normed, pk, pv, *rest):
    *refs, turned = rest
    step = pl.program_id(0)
    core = ids[1] % 2

    @pl.when(step == 0)
    def _():
        turned[...] = normed[...].T

    @pl.when(step < half)
    def _():
        put_halves(refs, nn(turned[...], pk[...]), core, slice(None))

    @pl.when(step >= half)
    def _():
        put_halves(refs, nn(turned[...], pv[...]), core, slice(None))


def input_back_kernel(pq, pk, pv, wq, wk, wv, tok, mb, gain, out_o, small_o):
    @pl.when(pl.program_id(0) == 0)
    def _():
        small_o[...] = jnp.zeros_like(small_o)

    from_norm = nt(pq[...], wq[...]) + nt(pk[...], wk[...]) + nt(pv[...], wv[...])
    xhat, scale = normalize(tok[...].astype(f32))
    small_o[0:1, :] += column_sum(from_norm * xhat)
    small_o[1:2, :] += column_sum(from_norm)
    for i, part in enumerate((pq, pk, pv)):
        small_o[2 + i : 3 + i, :] += column_sum(part[...].astype(f32))
    out_o[...] = (mb[...] + normalize_back(from_norm, xhat, scale, gain[...])).astype(bf16)


def spec(shape, index):
    return pl.BlockSpec(shape, index)


def estimate(micros):
    return pl.CostEstimate(
        flops=int(micros * PACE * 1e9), bytes_accessed=int(micros * PACE * 1e6), transcendentals=0
    )


def call(kernel, grid, ins, outs, scratch=(), scalars=0, name=None, micros=10, waits=(), into=()):
    waits = [*waits, *into]
    arrays = [entry[0] for entry in ins[scalars:]] + waits
    fetched = [entry[0] for entry in ins[:scalars]]
    read = len(ins)

    def body(*refs):
        kernel(*refs[:read], *refs[read + len(waits) :])

    return pl.pallas_call(
        body,
        out_shape=[jax.ShapeDtypeStruct(shape, kind) for shape, kind, _, _ in outs],
        grid_spec=pltpu.PrefetchScalarGridSpec(
            num_scalar_prefetch=scalars,
            grid=grid,
            in_specs=[spec(block, index) for _, block, index in ins[scalars:]]
            + [pl.BlockSpec(memory_space=pl.ANY)] * len(waits),
            out_specs=[spec(block, index) for _, _, block, index in outs],
            scratch_shapes=list(scratch),
        ),
        compiler_params=pltpu.CompilerParams(vmem_limit_bytes=VMEM),
        cost_estimate=estimate(micros),
        input_output_aliases={len(ins) + len(waits) - len(into) + i: i for i in range(len(into))},
        name=name,
    )(*fetched, *arrays)


def tie_kernel(*refs):
    del refs


def tie(values, *waits):
    anywhere = pl.BlockSpec(memory_space=pl.ANY)
    count = len(values)
    return pl.pallas_call(
        tie_kernel,
        out_shape=[jax.ShapeDtypeStruct(v.shape, v.dtype) for v in values],
        in_specs=[anywhere] * (count + len(waits)),
        out_specs=[anywhere] * count,
        input_output_aliases={i: i for i in range(count)},
        cost_estimate=estimate(0.5),
        name="tie",
    )(*values, *waits)


def gather_rows(part):
    return lax.all_gather(part, AXES, axis=0, tiled=True)


def scatter_rows(whole):
    return lax.psum_scatter(whole, AXES, scatter_dimension=0, tiled=True)


def scatter_columns(rows):
    return lax.psum_scatter(rows, AXES, scatter_dimension=1, tiled=True)


def swap(array, mask, axis="seq", name="swap"):
    size = lax.axis_size(axis)
    with jax.named_scope(name):
        return lax.ppermute(array, axis, [(i, i ^ mask) for i in range(size)])


def gather_cores(pieces, name):
    return pieces + [swap(piece, 1, name=name) for piece in pieces]


def put_piece(cuts, outs, at, piece):
    for out, first, last, sub in cuts:
        if sub is None:
            outs[out][at] = piece[:, first:last]
        else:
            outs[out][at, sub] = piece[:, first:last]


def place_kernel(cuts, ids, *refs):
    pieces, outs = refs[:8], refs[8:]

    def put(at, chips):
        for core in range(2):
            for piece, pair in zip(pieces[4 * core + at : 4 * core + at + 2], chips):
                for r, chip in enumerate(pair):
                    put_piece(cuts, outs, ids[1] ^ (2 * chip + core), piece[r, 0])

    @pl.when(pl.program_id(0) < 2)
    def _():
        put(0, ((0, 1), (2, 3)))

    @pl.when(pl.program_id(0) >= 2)
    def _():
        put(2, ((0, 2), (1, 3)))


def place(pieces, ids, cuts, shapes, name, micros, waits=()):
    rows, wide = pieces[0].shape[-2:]
    near = lambda s: jnp.minimum(s, 1)
    far = lambda s: jnp.maximum(s - 2, 0)
    ins = [
        (p.reshape(2, 2, rows, wide), (2, 1, rows, wide), lambda s, ids, at=at: (0, at(s), 0, 0))
        for p, at in zip(pieces, (near, near, far, far) * 2)
    ]

    def target(shape):
        return lambda s, ids: (ids[0] ^ s,) + (0,) * len(shape)

    return call(
        functools.partial(place_kernel, cuts),
        (4,),
        [(ids, None, None)] + ins,
        [((32, *shape), bf16, (8, *shape), target(shape)) for shape in shapes],
        [],
        1,
        name,
        micros,
        waits,
    )


def first_sum_kernel(parts, ids, *refs):
    ins, (near_keep, near_send, far_keep, far_send) = refs[: parts * 8], refs[parts * 8 :]
    step = pl.program_id(0)

    def put(targets):
        at = 0
        for part in range(parts):
            wide = ins[part * 8].shape[-1]
            for r, (out, i) in enumerate(targets):
                mine, got = ins[(part * 4 + r) * 2 : (part * 4 + r) * 2 + 2]
                total = mine[0, 0].astype(f32) + got[0, 0].astype(f32)
                out[i, 0, :, at : at + wide] = total.astype(bf16)
            at += wide

    @pl.when(step < 2)
    def _():
        put(((near_keep, 0), (near_send, 0), (near_keep, 1), (near_send, 1)))

    @pl.when(step >= 2)
    def _():
        put(((far_keep, 0), (far_keep, 1), (far_send, 0), (far_send, 1)))


def first_sum(mines, gots, ids, name, micros=4, waits=()):
    rows = mines[0].shape[-2]
    wides = [m.shape[-1] for m in mines]
    ins = [(ids, None, None)]

    def index(r):
        return lambda k, ids: (ids[0] ^ k, (ids[1] // 2) ^ r, 0, 0)

    for mine, got, wide in zip(mines, gots, wides):
        for r in range(4):
            for array in (mine, got):
                ins.append((array.reshape(4, 4, rows, wide), (1, 1, rows, wide), index(r)))
    total = sum(wides)
    near = lambda k, ids: (0, jnp.minimum(k, 1), 0, 0)
    far = lambda k, ids: (0, jnp.maximum(k - 2, 0), 0, 0)
    return call(
        functools.partial(first_sum_kernel, len(mines)),
        (4,),
        ins,
        [
            ((2, 2, rows, total), bf16, (2, 1, rows, total), at)
            for at in (near, near, far, far)
        ],
        [],
        1,
        name,
        micros,
        waits,
    )


def middle_sum_kernel(near_keep, near_got, far_keep, far_got, *outs):
    for at, (kept, got) in enumerate(((near_keep, near_got), (far_keep, far_got))):
        for i in range(2):
            total = kept[i].astype(f32) + got[i].astype(f32)
            outs[2 * at + i][...] = total.astype(bf16)


def middle_sum(sums, name, micros=3, waits=()):
    near_keep, near_send, far_keep, far_send = sums
    pieces = [near_keep, swap(near_send, 2, name=name + "_x1")]
    pieces += [far_keep, swap(far_send, 4, name=name + "_y1")]
    _, _, rows, wide = near_keep.shape
    tile = 1536 if wide % 1536 == 0 else wide
    near_keep, near_send, far_keep, far_send = call(
        middle_sum_kernel,
        (wide // tile,),
        [(p, (2, 2, rows, tile), lambda g: (0, 0, 0, g)) for p in pieces],
        [((2, rows, wide), bf16, (2, rows, tile), lambda g: (0, 0, g))] * 4,
        [],
        0,
        name,
        micros,
        waits,
    )
    near_got, far_got = swap(near_send, 4, name=name + "_y2"), swap(far_send, 2, name=name + "_x2")
    return [near_keep, near_got, far_keep, far_got]


def second_sum_kernel(direct, near, near_got, far, far_got, *outs):
    for k in range(4):
        kept, got = (near, near_got) if k < 2 else (far, far_got)
        total = kept[k % 2].astype(f32) + got[k % 2].astype(f32)
        if direct:
            outs[k][...] = total.astype(outs[k].dtype)
        else:
            outs[k // 2][k % 2] = total.astype(outs[k // 2].dtype)


def second_sum(pieces, name, micros=3, waits=(), direct=True):
    _, rows, wide = pieces[0].shape
    tile = 1536 if wide % 1536 == 0 else wide
    if direct:
        shape, cut = (rows, wide), (rows, tile)
        outs = [(shape, bf16 if k else f32, cut, lambda g: (0, g)) for k in range(4)]
    else:
        shape, cut = (2, rows, wide), (2, rows, tile)
        outs = [(shape, bf16 if k else f32, cut, lambda g: (0, 0, g)) for k in range(2)]
    return call(
        functools.partial(second_sum_kernel, direct),
        (wide // tile,),
        [(p, (2, rows, tile), lambda g: (0, 0, g)) for p in pieces],
        outs,
        [],
        0,
        name,
        micros,
        waits,
    )


def reduce_batch(sums, name, waits=()):
    if len(sums) == 4:
        total = sums[0]
        for k in range(1, 4):
            total = total + swap(sums[k], k, "batch", name + "_layer").astype(f32)
        return total
    got = swap(sums[1], 2, "batch", name + "_layer2")
    if waits:
        (got,) = tie([got], *waits)
    pair = sums[0] + got.astype(f32)
    return pair[0] + swap(pair[1].astype(bf16), 1, "batch", name + "_layer1").astype(f32)


def spots(length, each, owners):
    at = lane((F, length))
    owner = ((at.astype(f32) + 0.5) * (1.0 / each)).astype(jnp.int32)
    inside = (at - owner * each == sublane((F, length))).astype(bf16)
    at = lane((owners.shape[0], length))
    owner = ((at.astype(f32) + 0.5) * (1.0 / each)).astype(jnp.int32)
    return inside, owner == owners


def unpack_kernel(devices, block, *outs):
    rows = block.shape[0] // devices
    vectors = [(out, i) for out in outs for i in range(out.shape[0])]
    count = len(vectors)
    place_at = lane((count * devices, block.shape[0]))
    line = sublane((count * devices, block.shape[0]))
    vector = ((line.astype(f32) + 0.5) * (1.0 / devices)).astype(jnp.int32)
    picked = nn(
        (place_at == (line - vector * devices) * rows + vector).astype(bf16), block[...]
    ).astype(bf16)
    for j, (out, i) in enumerate(vectors):
        length = out.shape[1]
        owners = sublane((devices, length))
        inside, owned = spots(length, length // devices, owners)
        spread = nn(picked[j * devices : (j + 1) * devices], inside)
        out[i : i + 1, :] = column_sum(jnp.where(owned, spread, 0.0))


def shards_kernel(
    gain, shift, mix, offset, maps, out, branch, ex, hid, sh, first_o, rest_o, small
):
    rows = mix.shape[0]
    small[...] = jnp.zeros_like(small)
    for j, part in enumerate((gain, shift, branch)):
        small[2 * j : 2 * j + 2, 0:rows] = part[...].astype(f32)
    small[6:7, 0 : 3 * rows] = offset[...].astype(f32)
    small[7:8, 0 : 4 * rows] = hid[...].astype(f32)
    wide, width = mix.shape[1], sh.shape[1]
    first_o[:, 0:wide] = mix[...]
    first_o[:, wide : wide + F] = maps[...]
    first_o[:, wide + F : wide + 2 * F] = small[...].astype(bf16)
    for i in range(4):
        rest_o[i] = ex[:, i * width : (i + 1) * width]
        rest_o[4 + i] = sh[i * rows : (i + 1) * rows, :].astype(f32).astype(bf16)
    rest_o[8] = out[...]


def pack_kernel(
    devices, ids, small_in, small_mid, hid, maps, mine_o, other_o, lines
):
    offset = jnp.concatenate([small_in[i : i + 1, :] for i in range(2, 5)], axis=1)
    lines[...] = jnp.zeros_like(lines)
    vectors = [
        small_in[0:1, :],
        small_mid[0:1, :],
        small_in[1:2, :],
        small_mid[1:2, :],
        small_mid[2:3, :],
        small_mid[3:4, :],
        offset,
        hid[...],
    ]
    half = devices // 2
    core = ids[1] % 2
    for j, vector in enumerate(vectors):
        length = vector.shape[1]
        line = sublane((devices, length))
        owners = jnp.where(line < half, 2 * line + core, 2 * (line - half) + 1 - core)
        inside, owned = spots(length, length // devices, owners)
        share = jnp.where(owned, vector, 0.0).astype(bf16)
        lines[:, j, :] = nt(share, inside)
    put_halves((mine_o, other_o), maps[...], core, slice(0, F))
    mine_o[:, :, F:] = lines[:half].astype(bf16)
    other_o[:, :, F:] = lines[half:].astype(bf16)


def flags_kernel(levels, count, ids, lens, *outs):
    mine = ids[1]
    for row in range(lens.shape[0]):
        flags = []
        for reverse in (False, True):
            for level in range(levels):
                span = 1 << level
                begin = mine - lax.rem(mine, span)
                upper = lax.rem(mine // span, 2) == 1
                own_closed = starts_within(lens, row, begin * count, (begin + span) * count)
                if reverse:
                    receives = jnp.logical_not(upper)
                    closed = starts_within(lens, row, (mine + 1) * count, (begin + span) * count)
                    other = starts_within(lens, row, (begin - span) * count, begin * count)
                else:
                    receives = upper
                    closed = starts_within(lens, row, begin * count, mine * count)
                    other = starts_within(
                        lens, row, (begin + span) * count, (begin + 2 * span) * count
                    )
                flags.append(receives & jnp.logical_not(closed))
                flags.append(receives | jnp.logical_not(other))
                flags.append(jnp.logical_not(receives & own_closed))
        for out, flag in zip(outs, flags):
            out[row] = jnp.full((1, 1, F), jnp.where(flag, 1.0, 0.0), f32)


def carry(total, reached, flags, level, reverse, waits=()):
    levels = len(flags) // 6
    at = 3 * (level + (levels if reverse else 0))
    reaches, keeps, joins = flags[at : at + 3]
    other = swap(total, 1 << level, name=f"state{level}")
    if waits:
        (other,) = tie([other], *waits)
    other = other.astype(f32)
    arrived = reaches * other
    reached = arrived if reached is None else reached + arrived
    if level == levels - 1:
        return None, reached.astype(bf16)
    return (keeps * total.astype(f32) + joins * other).astype(bf16), reached


def local(
    tokens,
    sequence_lengths,
    norm_gains,
    norm_shifts,
    mixing_weight,
    mixing_offset,
    feature_maps,
    output_weight,
    branch_offsets,
    expand_weight,
    hidden_offset,
    shrink_weight,
    cotangent,
):
    row_count, tok_count, width = tokens.shape
    count = row_count * tok_count
    heads = width // HD
    pairs, quads = heads // 2, heads // 4
    quad = 2 * PAIR
    hidden_width = expand_weight.shape[1]
    batch, size = lax.axis_size("batch"), lax.axis_size("seq")
    devices = batch * size
    share = width // devices
    plain = size != 8 or batch != 4 or share % 8 != 0 or hidden_width != 4 * width or 4 * share > F

    mine = lax.axis_index("seq").astype(jnp.int32)
    ids = jnp.stack([lax.axis_index("batch").astype(jnp.int32), mine])
    lens = sequence_lengths
    scalars = [(ids, None, None), (lens, None, None)]
    levels = size.bit_length() - 1
    flag = (row_count, 1, 1, F)
    flags = call(
        functools.partial(flags_kernel, levels, tok_count),
        (1,),
        scalars,
        [(flag, f32, flag, lambda i, *s: (0, 0, 0, 0))] * (6 * levels),
        [],
        2,
        "flags",
        1,
    )

    if plain:
        gains = lax.all_gather(norm_gains, AXES, axis=1, tiled=True).astype(f32)[:, None]
        shifts = lax.all_gather(norm_shifts, AXES, axis=1, tiled=True).astype(f32)[:, None]
        branches = lax.all_gather(branch_offsets, AXES, axis=1, tiled=True).astype(f32)[:, None]
        offset = gather_rows(mixing_offset).astype(f32)[None]
        hidden_bias = gather_rows(hidden_offset).astype(f32)[None]
        first_weight = jnp.concatenate(
            [gather_rows(mixing_weight), gather_rows(feature_maps)], axis=1
        )
        out_weight = gather_rows(output_weight)
        expand = gather_rows(expand_weight)
        shrink = gather_rows(shrink_weight)
    else:
        wide = 3 * width + 2 * F
        shards = (
            norm_gains,
            norm_shifts,
            mixing_weight,
            mixing_offset[None],
            feature_maps,
            output_weight,
            branch_offsets,
            expand_weight,
            hidden_offset[None],
            shrink_weight,
        )
        at = lambda i: (0, 0)
        first, rest = call(
            shards_kernel,
            (1,),
            [(array, array.shape, at) for array in shards],
            [
                ((share, wide), bf16, (share, wide), at),
                ((9, share, width), bf16, (9, share, width), lambda i: (0, 0, 0)),
            ],
            [pltpu.VMEM((share, F), f32)],
            0,
            "shards",
            2,
        )
        layers = [first] + [swap(first, k, "batch", "first_layer") for k in range(1, 4)]
        near, far = jnp.stack(layers[:2]), jnp.stack(layers[2:])
        rest = lax.all_gather(rest, AXES)
        near = jnp.concatenate([near, swap(near, 2, name="first_x1")])
        far = jnp.concatenate([far, swap(far, 4, name="first_y1")])
        first = [
            near,
            swap(near, 4, name="first_y2"),
            far,
            swap(far, 2, name="first_x2"),
        ]
        first = gather_cores(first, "first_core")
        (first_weight,) = place(
            first, ids, ((0, 0, wide, None),), ((share, wide),), "place_first", 5
        )
        first_weight = first_weight.reshape(width, -1)
        *rows_out, offset, hidden_bias = call(
            functools.partial(unpack_kernel, devices),
            (1,),
            [(first_weight, (width, F), lambda i: (0, 3 * width // F + 1))],
            [
                ((n, length), f32, (n, length), lambda i: (0, 0))
                for n, length in [(1, width)] * 6 + [(1, 3 * width), (1, hidden_width)]
            ],
            [],
            0,
            "unpack",
            2,
        )
        gains, shifts, branches = (rows_out[i : i + 2] for i in (0, 2, 4))

    tok = tokens.reshape(count, width)
    cot = cotangent.reshape(count, width)
    full = lambda r, q, *s: (0, 0)

    def columns(first):
        return lambda r, q, *s: (0, first + q)


    def project(first, into=(), waits=()):
        own = lambda r, q, *s: (r + first, 0)
        cell = lambda r, q, *s: (r + first, q)
        return call(
            functools.partial(keys_kernel, first),
            (1, quads),
            [
                *scalars,
                (tok, (tok_count, width), own),
                (gains[0], (1, width), full),
                (shifts[0], (1, width), full),
                (first_weight, (width, quad), columns(quads)),
                (first_weight, (width, quad), columns(2 * quads)),
                (offset, (1, quad), columns(quads)),
                (offset, (1, quad), columns(2 * quads)),
                (first_weight, (quad, F), lambda r, q, *s: (q, 3 * width // F)),
            ],
            [
                ((count, width), bf16, (tok_count, width), own),
                ((count, width), bf16, (tok_count, quad), cell),
                ((count, width), bf16, (tok_count, quad), cell),
                ((count, heads * F), bf16, (tok_count, 4 * F), cell),
                (
                    (row_count, pairs, WIRE, F),
                    bf16,
                    (1, 2, WIRE, F),
                    lambda r, q, *s: (r + first, q, 0, 0),
                ),
            ],
            [pltpu.VMEM((tok_count, width), bf16)],
            2,
            "keys",
            15 / row_count,
            waits,
            into,
        )

    projected = project(0, (), flags)
    for first in range(1, row_count):
        projected = project(first, projected)
    normed, keys, values, phi_key, wire = projected

    def attend(first, into=(), waits=()):
        own = lambda r, q, *s: (r + first, 0)
        cell = lambda r, q, *s: (r + first, q)
        return call(
            functools.partial(local_kernel, first),
            (1, quads),
            [
                *scalars,
                (normed, (tok_count, width), own),
                (first_weight, (width, quad), columns(0)),
                (offset, (1, quad), columns(0)),
                (first_weight, (quad, F), lambda r, q, *s: (q, 3 * width // F)),
                (phi_key, (tok_count, 4 * F), cell),
                (values, (tok_count, quad), cell),
            ],
            [
                ((count, width), bf16, (tok_count, quad), cell),
                ((count, heads * F), bf16, (tok_count, 4 * F), cell),
                ((count, heads * F), f32, (tok_count, 4 * F), cell),
            ],
            [],
            2,
            "local_attention",
            20 / row_count,
            waits,
            into,
        )

    total, reached = carry(wire, None, flags, 0, False)
    partial = ()
    for level in range(1, levels):
        if level <= row_count:
            partial = attend(level - 1, partial, (total,))
        total, reached = carry(total, reached, flags, level, False, partial[2:])
    for first in range(levels - 1, row_count):
        partial = attend(first, partial)
    queries, phi_query, numerator = partial
    memory = reached
    if plain:
        out_part = (out_weight, (width, width), lambda r, *s: (0, 0))
        expand_part = (expand, (width, width), lambda f, *s: (0, f))
        shrink_part = (shrink, (width, width), lambda f, *s: (f, 0))
    else:
        cut = (devices, 1, share, width)
        out_part = (rest, cut, lambda r, *s: (0, 8, 0, 0))
        expand_part = (rest, cut, lambda f, *s: (0, f, 0, 0))
        cut = (devices // 4, 4, share, width)
        shrink_part = (rest, cut, lambda f, *s: (f, 1, 0, 0))
    one = lambda r, *s: (r, 0)
    whole = lambda r, *s: (0, 0)
    attended, inverse, middle, normed_mid = call(
        middle_kernel,
        (row_count,),
        [
            *scalars,
            (numerator, (tok_count, heads * F), one),
            (phi_query, (tok_count, heads * F), one),
            (memory, (1, pairs, WIRE, F), lambda r, *s: (r, 0, 0, 0)),
            (tok, (tok_count, width), one),
            out_part,
            (branches[0], (1, width), whole),
            (gains[1], (1, width), whole),
            (shifts[1], (1, width), whole),
        ],
        [
            ((count, width), bf16, (tok_count, width), one),
            ((count, width), f32, (tok_count, width), one),
            ((count, width), f32, (tok_count, width), one),
            ((count, width), bf16, (tok_count, width), one),
        ],
        [],
        2,
        "middle",
        9,
    )
    tile = width
    steps = hidden_width // tile

    def halves(wide, block, index):
        if plain:
            return [((width, wide), f32, (width, block), lambda *i: (0, index(*i)))]
        shape = (devices // 2, share, wide)
        cut = (devices // 2, share, block)
        return [(shape, bf16, cut, lambda *i: (0, 0, index(*i)))] * 2

    y, normed_mid_back, hidden_grad, *mlp_grads = call(
        functools.partial(mlp_kernel, plain),
        (steps,),
        [
            *scalars,
            (normed_mid, (count, width), lambda f, *s: (0, 0)),
            (cot, (count, width), lambda f, *s: (0, 0)),
            expand_part,
            shrink_part,
            (hidden_bias, (1, tile), lambda f, *s: (0, f)),
        ],
        [
            ((count, width), f32, (count, width), lambda f, *s: (0, 0)),
            ((count, width), f32, (count, width), lambda f, *s: (0, 0)),
            ((1, hidden_width), f32, (1, tile), lambda f, *s: (0, f)),
            *halves(hidden_width, tile, lambda f, *s: f),
            *(
                [((hidden_width, width), f32, (tile, width), lambda f, *s: (f, 0))]
                if plain
                else [
                    (
                        (devices // 2, share, 4 * width),
                        bf16,
                        (devices // 2 // steps, share, 4 * width),
                        lambda f, *s: (f, 0, 0),
                    )
                ]
                * 2
            ),
        ],
        [pltpu.VMEM((width, count), bf16)],
        2,
        "mlp",
        37,
    )
    layer_output, middle_back, extended, wire_back, small_mid, *output_grads = call(
        middle_back_kernel,
        (row_count,),
        [
            *scalars,
            (middle, (tok_count, width), one),
            (y, (tok_count, width), one),
            (normed_mid_back, (tok_count, width), one),
            (cot, (tok_count, width), one),
            (attended, (tok_count, width), one),
            (inverse, (tok_count, width), one),
            (phi_query, (tok_count, heads * F), one),
            out_part,
            (gains[1], (1, width), whole),
            (branches[1], (1, width), whole),
        ],
        [
            ((count, width), bf16, (tok_count, width), one),
            ((count, width), f32, (tok_count, width), one),
            ((count, heads * F), bf16, (tok_count, heads * F), one),
            ((row_count, pairs, WIRE, F), bf16, (1, pairs, WIRE, F), lambda r, *s: (r, 0, 0, 0)),
            ((8, width), f32, (8, width), whole),
            *halves(width, width, lambda r, *s: 0),
        ],
        [pltpu.VMEM((width, width), f32)],
        2,
        "middle_back",
        17,
    )
    if not plain:
        expand_mine, expand_other, shrink_mine, shrink_other = mlp_grads
        mlp_waits = first_sum(
            (expand_mine, shrink_mine),
            (swap(expand_other, 1, name="mlp_core"), swap(shrink_other, 1, name="mlp_core")),
            ids,
            "mlp_first_sum",
            7,
            (middle_back,),
        )
    total, reached = carry(wire_back, None, flags, 0, True)
    for level in range(1, levels):
        if level == levels - 1 and not plain:
            mlp_sums = list(tie(mlp_waits, total))
            mlp_waits = [total, mlp_sums[1]]
        waits = [] if plain else [mlp_waits[0]]
        total, reached = carry(total, reached, flags, level, True, waits)
    memory_back = reached
    cell = lambda p, r, *s: (r, p)
    of_pair = lambda p, r, *s: (p, 0)
    from_wire = lambda p, r, *s: (r, p, 0, 0)
    queries_back, map_query, key_feat, value_feat = call(
        local_back_kernel,
        (pairs, row_count),
        [
            *scalars,
            (phi_query, (tok_count, 2 * F), cell),
            (phi_key, (tok_count, 2 * F), cell),
            (values, (tok_count, PAIR), cell),
            (extended, (tok_count, 2 * F), cell),
            (memory, (1, 1, WIRE, F), from_wire),
            (queries, (tok_count, PAIR), cell),
            (first_weight, (PAIR, F), lambda p, r, *s: (p, 3 * width // F)),
        ],
        [
            ((count, width), bf16, (tok_count, PAIR), cell),
            ((width, F), f32, (PAIR, F), of_pair),
            ((count, heads * F), f32, (tok_count, 2 * F), cell),
            ((count, width), f32, (tok_count, PAIR), cell),
        ],
        [],
        2,
        "local_back",
        32,
        () if plain else mlp_waits,
    )
    def weight_back(pb, waits=()):
        return call(
            weight_back_kernel,
            (quads,),
            [
                *scalars,
                (normed, (count, width), lambda q, *s: (0, 0)),
                (pb, (count, quad), lambda q, *s: (0, q)),
            ],
            halves(width, quad, lambda q, *s: q),
            [pltpu.VMEM((width, count), bf16)],
            2,
            "weight_back",
            5,
            waits,
        )

    query_grads = weight_back(queries_back)
    if not plain:
        query_waits = first_sum(
            (query_grads[0], output_grads[0]),
            (swap(query_grads[1], 1, name="query_core"), swap(output_grads[1], 1, name="query_core")),
            ids,
            "query_first_sum",
        )
        mlp_sums = middle_sum(mlp_sums, "mlp_middle_sum", 4, (map_query,))
    keys_back, values_back, map_grad = call(
        keys_back_kernel,
        (pairs, row_count),
        [
            *scalars,
            (key_feat, (tok_count, 2 * F), cell),
            (value_feat, (tok_count, PAIR), cell),
            (phi_key, (tok_count, 2 * F), cell),
            (values, (tok_count, PAIR), cell),
            (memory_back, (1, 1, WIRE, F), from_wire),
            (keys, (tok_count, PAIR), cell),
            (first_weight, (PAIR, F), lambda p, r, *s: (p, 3 * width // F)),
            (map_query, (PAIR, F), of_pair),
        ],
        [
            ((count, width), bf16, (tok_count, PAIR), cell),
            ((count, width), bf16, (tok_count, PAIR), cell),
            ((width, F), f32, (PAIR, F), of_pair),
        ],
        [],
        2,
        "keys_back",
        17,
        () if plain else query_waits,
    )

    if not plain:
        mlp_sums = second_sum(mlp_sums, "mlp_second_sum", 4, (keys_back,), False)
        query_sums = middle_sum(query_waits, "query_middle_sum", 2, (mlp_sums[1],))
    row = lambda r: (r, 0)
    fixed = lambda r: (0, 0)
    input_gradient, small_in = call(
        input_back_kernel,
        (row_count,),
        [
            (queries_back, (tok_count, width), row),
            (keys_back, (tok_count, width), row),
            (values_back, (tok_count, width), row),
            (first_weight, (width, width), lambda r: (0, 0)),
            (first_weight, (width, width), lambda r: (0, 1)),
            (first_weight, (width, width), lambda r: (0, 2)),
            (tok, (tok_count, width), row),
            (middle_back, (tok_count, width), row),
            (gains[0], (1, width), fixed),
        ],
        [
            ((count, width), bf16, (tok_count, width), row),
            ((8, width), f32, (8, width), fixed),
        ],
        [],
        0,
        "input_back",
        10,
        () if plain else (mlp_sums[1],),
    )
    if not plain:
        at = lambda i, ids: (0, 0)
        half = (devices // 2, share, 2 * F)
        small_grads = call(
            functools.partial(pack_kernel, devices),
            (1,),
            [(ids, None, None)]
            + [(array, array.shape, at) for array in (small_in, small_mid, hidden_grad, map_grad)],
            [(half, bf16, half, lambda i, ids: (0, 0, 0))] * 2,
            [pltpu.VMEM((devices, share, F), f32)],
            1,
            "pack",
            2,
        )
        query_sums = second_sum(query_sums, "query_second_sum", 3, (small_grads[0],), False)
    key_grads = call(
        functools.partial(key_weight_back_kernel, quads),
        (2 * quads,),
        [
            *scalars,
            (normed, (count, width), lambda q, *s: (0, 0)),
            (keys_back, (count, quad), lambda q, *s: (0, jnp.minimum(q, quads - 1))),
            (values_back, (count, quad), lambda q, *s: (0, jnp.maximum(q - quads, 0))),
        ],
        halves(2 * width, quad, lambda q, *s: q),
        [pltpu.VMEM((width, count), bf16)],
        2,
        "key_weight_back",
        10,
        () if plain else (query_sums[1],),
    )
    if plain:
        mixing_grad = jnp.concatenate([query_grads[0], key_grads[0]], axis=1)
        offset_grad = small_in[2:5].reshape(-1)
        grads = (
            scatter_columns(jnp.stack([small_in[0], small_mid[0]])),
            scatter_columns(jnp.stack([small_in[1], small_mid[1]])),
            scatter_rows(mixing_grad),
            scatter_rows(offset_grad),
            scatter_rows(map_grad),
            scatter_rows(output_grads[0]),
            scatter_columns(small_mid[2:4]),
            scatter_rows(mlp_grads[0]),
            scatter_rows(hidden_grad[0]),
            scatter_rows(mlp_grads[1]),
        )
    else:
        key_sums = first_sum(
            (key_grads[0], small_grads[0]),
            (swap(key_grads[1], 1, name="key_core"), swap(small_grads[1], 1, name="key_core")),
            ids,
            "key_first_sum",
        )
        query_total = reduce_batch(query_sums, "query", key_sums[1:2])
        key_sums = middle_sum(key_sums, "key_middle_sum", 2)
        mlp_total = reduce_batch(mlp_sums, "mlp", key_sums[1:2])
        key_sums = second_sum(key_sums, "key_second_sum")
        key_total = reduce_batch(key_sums, "key")
        small_total = key_total[0:8, 2 * width + F :]
        mixing_grad = jnp.concatenate(
            [query_total[:, :width], key_total[:, : 2 * width]], axis=1
        )
        shrink_grad = mlp_total[:, hidden_width:].reshape(share, 4, width)
        grads = (
            small_total[0:2, :share],
            small_total[2:4, :share],
            mixing_grad,
            small_total[6, : 3 * share],
            key_total[:, 2 * width : 2 * width + F],
            query_total[:, width:],
            small_total[4:6, :share],
            mlp_total[:, :hidden_width],
            small_total[7, : 4 * share],
            shrink_grad.transpose(1, 0, 2).reshape(4 * share, width),
        )
    return (layer_output.reshape(tokens.shape), input_gradient.reshape(tokens.shape), *grads)


def solution(mesh):
    rows = P("batch", "seq", None)
    split_rows = P(AXES, None)
    split_columns = P(None, AXES)
    split_vector = P(AXES)
    return jax.shard_map(
        local,
        mesh=mesh,
        in_specs=(
            rows,
            P("batch", None),
            split_columns,
            split_columns,
            split_rows,
            split_vector,
            split_rows,
            split_rows,
            split_columns,
            split_rows,
            split_vector,
            split_rows,
            rows,
        ),
        out_specs=(
            rows,
            rows,
            split_columns,
            split_columns,
            split_rows,
            split_vector,
            split_rows,
            split_rows,
            split_columns,
            split_rows,
            split_vector,
            split_rows,
        ),
        check_vma=False,
    )
```

```python
import functools

import jax
import jax.numpy as jnp
from jax import lax
from jax.experimental import pallas as pl
from jax.experimental.pallas import tpu as pltpu
from jax.sharding import PartitionSpec as P

HD = 64
F = 2 * HD
PAIR = 2 * HD
SUB = 256
WIRE = F + 16
EPSILON = 1e-05
AXES = ("batch", "seq")
LIMIT = 28
LIMITS = {"mlp": 52, "attention": 32, "middle_back": 40, "local_back": 40, "middle": 40, "input_back": 32}
SUMS = {
    group + part
    for group in ("mlp", "query", "key")
    for part in ("_first_sum", "_middle_sum", "_second_sum")
}
FREE_INS = SUMS | {"place_first", "unpack"}
FREE_OUTS = SUMS | {"shards", "place_first", "unpack"}
PACE = 0.01
bf16 = jnp.bfloat16
f32 = jnp.float32


def dot(a, b, left, right):
    return lax.dot_general(a, b, (((left,), (right,)), ((), ())), preferred_element_type=f32)


def nn(a, b):
    return dot(a, b, 1, 0)


def nt(a, b):
    return dot(a, b, 1, 1)


def tn(a, b):
    return dot(a, b, 0, 0)


def lane(shape):
    return lax.broadcasted_iota(jnp.int32, shape, len(shape) - 1)


def sublane(shape):
    return lax.broadcasted_iota(jnp.int32, shape, len(shape) - 2)


def normalize(values):
    center = jnp.mean(values, axis=-1, keepdims=True)
    centered = values - center
    spread = jnp.mean(centered * centered, axis=-1, keepdims=True)
    scale = lax.rsqrt(spread + EPSILON)
    return centered * scale, scale


def normalize_back(upstream, xhat, scale, gain):
    entry = upstream * gain
    first = jnp.mean(entry, axis=-1, keepdims=True)
    second = jnp.mean(entry * xhat, axis=-1, keepdims=True)
    return scale * (entry - first - xhat * second)


def map_weight(rows, keys):
    rows = rows.astype(f32)
    turned = pltpu.roll(rows, HD, 1)
    low = lane(rows.shape) < HD
    signed = jnp.where(low, turned, -rows) if keys else jnp.where(low, rows, -turned)
    top = sublane(rows.shape) < HD
    return jnp.concatenate(
        [jnp.where(top, signed, 0.0), jnp.where(top, 0.0, signed)], axis=1
    ).astype(bf16)


def segment_ones(width):
    shape = (width, width)
    return (lane(shape) // HD == sublane(shape) // HD).astype(bf16)


def segment_sum(values, ones):
    high = values.astype(bf16)
    low = (values - high.astype(f32)).astype(bf16)
    return nn(high, ones) + nn(low, ones)


def features(logits, ones):
    parts = []
    for at in range(0, logits.shape[1], F):
        part = logits[:, at : at + F]
        low = lane(part.shape) < HD
        first = jnp.max(jnp.where(low, part, -jnp.inf), axis=1, keepdims=True)
        second = jnp.max(jnp.where(low, -jnp.inf, part), axis=1, keepdims=True)
        parts.append(jnp.exp(part - jnp.where(low, first, second)))
    powers = jnp.concatenate(parts, axis=1)
    return powers / nn(powers.astype(bf16), ones)


def features_back(phi, upstream, ones):
    phi = phi.astype(f32)
    return phi * (upstream - segment_sum(phi * upstream, ones))


def split_of(ids, lens, row, count):
    first = ids[1] * count
    start, split = 0, count
    for n in range(lens.shape[1]):
        inside = (start >= first) & (start < first + count)
        split = jnp.where(inside, start - first, split)
        start = start + lens[row, n]
    return split


def starts_within(lens, row, low, high):
    start, found = 0, 0
    for n in range(lens.shape[1]):
        found = found | jnp.where((start >= low) & (start < high), 1, 0)
        start = start + lens[row, n]
    return found == 1


def matrix(ref):
    value = ref[...]
    return value if value.ndim == 2 else value.reshape(-1, value.shape[-1])


def with_aux(pair, head, aux):
    own = (lane(pair.shape) < HD) if head == 0 else (lane(pair.shape) >= HD)
    return jnp.where(own, pair, aux)


def pair_rows(first, second):
    top = sublane(first.shape) < HD
    return jnp.where(top, first, second)


def put_wire(ref, at, first, second, aux_rows):
    ref[0, at, 0:F, :] = pair_rows(first, second).astype(bf16)
    sums = [sum(x[a : a + 1] for a in rows) for x, rows in zip((first, second), aux_rows)]
    row = sublane((16, F))
    ref[0, at, F:WIRE, :] = jnp.where(
        row == 0, sums[0], jnp.where(row == 1, sums[1], 0.0)
    ).astype(bf16)


def take_wire(ref, at):
    state = ref[0, at, 0:F, :]
    sums = ref[0, at, F:WIRE, :]
    top = sublane(state.shape) < HD
    return jnp.where(top, state, sums[0:1]), jnp.where(top, sums[1:2], state)


def block_masks(split, count, flipped):
    masks = []
    for first in range(0, count, SUB):
        if flipped:
            shape = (SUB, count - first)
            i, j = lane(shape) + first, sublane(shape) + first
        else:
            shape = (SUB, first + SUB)
            i, j = sublane(shape) + first, lane(shape)
        masks.append(((i < split) | (j >= split)) & (j <= i))
    return masks


def masked(scores, mask):
    return jnp.where(mask, scores, 0.0).astype(bf16)


def keys_kernel(
    ids, lens, tok, gain, shift, wk, wv, ok, ov, maps, normed_o, k_o, v_o, phi_o, wire_o, kept
):
    row, quad = pl.program_id(0), pl.program_id(1)

    @pl.when(quad == 0)
    def _():
        xhat, _ = normalize(tok[...].astype(f32))
        normed = (xhat * gain[...] + shift[...]).astype(bf16)
        kept[...] = normed
        normed_o[...] = normed

    normed = kept[...]
    keys = (nn(normed, wk[...]) + ok[...]).astype(bf16)
    values = (nn(normed, wv[...]) + ov[...]).astype(bf16)
    k_o[...] = keys
    v_o[...] = values
    count = keys.shape[0]
    split = split_of(ids, lens, row, count)
    begin = jnp.where(split < count, split, 0)
    last = sublane((count, PAIR)) >= begin
    ones = segment_ones(2 * F)
    cuts = [slice(p * PAIR, (p + 1) * PAIR) for p in range(2)]
    logits = [nn(keys[:, at], map_weight(maps[at, :], True)) for at in cuts]
    phis = [features(part, ones).astype(bf16) for part in logits]
    for p, at in enumerate(cuts):
        phi_o[:, 2 * p * F : 2 * (p + 1) * F] = phis[p]
    for p, at in enumerate(cuts):
        pair = values[:, at].astype(f32)
        sums = [
            tn(
                jnp.where(last, with_aux(pair, h, 1.0), 0.0).astype(bf16),
                phis[p][:, h * F : (h + 1) * F],
            )
            for h in range(2)
        ]
        put_wire(wire_o, p, sums[0], sums[1], ((HD,), (0,)))


def queries_kernel(normed, wq, oq, maps, q_o, phi_o):
    queries = (nn(normed[...], wq[...]) + oq[...]).astype(bf16)
    q_o[...] = queries
    ones = segment_ones(2 * F)
    cuts = [slice(p * PAIR, (p + 1) * PAIR) for p in range(2)]
    logits = [nn(queries[:, at], map_weight(maps[at, :], False)) for at in cuts]
    for p, part in enumerate(logits):
        phi_o[:, 2 * p * F : 2 * (p + 1) * F] = features(part, ones).astype(bf16)


def attention_kernel(ids, lens, phi_query, phi_key, val, num_o):
    count = val.shape[0]
    split = split_of(ids, lens, pl.program_id(0), count)
    masks = block_masks(split, count, False)
    columns = [slice(h * F, (h + 1) * F) for h in range(4)]
    blocks = [slice(first, first + SUB) for first in range(0, count, SUB)]
    scores = [
        [
            masked(nt(phi_query[rows, at], phi_key[: rows.stop, at]), mask)
            for rows, mask in zip(blocks, masks)
        ]
        for at in columns
    ]
    for h, at in enumerate(columns):
        pair = val[:, h // 2 * PAIR : (h // 2 + 1) * PAIR].astype(f32)
        extended = with_aux(pair, h % 2, 1.0).astype(bf16)
        for rows, part in zip(blocks, scores[h]):
            num_o[rows, at] = nn(part, extended[: rows.stop])


def middle_kernel(
    ids, lens, num, phi_query, wire, tok, wo, bias, gain, shift, att_o, rden_o, mid_o, normed_o
):
    row = pl.program_id(0)
    count = num.shape[0]
    carry = sublane((count, F)) < split_of(ids, lens, row, count)
    for p in range(wire.shape[1]):
        sums = []
        for h, memory in enumerate(take_wire(wire, p)):
            column = slice((2 * p + h) * F, (2 * p + h + 1) * F)
            sums.append(
                num[:, column] + jnp.where(carry, nt(phi_query[:, column], memory), 0.0)
            )
        low = lane((count, PAIR)) < HD
        numerator = jnp.where(low, sums[0], sums[1])
        denominator = pltpu.roll(jnp.where(low, sums[1], sums[0]), HD, 1)
        inverse = 1.0 / denominator
        at = slice(p * PAIR, (p + 1) * PAIR)
        rden_o[:, at] = inverse
        att_o[:, at] = (numerator * inverse).astype(bf16)
    middle = tok[...].astype(f32) + nn(att_o[...], matrix(wo)) + bias[...]
    mid_o[...] = middle
    xhat, _ = normalize(middle)
    normed_o[...] = (xhat * gain[...] + shift[...]).astype(bf16)


def put_halves(refs, value, core, at):
    if len(refs) == 1:
        refs[0][:, at] = value
        return
    mine_o, other_o = refs
    chips, rows, _ = mine_o.shape
    parted = value.reshape(chips, 2, rows, value.shape[1])
    even, odd = parted[:, 0], parted[:, 1]
    first = core == 0
    mine_o[:, :, at] = jnp.where(first, even, odd).astype(bf16)
    other_o[:, :, at] = jnp.where(first, odd, even).astype(bf16)


def mlp_kernel(plain, ids, lens, normed, cot, ex, sh, bias, *rest):
    if plain:
        y_o, back_o, bg_o, eg_o, sg_o, turned = rest
    else:
        y_o, back_o, bg_o, em_o, eo_o, sm_o, so_o, turned = rest
    step = pl.program_id(0)

    @pl.when(step == 0)
    def _():
        turned[...] = normed[...].T
        y_o[...] = jnp.zeros_like(y_o)
        back_o[...] = jnp.zeros_like(back_o)

    slope = 0.7978845608028654
    cubic = 0.044715
    expand, shrink = matrix(ex), matrix(sh)
    pre = nn(normed[...], expand) + bias[...]
    square = pre * pre
    bend = jnp.tanh(slope * (pre + cubic * pre * square))
    hidden = (0.5 * pre * (1.0 + bend)).astype(bf16)
    rise = 0.5 * (1.0 + bend) + 0.5 * pre * (1.0 - bend * bend) * slope * (
        1.0 + 3.0 * cubic * square
    )
    back = (nt(cot[...], shrink) * rise).astype(bf16)
    bg_o[...] = jnp.sum(back.astype(f32), axis=0, keepdims=True)
    y_o[...] += nn(hidden, shrink)
    back_o[...] += nt(back, expand)
    shrink_grad = tn(hidden, cot[...])
    expand_grad = nn(turned[...], back)
    if plain:
        sg_o[...] = shrink_grad
        eg_o[...] = expand_grad
        return
    core = ids[1] % 2
    first = core == 0
    put_halves((em_o, eo_o), expand_grad, core, slice(None))
    chips, rows, lanes = sm_o.shape
    width = shrink_grad.shape[1]
    subs = lanes // width
    parted = shrink_grad.reshape(chips, 2, subs, rows, width)
    for sub in range(subs):
        even, odd = parted[:, 0, sub], parted[:, 1, sub]
        at = slice(sub * width, (sub + 1) * width)
        sm_o[:, :, at] = jnp.where(first, even, odd).astype(bf16)
        so_o[:, :, at] = jnp.where(first, odd, even).astype(bf16)


def column_sum(values):
    return jnp.sum(values, axis=0, keepdims=True)


def middle_back_kernel(
    ids,
    lens,
    mid,
    y,
    back,
    cot,
    att,
    rden,
    phi_query,
    wo,
    gain,
    bias,
    out_o,
    mb_o,
    ext_o,
    wire_o,
    small_o,
    *rest,
):
    *og_refs, og_s = rest
    row = pl.program_id(0)

    @pl.when(row == 0)
    def _():
        og_s[...] = jnp.zeros_like(og_s)
        small_o[...] = jnp.zeros_like(small_o)

    middle = mid[...]
    upstream = cot[...].astype(f32)
    out_o[...] = (middle + y[...] + bias[...]).astype(bf16)
    xhat, scale = normalize(middle)
    from_norm = back[...]
    middle_back = upstream + normalize_back(from_norm, xhat, scale, gain[...])
    mb_o[...] = middle_back
    branch_back = middle_back.astype(bf16)
    small_o[0:1, :] += column_sum(from_norm * xhat)
    small_o[1:2, :] += column_sum(from_norm)
    small_o[2:3, :] += column_sum(branch_back.astype(f32))
    small_o[3:4, :] += column_sum(upstream)
    og_s[...] += tn(att[...], branch_back)

    @pl.when(row == pl.num_programs(0) - 1)
    def _():
        put_halves(og_refs, og_s[...], ids[1] % 2, slice(None))

    attended_back = nt(branch_back, matrix(wo))
    count = middle.shape[0]
    carry = sublane((count, F)) < split_of(ids, lens, row, count)
    ones = segment_ones(PAIR)
    spot = lane((count, PAIR))
    for p in range(wire_o.shape[1]):
        at = slice(p * PAIR, (p + 1) * PAIR)
        given = attended_back[:, at]
        inverse = rden[:, at]
        numerator_back = given * inverse
        denominator_back = -segment_sum(given * att[:, at].astype(f32), ones) * inverse
        aux = pltpu.roll(denominator_back, HD, 1)
        high = aux.astype(bf16).astype(f32)
        rest = aux - high
        sums = []
        for h in range(2):
            first = HD if h == 0 else 0
            extended = with_aux(
                numerator_back,
                h,
                jnp.where(spot == first, high, jnp.where(spot == first + 1, rest, 0.0)),
            ).astype(bf16)
            column = slice((2 * p + h) * F, (2 * p + h + 1) * F)
            ext_o[:, column] = extended
            query = jnp.where(carry, phi_query[:, column].astype(f32), 0.0).astype(bf16)
            sums.append(tn(extended, query))
        put_wire(wire_o, p, sums[0], sums[1], ((HD, HD + 1), (0, 1)))


def map_gradient(pair, logits_back):
    both = tn(pair, logits_back)
    rows = pair_rows(both[:, :F], both[:, F:])
    return rows - pltpu.roll(rows, HD, 1)


def add_by_row(out, row, value):
    @pl.when(row == 0)
    def _():
        out[...] = value

    @pl.when(row > 0)
    def _():
        out[...] += value


def local_back_kernel(
    first, ids, lens, phi_query, phi_key, val, ext, wire, queries, maps, pq_o, kg_o, vg_o, mg_o
):
    row = pl.program_id(1) + first
    count = val.shape[0]
    split = split_of(ids, lens, row, count)
    flipped = block_masks(split, count, True)
    carry = sublane((count, F)) < split
    ones = segment_ones(2 * F)
    columns = [slice(h * F, (h + 1) * F) for h in range(4)]
    cuts = [slice(p * PAIR, (p + 1) * PAIR) for p in range(2)]
    pairs = [val[:, at].astype(f32) for at in cuts]
    extended = [with_aux(pairs[h // 2], h % 2, 1.0).astype(bf16) for h in range(4)]
    memories = [memory for p in range(2) for memory in take_wire(wire, p)]
    grads = [
        jnp.where(carry, nn(ext[:, columns[h]], memories[h]), 0.0) for h in range(4)
    ]
    blocks = [slice(first, first + SUB) for first in range(0, count, SUB)]
    heads, tops = [], []
    for h, at in enumerate(columns):
        back, scores = [], []
        for rows, mask in zip(blocks, flipped):
            on = slice(rows.start, count)
            back.append(masked(nt(extended[h][rows], ext[on, at]), mask))
            scores.append(masked(nt(phi_key[rows, at], phi_query[on, at]), mask))
        heads.append((back, scores))
    for h, at in enumerate(columns):
        back, scores = heads[h]
        value_parts = []
        for rows, given, score in zip(blocks, back, scores):
            on = slice(rows.start, count)
            kg_o[rows, at] = nn(given, phi_query[on, at])
            value_parts.append(nn(score, ext[on, at]))
        tops.append(jnp.concatenate(value_parts, axis=0))
        query_parts = []
        for i, rows in enumerate(blocks):
            part = [
                tn(given[:, rows.start - on.start : rows.stop - on.start], phi_key[on, at])
                for given, on in zip(back[: i + 1], blocks)
            ]
            query_parts.append(sum(part[1:], part[0]))
        grads[h] = grads[h] + jnp.concatenate(query_parts, axis=0)
    low = lane((count, PAIR)) < HD
    for p, at in enumerate(cuts):
        vg_o[:, at] = jnp.where(low, tops[2 * p], tops[2 * p + 1])
    logits_back = [
        features_back(
            phi_query[:, 2 * p * F : 2 * (p + 1) * F],
            jnp.concatenate(grads[2 * p : 2 * p + 2], axis=1),
            ones,
        ).astype(bf16)
        for p in range(2)
    ]
    for p, at in enumerate(cuts):
        pq_o[:, at] = nt(logits_back[p], map_weight(maps[at, :], False)).astype(bf16)
    gradient = [map_gradient(queries[:, at], logits_back[p]) for p, at in enumerate(cuts)]
    gradient = jnp.concatenate(gradient, axis=0)
    mg_o[...] = jnp.where(lane(gradient.shape) < HD, gradient, 0.0)


def keys_back_kernel(
    first, ids, lens, kg, vg, phi_key, val, wire, keys, maps, *rest
):
    *from_before, pk_o, pv_o, mg_o = rest
    row = pl.program_id(1) + first
    count = val.shape[0]
    split = split_of(ids, lens, row, count)
    begin = jnp.where(split < count, split, 0)
    last = sublane((count, F)) >= begin
    low = lane((count, PAIR)) < HD
    ones = segment_ones(2 * F)
    cuts = [slice(p * PAIR, (p + 1) * PAIR) for p in range(2)]
    logits_back = []
    for p, at in enumerate(cuts):
        pair = val[:, at].astype(f32)
        state = wire[0, p, 0:F, :]
        spot = sublane(state.shape)
        grads, tops = [], []
        for h, memory in enumerate(take_wire(wire, p)):
            column = slice((2 * p + h) * F, (2 * p + h + 1) * F)
            first = HD if h == 0 else 0
            own = (spot < HD) if h == 0 else (spot >= HD)
            memory = jnp.where(own | (spot == first), memory.astype(f32), 0.0).astype(bf16)
            extended = with_aux(pair, h, 1.0).astype(bf16)
            grads.append(kg[:, column] + jnp.where(last, nn(extended, memory), 0.0))
            tops.append(nt(phi_key[:, column], state))
        pv_o[:, at] = (
            vg[:, at] + jnp.where(last, jnp.where(low, tops[0], tops[1]), 0.0)
        ).astype(bf16)
        both = slice(2 * p * F, 2 * (p + 1) * F)
        logits_back.append(
            features_back(phi_key[:, both], jnp.concatenate(grads, axis=1), ones).astype(bf16)
        )
    for p, at in enumerate(cuts):
        pk_o[:, at] = nt(logits_back[p], map_weight(maps[at, :], True)).astype(bf16)
    gradient = jnp.concatenate(
        [
            pltpu.roll(map_gradient(keys[:, at], logits_back[p]), HD, 1)
            for p, at in enumerate(cuts)
        ],
        axis=0,
    )
    before = sum(part[...] for part in from_before)
    mg_o[...] = before + jnp.where(lane(gradient.shape) < HD, 0.0, gradient)


def weight_back_kernel(ids, lens, normed, pb, *rest):
    *refs, turned = rest

    @pl.when(pl.program_id(0) == 0)
    def _():
        turned[...] = normed[...].T

    put_halves(refs, nn(turned[...], pb[...]), ids[1] % 2, slice(None))


def key_weight_back_kernel(
    half, devices, ids, lens, normed, pk, pv, small_in, small_mid, hid, maps, *rest
):
    *refs, turned, lines = rest
    step = pl.program_id(0)
    core = ids[1] % 2

    @pl.when(step == 0)
    def _():
        turned[...] = normed[...].T

    @pl.when(step < half)
    def _():
        put_halves(refs, nn(turned[...], pk[...]), core, slice(None))

    @pl.when((step >= half) & (step < 2 * half))
    def _():
        put_halves(refs, nn(turned[...], pv[...]), core, slice(None))

    if devices:

        @pl.when(step == 2 * half)
        def _():
            pack(devices, core, small_in, small_mid, hid, maps, *refs, lines)


def input_back_kernel(pq, pk, pv, wq, wk, wv, tok, mb, gain, out_o, small_o):
    @pl.when(pl.program_id(0) == 0)
    def _():
        small_o[...] = jnp.zeros_like(small_o)

    from_norm = nt(pq[...], wq[...]) + nt(pk[...], wk[...]) + nt(pv[...], wv[...])
    xhat, scale = normalize(tok[...].astype(f32))
    small_o[0:1, :] += column_sum(from_norm * xhat)
    small_o[1:2, :] += column_sum(from_norm)
    for i, part in enumerate((pq, pk, pv)):
        small_o[2 + i : 3 + i, :] += column_sum(part[...].astype(f32))
    out_o[...] = (mb[...] + normalize_back(from_norm, xhat, scale, gain[...])).astype(bf16)


def spec(shape, index):
    return pl.BlockSpec(shape, index)


def estimate(micros):
    return pl.CostEstimate(
        flops=int(micros * PACE * 1e9), bytes_accessed=int(micros * PACE * 1e6), transcendentals=0
    )


def call(kernel, grid, ins, outs, scratch=(), scalars=0, name=None, micros=10, waits=(), into=()):
    waits = [*waits, *into]
    arrays = [entry[0] for entry in ins[scalars:]]
    if name not in FREE_INS:
        arrays = [pltpu.with_memory_space_constraint(array, pltpu.HBM) for array in arrays]
    arrays += waits
    fetched = [entry[0] for entry in ins[:scalars]]
    read = len(ins)

    def body(*refs):
        kernel(*refs[:read], *refs[read + len(waits) :])

    def shaped(shape, kind, block, index, free=False):
        free = free or name in FREE_OUTS
        return (jax.ShapeDtypeStruct if free else pltpu.HBM)(shape, kind)

    return pl.pallas_call(
        body,
        out_shape=[shaped(*out) for out in outs],
        grid_spec=pltpu.PrefetchScalarGridSpec(
            num_scalar_prefetch=scalars,
            grid=grid,
            in_specs=[spec(block, index) for _, block, index in ins[scalars:]]
            + [pl.BlockSpec(memory_space=pl.ANY)] * len(waits),
            out_specs=[spec(*out[2:4]) for out in outs],
            scratch_shapes=list(scratch),
        ),
        compiler_params=pltpu.CompilerParams(
            vmem_limit_bytes=LIMITS.get(name, LIMIT) * 1024 * 1024
        ),
        cost_estimate=estimate(micros),
        input_output_aliases={len(ins) + len(waits) - len(into) + i: i for i in range(len(into))},
        name=name,
    )(*fetched, *arrays)


def tie_kernel(*refs):
    del refs


def tie(values, *waits):
    anywhere = pl.BlockSpec(memory_space=pl.ANY)
    count = len(values)
    return pl.pallas_call(
        tie_kernel,
        out_shape=[jax.ShapeDtypeStruct(v.shape, v.dtype) for v in values],
        in_specs=[anywhere] * (count + len(waits)),
        out_specs=[anywhere] * count,
        input_output_aliases={i: i for i in range(count)},
        cost_estimate=estimate(0.5),
        name="tie",
    )(*values, *waits)


def gather_rows(part):
    return lax.all_gather(part, AXES, axis=0, tiled=True)


def scatter_rows(whole):
    return lax.psum_scatter(whole, AXES, scatter_dimension=0, tiled=True)


def scatter_columns(rows):
    return lax.psum_scatter(rows, AXES, scatter_dimension=1, tiled=True)


def swap(array, mask, axis="seq", name="swap"):
    size = lax.axis_size(axis)
    with jax.named_scope(name):
        return lax.ppermute(array, axis, [(i, i ^ mask) for i in range(size)])


def gather_cores(pieces, name):
    return pieces + [swap(piece, 1, name=name) for piece in pieces]


def put_piece(cuts, outs, at, piece):
    for out, first, last, sub in cuts:
        if sub is None:
            outs[out][at] = piece[:, first:last]
        else:
            outs[out][at, sub] = piece[:, first:last]


def place_kernel(cuts, ids, *refs):
    pieces, outs = refs[:8], refs[8:]

    def put(at, chips):
        for core in range(2):
            for piece, pair in zip(pieces[4 * core + at : 4 * core + at + 2], chips):
                for r, chip in enumerate(pair):
                    put_piece(cuts, outs, ids[1] ^ (2 * chip + core), piece[r, 0])

    @pl.when(pl.program_id(0) < 2)
    def _():
        put(0, ((0, 1), (2, 3)))

    @pl.when(pl.program_id(0) >= 2)
    def _():
        put(2, ((0, 2), (1, 3)))


def place(pieces, ids, cuts, shapes, name, micros, waits=()):
    rows, wide = pieces[0].shape[-2:]
    near = lambda s: jnp.minimum(s, 1)
    far = lambda s: jnp.maximum(s - 2, 0)
    ins = [
        (p.reshape(2, 2, rows, wide), (2, 1, rows, wide), lambda s, ids, at=at: (0, at(s), 0, 0))
        for p, at in zip(pieces, (near, near, far, far) * 2)
    ]

    def target(shape):
        return lambda s, ids: (ids[0] ^ s,) + (0,) * len(shape)

    return call(
        functools.partial(place_kernel, cuts),
        (4,),
        [(ids, None, None)] + ins,
        [((32, *shape), bf16, (8, *shape), target(shape)) for shape in shapes],
        [],
        1,
        name,
        micros,
        waits,
    )


def first_sum_kernel(parts, ids, *refs):
    ins, (near_keep, near_send, far_keep, far_send) = refs[: parts * 8], refs[parts * 8 :]
    step = pl.program_id(0)

    def put(targets):
        at = 0
        for part in range(parts):
            wide = ins[part * 8].shape[-1]
            for r, (out, i) in enumerate(targets):
                mine, got = ins[(part * 4 + r) * 2 : (part * 4 + r) * 2 + 2]
                total = mine[0, 0].astype(f32) + got[0, 0].astype(f32)
                out[i, 0, :, at : at + wide] = total.astype(bf16)
            at += wide

    @pl.when(step < 2)
    def _():
        put(((near_keep, 0), (near_send, 0), (near_keep, 1), (near_send, 1)))

    @pl.when(step >= 2)
    def _():
        put(((far_keep, 0), (far_keep, 1), (far_send, 0), (far_send, 1)))


def first_sum(mines, gots, ids, name, micros=4, waits=()):
    rows = mines[0].shape[-2]
    wides = [m.shape[-1] for m in mines]
    ins = [(ids, None, None)]

    def index(r):
        return lambda k, ids: (ids[0] ^ k, (ids[1] // 2) ^ r, 0, 0)

    for mine, got, wide in zip(mines, gots, wides):
        for r in range(4):
            for array in (mine, got):
                ins.append((array.reshape(4, 4, rows, wide), (1, 1, rows, wide), index(r)))
    total = sum(wides)
    near = lambda k, ids: (0, jnp.minimum(k, 1), 0, 0)
    far = lambda k, ids: (0, jnp.maximum(k - 2, 0), 0, 0)
    return call(
        functools.partial(first_sum_kernel, len(mines)),
        (4,),
        ins,
        [
            ((2, 2, rows, total), bf16, (2, 1, rows, total), at)
            for at in (near, near, far, far)
        ],
        [],
        1,
        name,
        micros,
        waits,
    )


def middle_sum_kernel(near_keep, near_got, far_keep, far_got, *outs):
    for at, (kept, got) in enumerate(((near_keep, near_got), (far_keep, far_got))):
        for i in range(2):
            total = kept[i].astype(f32) + got[i].astype(f32)
            outs[2 * at + i][...] = total.astype(bf16)


def middle_sum(sums, name, micros=3, waits=()):
    near_keep, near_send, far_keep, far_send = sums
    pieces = [near_keep, swap(near_send, 2, name=name + "_x1")]
    pieces += [far_keep, swap(far_send, 4, name=name + "_y1")]
    _, _, rows, wide = near_keep.shape
    tile = 1536 if wide % 1536 == 0 else wide
    near_keep, near_send, far_keep, far_send = call(
        middle_sum_kernel,
        (wide // tile,),
        [(p, (2, 2, rows, tile), lambda g: (0, 0, 0, g)) for p in pieces],
        [((2, rows, wide), bf16, (2, rows, tile), lambda g: (0, 0, g))] * 4,
        [],
        0,
        name,
        micros,
        waits,
    )
    near_got, far_got = swap(near_send, 4, name=name + "_y2"), swap(far_send, 2, name=name + "_x2")
    return [near_keep, near_got, far_keep, far_got]


def second_sum_kernel(direct, near, near_got, far, far_got, *outs):
    for k in range(4):
        kept, got = (near, near_got) if k < 2 else (far, far_got)
        total = kept[k % 2].astype(f32) + got[k % 2].astype(f32)
        if direct:
            outs[k][...] = total.astype(outs[k].dtype)
        else:
            outs[k // 2][k % 2] = total.astype(outs[k // 2].dtype)


def second_sum(pieces, name, micros=3, waits=(), direct=True):
    _, rows, wide = pieces[0].shape
    tile = 1536 if wide % 1536 == 0 else wide
    if direct:
        shape, cut = (rows, wide), (rows, tile)
        outs = [(shape, bf16 if k else f32, cut, lambda g: (0, g)) for k in range(4)]
    else:
        shape, cut = (2, rows, wide), (2, rows, tile)
        outs = [(shape, bf16 if k else f32, cut, lambda g: (0, 0, g)) for k in range(2)]
    return call(
        functools.partial(second_sum_kernel, direct),
        (wide // tile,),
        [(p, (2, rows, tile), lambda g: (0, 0, g)) for p in pieces],
        outs,
        [],
        0,
        name,
        micros,
        waits,
    )


def reduce_batch(sums, name):
    total = sums[0]
    for k in range(1, 4):
        total = total + swap(sums[k], k, "batch", name + "_layer").astype(f32)
    return total


def reduce_layer2(sums, name, waits):
    (kept,) = tie(sums[:1], *waits)
    return kept + swap(sums[1], 2, "batch", name + "_layer2").astype(f32)


def reduce_layer1(pair, name, waits):
    got = swap(pair[1].astype(bf16), 1, "batch", name + "_layer1")
    (kept,) = tie([pair[0]], *waits)
    return kept + got.astype(f32)


def spots(length, each, owners):
    at = lane((F, length))
    owner = ((at.astype(f32) + 0.5) * (1.0 / each)).astype(jnp.int32)
    inside = (at - owner * each == sublane((F, length))).astype(bf16)
    at = lane((owners.shape[0], length))
    owner = ((at.astype(f32) + 0.5) * (1.0 / each)).astype(jnp.int32)
    return inside, owner == owners


def unpack_kernel(devices, block, *outs):
    rows = block.shape[0] // devices
    vectors = [(out, i) for out in outs for i in range(out.shape[0])]
    count = len(vectors)
    place_at = lane((count * devices, block.shape[0]))
    line = sublane((count * devices, block.shape[0]))
    vector = ((line.astype(f32) + 0.5) * (1.0 / devices)).astype(jnp.int32)
    picked = nn(
        (place_at == (line - vector * devices) * rows + vector).astype(bf16), block[...]
    ).astype(bf16)
    for j, (out, i) in enumerate(vectors):
        length = out.shape[1]
        owners = sublane((devices, length))
        inside, owned = spots(length, length // devices, owners)
        spread = nn(picked[j * devices : (j + 1) * devices], inside)
        out[i : i + 1, :] = column_sum(jnp.where(owned, spread, 0.0))


def shards_kernel(
    gain, shift, mix, offset, maps, out, branch, ex, hid, sh, first_o, rest_o, small
):
    rows = mix.shape[0]
    small[...] = jnp.zeros_like(small)
    for j, part in enumerate((gain, shift, branch)):
        small[2 * j : 2 * j + 2, 0:rows] = part[...].astype(f32)
    small[6:7, 0 : 3 * rows] = offset[...].astype(f32)
    small[7:8, 0 : 4 * rows] = hid[...].astype(f32)
    wide, width = mix.shape[1], sh.shape[1]
    first_o[:, 0:wide] = mix[...]
    first_o[:, wide : wide + F] = maps[...]
    first_o[:, wide + F : wide + 2 * F] = small[...].astype(bf16)
    for i in range(4):
        rest_o[i] = ex[:, i * width : (i + 1) * width]
        rest_o[4 + i] = sh[i * rows : (i + 1) * rows, :].astype(f32).astype(bf16)
    rest_o[8] = out[...]


def pack(devices, core, small_in, small_mid, hid, maps, mine_o, other_o, lines):
    offset = jnp.concatenate([small_in[i : i + 1, :] for i in range(2, 5)], axis=1)
    lines[...] = jnp.zeros_like(lines)
    vectors = [
        small_in[0:1, :],
        small_mid[0:1, :],
        small_in[1:2, :],
        small_mid[1:2, :],
        small_mid[2:3, :],
        small_mid[3:4, :],
        offset,
        hid[...],
    ]
    half = devices // 2
    for j, vector in enumerate(vectors):
        length = vector.shape[1]
        line = sublane((devices, length))
        owners = jnp.where(line < half, 2 * line + core, 2 * (line - half) + 1 - core)
        inside, owned = spots(length, length // devices, owners)
        share = jnp.where(owned, vector, 0.0).astype(bf16)
        lines[:, j, :] = nt(share, inside)
    put_halves((mine_o, other_o), maps[...], core, slice(0, F))
    mine_o[:, :, F:] = lines[:half].astype(bf16)
    other_o[:, :, F:] = lines[half:].astype(bf16)


def flags_kernel(levels, count, ids, lens, *outs):
    mine = ids[1]
    for row in range(lens.shape[0]):
        flags = []
        for reverse in (False, True):
            for level in range(levels):
                span = 1 << level
                begin = mine - lax.rem(mine, span)
                upper = lax.rem(mine // span, 2) == 1
                own_closed = starts_within(lens, row, begin * count, (begin + span) * count)
                if reverse:
                    receives = jnp.logical_not(upper)
                    closed = starts_within(lens, row, (mine + 1) * count, (begin + span) * count)
                    other = starts_within(lens, row, (begin - span) * count, begin * count)
                else:
                    receives = upper
                    closed = starts_within(lens, row, begin * count, mine * count)
                    other = starts_within(
                        lens, row, (begin + span) * count, (begin + 2 * span) * count
                    )
                flags.append(receives & jnp.logical_not(closed))
                flags.append(receives | jnp.logical_not(other))
                flags.append(jnp.logical_not(receives & own_closed))
        for out, flag in zip(outs, flags):
            out[row] = jnp.full((1, 1, F), jnp.where(flag, 1.0, 0.0), f32)


def carry(total, reached, flags, level, reverse, waits=()):
    levels = len(flags) // 6
    at = 3 * (level + (levels if reverse else 0))
    reaches, keeps, joins = flags[at : at + 3]
    if len(waits):
        reaches, keeps, joins = tie([reaches, keeps, joins], *waits)
    other = swap(total, 1 << level, name=f"state{level}").astype(f32)
    arrived = reaches * other
    reached = arrived if reached is None else reached + arrived
    if level == levels - 1:
        return None, reached.astype(bf16)
    return (keeps * total.astype(f32) + joins * other).astype(bf16), reached


def local(
    tokens,
    sequence_lengths,
    norm_gains,
    norm_shifts,
    mixing_weight,
    mixing_offset,
    feature_maps,
    output_weight,
    branch_offsets,
    expand_weight,
    hidden_offset,
    shrink_weight,
    cotangent,
):
    row_count, tok_count, width = tokens.shape
    count = row_count * tok_count
    heads = width // HD
    pairs, quads = heads // 2, heads // 4
    quad = 2 * PAIR
    hidden_width = expand_weight.shape[1]
    batch, size = lax.axis_size("batch"), lax.axis_size("seq")
    devices = batch * size
    share = width // devices
    plain = size != 8 or batch != 4 or share % 8 != 0 or hidden_width != 4 * width or 4 * share > F

    mine = lax.axis_index("seq").astype(jnp.int32)
    ids = jnp.stack([lax.axis_index("batch").astype(jnp.int32), mine])
    lens = sequence_lengths
    scalars = [(ids, None, None), (lens, None, None)]
    levels = size.bit_length() - 1
    flag = (row_count, 1, 1, F)
    flags = call(
        functools.partial(flags_kernel, levels, tok_count),
        (1,),
        scalars,
        [(flag, f32, flag, lambda i, *s: (0, 0, 0, 0))] * (6 * levels),
        [],
        2,
        "flags",
        1,
    )

    if plain:
        gains = lax.all_gather(norm_gains, AXES, axis=1, tiled=True).astype(f32)[:, None]
        shifts = lax.all_gather(norm_shifts, AXES, axis=1, tiled=True).astype(f32)[:, None]
        branches = lax.all_gather(branch_offsets, AXES, axis=1, tiled=True).astype(f32)[:, None]
        offset = gather_rows(mixing_offset).astype(f32)[None]
        hidden_bias = gather_rows(hidden_offset).astype(f32)[None]
        first_weight = jnp.concatenate(
            [gather_rows(mixing_weight), gather_rows(feature_maps)], axis=1
        )
        out_weight = gather_rows(output_weight)
        expand = gather_rows(expand_weight)
        shrink = gather_rows(shrink_weight)
    else:
        wide = 3 * width + 2 * F
        shards = (
            norm_gains,
            norm_shifts,
            mixing_weight,
            mixing_offset[None],
            feature_maps,
            output_weight,
            branch_offsets,
            expand_weight,
            hidden_offset[None],
            shrink_weight,
        )
        at = lambda i: (0, 0)
        first, rest = call(
            shards_kernel,
            (1,),
            [(array, array.shape, at) for array in shards],
            [
                ((share, wide), bf16, (share, wide), at),
                ((9, share, width), bf16, (9, share, width), lambda i: (0, 0, 0)),
            ],
            [pltpu.VMEM((share, F), f32)],
            0,
            "shards",
            2,
        )
        layers = [first] + [swap(first, k, "batch", "first_layer") for k in range(1, 4)]
        near, far = jnp.stack(layers[:2]), jnp.stack(layers[2:])
        rest = lax.all_gather(rest, AXES)
        near = jnp.concatenate([near, swap(near, 2, name="first_x1")])
        far = jnp.concatenate([far, swap(far, 4, name="first_y1")])
        first = [
            near,
            swap(near, 4, name="first_y2"),
            far,
            swap(far, 2, name="first_x2"),
        ]
        first = gather_cores(first, "first_core")
        (first_weight,) = place(
            first, ids, ((0, 0, wide, None),), ((share, wide),), "place_first", 5
        )
        first_weight = first_weight.reshape(width, -1)
        *rows_out, offset, hidden_bias = call(
            functools.partial(unpack_kernel, devices),
            (1,),
            [(first_weight, (width, F), lambda i: (0, 3 * width // F + 1))],
            [
                ((n, length), f32, (n, length), lambda i: (0, 0))
                for n, length in [(1, width)] * 6 + [(1, 3 * width), (1, hidden_width)]
            ],
            [],
            0,
            "unpack",
            2,
        )
        gains, shifts, branches = (rows_out[i : i + 2] for i in (0, 2, 4))

    tok = tokens.reshape(count, width)
    cot = cotangent.reshape(count, width)
    full = lambda r, q, *s: (0, 0)

    def columns(first):
        return lambda r, q, *s: (0, first + q)

    own = lambda r, q, *s: (r, 0)
    cell = lambda r, q, *s: (r, q)
    normed, keys, values, phi_key, wire = call(
        keys_kernel,
        (row_count, quads),
        [
            *scalars,
            (tok, (tok_count, width), own),
            (gains[0], (1, width), full),
            (shifts[0], (1, width), full),
            (first_weight, (width, quad), columns(quads)),
            (first_weight, (width, quad), columns(2 * quads)),
            (offset, (1, quad), columns(quads)),
            (offset, (1, quad), columns(2 * quads)),
            (first_weight, (quad, F), lambda r, q, *s: (q, 3 * width // F)),
        ],
        [
            ((count, width), bf16, (tok_count, width), own),
            ((count, width), bf16, (tok_count, quad), cell),
            ((count, width), bf16, (tok_count, quad), cell),
            ((count, heads * F), bf16, (tok_count, 4 * F), cell),
            (
                (row_count, pairs, WIRE, F),
                bf16,
                (1, 2, WIRE, F),
                lambda r, q, *s: (r, q, 0, 0),
            ),
        ],
        [pltpu.VMEM((tok_count, width), bf16)],
        2,
        "keys",
        15,
        flags,
    )
    queries, phi_query = call(
        queries_kernel,
        (row_count, quads),
        [
            (normed, (tok_count, width), own),
            (first_weight, (width, quad), columns(0)),
            (offset, (1, quad), columns(0)),
            (first_weight, (quad, F), lambda r, q, *s: (q, 3 * width // F)),
        ],
        [
            ((count, width), bf16, (tok_count, quad), cell),
            ((count, heads * F), bf16, (tok_count, 4 * F), cell),
        ],
        [],
        0,
        "queries",
        8,
    )
    total, reached = carry(wire, None, flags, 0, False)
    total, reached = carry(total, reached, flags, 1, False, (phi_query,))
    (numerator,) = call(
        attention_kernel,
        (row_count, quads),
        [
            *scalars,
            (phi_query, (tok_count, 4 * F), cell),
            (phi_key, (tok_count, 4 * F), cell),
            (values, (tok_count, quad), cell),
        ],
        [((count, heads * F), f32, (tok_count, 4 * F), cell)],
        [],
        2,
        "attention",
        12,
        (total,),
    )
    for level in range(2, levels):
        total, reached = carry(total, reached, flags, level, False, (numerator,))
    memory = reached
    if plain:
        out_part = (out_weight, (width, width), lambda r, *s: (0, 0))
        expand_part = (expand, (width, width), lambda f, *s: (0, f))
        shrink_part = (shrink, (width, width), lambda f, *s: (f, 0))
    else:
        cut = (devices, 1, share, width)
        out_part = (rest, cut, lambda r, *s: (0, 8, 0, 0))
        expand_part = (rest, cut, lambda f, *s: (0, f, 0, 0))
        cut = (devices // 4, 4, share, width)
        shrink_part = (rest, cut, lambda f, *s: (f, 1, 0, 0))
    one = lambda r, *s: (r, 0)
    whole = lambda r, *s: (0, 0)
    attended, inverse, middle, normed_mid = call(
        middle_kernel,
        (row_count,),
        [
            *scalars,
            (numerator, (tok_count, heads * F), one),
            (phi_query, (tok_count, heads * F), one),
            (memory, (1, pairs, WIRE, F), lambda r, *s: (r, 0, 0, 0)),
            (tok, (tok_count, width), one),
            out_part,
            (branches[0], (1, width), whole),
            (gains[1], (1, width), whole),
            (shifts[1], (1, width), whole),
        ],
        [
            ((count, width), bf16, (tok_count, width), one),
            ((count, width), f32, (tok_count, width), one),
            ((count, width), f32, (tok_count, width), one),
            ((count, width), bf16, (tok_count, width), one),
        ],
        [],
        2,
        "middle",
        9,
    )
    tile = width
    steps = hidden_width // tile

    def halves(wide, block, index):
        if plain:
            return [((width, wide), f32, (width, block), lambda *i: (0, index(*i)))]
        shape = (devices // 2, share, wide)
        cut = (devices // 2, share, block)
        return [(shape, bf16, cut, lambda *i: (0, 0, index(*i)), True)] * 2

    y, normed_mid_back, hidden_grad, *mlp_grads = call(
        functools.partial(mlp_kernel, plain),
        (steps,),
        [
            *scalars,
            (normed_mid, (count, width), lambda f, *s: (0, 0)),
            (cot, (count, width), lambda f, *s: (0, 0)),
            expand_part,
            shrink_part,
            (hidden_bias, (1, tile), lambda f, *s: (0, f)),
        ],
        [
            ((count, width), f32, (count, width), lambda f, *s: (0, 0)),
            ((count, width), f32, (count, width), lambda f, *s: (0, 0)),
            ((1, hidden_width), f32, (1, tile), lambda f, *s: (0, f)),
            *halves(hidden_width, tile, lambda f, *s: f),
            *(
                [((hidden_width, width), f32, (tile, width), lambda f, *s: (f, 0))]
                if plain
                else [
                    (
                        (devices // 2, share, 4 * width),
                        bf16,
                        (devices // 2 // steps, share, 4 * width),
                        lambda f, *s: (f, 0, 0),
                        True,
                    )
                ]
                * 2
            ),
        ],
        [pltpu.VMEM((width, count), bf16)],
        2,
        "mlp",
        37,
    )
    layer_output, middle_back, extended, wire_back, small_mid, *output_grads = call(
        middle_back_kernel,
        (row_count,),
        [
            *scalars,
            (middle, (tok_count, width), one),
            (y, (tok_count, width), one),
            (normed_mid_back, (tok_count, width), one),
            (cot, (tok_count, width), one),
            (attended, (tok_count, width), one),
            (inverse, (tok_count, width), one),
            (phi_query, (tok_count, heads * F), one),
            out_part,
            (gains[1], (1, width), whole),
            (branches[1], (1, width), whole),
        ],
        [
            ((count, width), bf16, (tok_count, width), one),
            ((count, width), f32, (tok_count, width), one),
            ((count, heads * F), bf16, (tok_count, heads * F), one),
            ((row_count, pairs, WIRE, F), bf16, (1, pairs, WIRE, F), lambda r, *s: (r, 0, 0, 0)),
            ((8, width), f32, (8, width), whole),
            *halves(width, width, lambda r, *s: 0),
        ],
        [pltpu.VMEM((width, width), f32)],
        2,
        "middle_back",
        17,
    )
    total, reached = carry(wire_back, None, flags, 0, True)
    if not plain:
        expand_mine, expand_other, shrink_mine, shrink_other = mlp_grads
        mlp_waits = first_sum(
            (expand_mine, shrink_mine),
            (swap(expand_other, 1, name="mlp_core"), swap(shrink_other, 1, name="mlp_core")),
            ids,
            "mlp_first_sum",
            7,
            (total,),
        )
    cell = lambda p, r, *s: (r, p)
    of_pair = lambda p, r, *s: (p, 0)
    from_wire = lambda p, r, *s: (r, p, 0, 0)

    def attend_back(first, into=(), waits=()):
        cell = lambda p, r, *s: (r + first, p)
        from_wire = lambda p, r, *s: (r + first, p, 0, 0)
        return call(
            functools.partial(local_back_kernel, first),
            (quads, 1),
            [
                *scalars,
                (phi_query, (tok_count, 4 * F), cell),
                (phi_key, (tok_count, 4 * F), cell),
                (values, (tok_count, quad), cell),
                (extended, (tok_count, 4 * F), cell),
                (memory, (1, 2, WIRE, F), from_wire),
                (queries, (tok_count, quad), cell),
                (first_weight, (quad, F), lambda p, r, *s: (p, 3 * width // F)),
            ],
            [
                ((count, width), bf16, (tok_count, quad), cell),
                ((count, heads * F), f32, (tok_count, 4 * F), cell),
                ((count, width), f32, (tok_count, quad), cell),
                ((width, F), f32, (quad, F), of_pair),
            ],
            [],
            2,
            "local_back",
            25 / row_count,
            waits,
            into,
        )

    partial, maps_query = (), []
    for level in range(1, levels):
        if level <= row_count:
            waits = (total, *(mlp_waits[:1] if level == 1 and not plain else ()))
            *partial, map_query = attend_back(level - 1, partial, waits)
            maps_query.append(map_query)
        total, reached = carry(total, reached, flags, level, True, partial[:1])
        if level == 1 and not plain:
            mlp_waits = [mlp_waits[0], *tie(mlp_waits[1:2], total), *mlp_waits[2:]]
    for first in range(levels - 1, row_count):
        *partial, map_query = attend_back(first, partial)
        maps_query.append(map_query)
    queries_back, key_feat, value_feat = partial
    memory_back = reached

    def weight_back(pb, waits=()):
        return call(
            weight_back_kernel,
            (quads,),
            [
                *scalars,
                (normed, (count, width), lambda q, *s: (0, 0)),
                (pb, (count, quad), lambda q, *s: (0, q)),
            ],
            halves(width, quad, lambda q, *s: q),
            [pltpu.VMEM((width, count), bf16)],
            2,
            "weight_back",
            5,
            waits,
        )

    query_grads = weight_back(queries_back)

    def attend_keys_back(first, map_grads, into=(), waits=()):
        cell = lambda p, r, *s: (r + first, p)
        return call(
            functools.partial(keys_back_kernel, first),
            (quads, 1),
            [
                *scalars,
                (key_feat, (tok_count, 4 * F), cell),
                (value_feat, (tok_count, quad), cell),
                (phi_key, (tok_count, 4 * F), cell),
                (values, (tok_count, quad), cell),
                (
                    memory_back,
                    (1, 2, WIRE, F),
                    lambda p, r, *s: (r + first, p, 0, 0),
                ),
                (keys, (tok_count, quad), cell),
                (first_weight, (quad, F), lambda p, r, *s: (p, 3 * width // F)),
                *[(map_grad, (quad, F), of_pair) for map_grad in map_grads],
            ],
            [
                ((count, width), bf16, (tok_count, quad), cell),
                ((count, width), bf16, (tok_count, quad), cell),
                ((width, F), f32, (quad, F), of_pair),
            ],
            [],
            2,
            "keys_back",
            13 / row_count,
            waits,
            into,
        )

    *partial, map_grad = attend_keys_back(0, maps_query, (), query_grads[:1])
    if not plain:
        mlp_sums = middle_sum(mlp_waits, "mlp_middle_sum", 4, partial[:1])
        query_waits = first_sum(
            (query_grads[0], output_grads[0]),
            (swap(query_grads[1], 1, name="query_core"), swap(output_grads[1], 1, name="query_core")),
            ids,
            "query_first_sum",
            3,
            mlp_sums[:1],
        )
    for first in range(1, row_count):
        waits = () if plain else query_waits[:1]
        *partial, map_grad = attend_keys_back(first, [map_grad], partial, waits)
    keys_back, values_back = partial
    if not plain:
        mlp_sums = second_sum(mlp_sums, "mlp_second_sum", 4, (keys_back,), False)
    row = lambda r: (r, 0)
    fixed = lambda r: (0, 0)
    input_gradient, small_in = call(
        input_back_kernel,
        (row_count,),
        [
            (queries_back, (tok_count, width), row),
            (keys_back, (tok_count, width), row),
            (values_back, (tok_count, width), row),
            (first_weight, (width, width), lambda r: (0, 0)),
            (first_weight, (width, width), lambda r: (0, 1)),
            (first_weight, (width, width), lambda r: (0, 2)),
            (tok, (tok_count, width), row),
            (middle_back, (tok_count, width), row),
            (gains[0], (1, width), fixed),
        ],
        [
            ((count, width), bf16, (tok_count, width), row),
            ((8, width), f32, (8, width), fixed),
        ],
        [],
        0,
        "input_back",
        10,
        () if plain else mlp_sums[1:2],
    )
    if not plain:
        query_sums = middle_sum(query_waits, "query_middle_sum", 2, (input_gradient,))
    small_parts = [
        (array, array.shape, lambda q, *s: (0, 0))
        for array in (small_in, small_mid, hidden_grad, map_grad)
    ]
    key_grads = call(
        functools.partial(key_weight_back_kernel, quads, 0 if plain else devices),
        (2 * quads + (0 if plain else 1),),
        [
            *scalars,
            (normed, (count, width), lambda q, *s: (0, 0)),
            (keys_back, (count, quad), lambda q, *s: (0, jnp.minimum(q, quads - 1))),
            (
                values_back,
                (count, quad),
                lambda q, *s: (0, jnp.clip(q - quads, 0, quads - 1)),
            ),
            *small_parts,
        ],
        halves(2 * width + (0 if plain else quad), quad, lambda q, *s: q),
        [pltpu.VMEM((width, count), bf16), pltpu.VMEM((devices, share, F), f32)],
        2,
        "key_weight_back",
        10,
        () if plain else query_sums[:1],
    )
    if plain:
        mixing_grad = jnp.concatenate([query_grads[0], key_grads[0]], axis=1)
        offset_grad = small_in[2:5].reshape(-1)
        grads = (
            scatter_columns(jnp.stack([small_in[0], small_mid[0]])),
            scatter_columns(jnp.stack([small_in[1], small_mid[1]])),
            scatter_rows(mixing_grad),
            scatter_rows(offset_grad),
            scatter_rows(map_grad),
            scatter_rows(output_grads[0]),
            scatter_columns(small_mid[2:4]),
            scatter_rows(mlp_grads[0]),
            scatter_rows(hidden_grad[0]),
            scatter_rows(mlp_grads[1]),
        )
    else:
        query_sums = second_sum(query_sums, "query_second_sum", 3, (key_grads[0],), False)
        mlp_pair = reduce_layer2(mlp_sums, "mlp", query_sums[:1])
        key_sums = first_sum(
            (key_grads[0],),
            (swap(key_grads[1], 1, name="key_core"),),
            ids,
            "key_first_sum",
            4,
            (mlp_pair,),
        )
        query_pair = reduce_layer2(query_sums, "query", key_sums[:1])
        key_sums = middle_sum(key_sums, "key_middle_sum", 2, (query_pair,))
        key_sums = second_sum(key_sums, "key_second_sum")
        mlp_total = reduce_layer1(mlp_pair, "mlp", key_sums[:1])
        query_total = reduce_layer1(query_pair, "query", key_sums[:1])
        key_total = reduce_batch(key_sums, "key")
        small_total = key_total[0:8, 2 * width + F :]
        mixing_grad = jnp.concatenate(
            [query_total[:, :width], key_total[:, : 2 * width]], axis=1
        )
        shrink_grad = mlp_total[:, hidden_width:].reshape(share, 4, width)
        grads = (
            small_total[0:2, :share],
            small_total[2:4, :share],
            mixing_grad,
            small_total[6, : 3 * share],
            key_total[:, 2 * width : 2 * width + F],
            query_total[:, width:],
            small_total[4:6, :share],
            mlp_total[:, :hidden_width],
            small_total[7, : 4 * share],
            shrink_grad.transpose(1, 0, 2).reshape(4 * share, width),
        )
    return (layer_output.reshape(tokens.shape), input_gradient.reshape(tokens.shape), *grads)


def solution(mesh):
    rows = P("batch", "seq", None)
    split_rows = P(AXES, None)
    split_columns = P(None, AXES)
    split_vector = P(AXES)
    return jax.shard_map(
        local,
        mesh=mesh,
        in_specs=(
            rows,
            P("batch", None),
            split_columns,
            split_columns,
            split_rows,
            split_vector,
            split_rows,
            split_rows,
            split_columns,
            split_rows,
            split_vector,
            split_rows,
            rows,
        ),
        out_specs=(
            rows,
            rows,
            split_columns,
            split_columns,
            split_rows,
            split_vector,
            split_rows,
            split_rows,
            split_columns,
            split_rows,
            split_vector,
            split_rows,
        ),
        check_vma=False,
    )
```

```python
import functools

import jax
import jax.numpy as jnp
from jax import lax
from jax.experimental import pallas as pl
from jax.experimental.pallas import tpu as pltpu
from jax.sharding import PartitionSpec as P

HD = 64
F = 2 * HD
PAIR = 2 * HD
SUB = 256
WIRE = F + 16
EPSILON = 1e-05
AXES = ("batch", "seq")
LIMIT = 28
LIMITS = {"mlp": 56, "attention": 32, "middle_back": 40, "local_back": 40, "middle": 40, "input_back": 32}
SUMS = {
    group + part
    for group in ("mlp", "query", "key")
    for part in ("_first_sum", "_middle_sum", "_second_sum")
}
FREE_INS = SUMS | {"place_first", "unpack", "keys", "queries"}
PACE = 0.01
bf16 = jnp.bfloat16
f32 = jnp.float32


def dot(a, b, left, right):
    return lax.dot_general(a, b, (((left,), (right,)), ((), ())), preferred_element_type=f32)


def nn(a, b):
    return dot(a, b, 1, 0)


def nt(a, b):
    return dot(a, b, 1, 1)


def tn(a, b):
    return dot(a, b, 0, 0)


def lane(shape):
    return lax.broadcasted_iota(jnp.int32, shape, len(shape) - 1)


def sublane(shape):
    return lax.broadcasted_iota(jnp.int32, shape, len(shape) - 2)


def normalize(values):
    center = jnp.mean(values, axis=-1, keepdims=True)
    centered = values - center
    spread = jnp.mean(centered * centered, axis=-1, keepdims=True)
    scale = lax.rsqrt(spread + EPSILON)
    return centered * scale, scale


def normalize_back(upstream, xhat, scale, gain):
    entry = upstream * gain
    first = jnp.mean(entry, axis=-1, keepdims=True)
    second = jnp.mean(entry * xhat, axis=-1, keepdims=True)
    return scale * (entry - first - xhat * second)


def map_weight(rows, keys):
    rows = rows.astype(f32)
    turned = pltpu.roll(rows, HD, 1)
    low = lane(rows.shape) < HD
    signed = jnp.where(low, turned, -rows) if keys else jnp.where(low, rows, -turned)
    top = sublane(rows.shape) < HD
    return jnp.concatenate(
        [jnp.where(top, signed, 0.0), jnp.where(top, 0.0, signed)], axis=1
    ).astype(bf16)


def segment_ones(width):
    shape = (width, width)
    return (lane(shape) // HD == sublane(shape) // HD).astype(bf16)


def segment_sum(values, ones):
    high = values.astype(bf16)
    low = (values - high.astype(f32)).astype(bf16)
    return nn(high, ones) + nn(low, ones)


def features(logits, ones):
    parts = []
    for at in range(0, logits.shape[1], F):
        part = logits[:, at : at + F]
        low = lane(part.shape) < HD
        first = jnp.max(jnp.where(low, part, -jnp.inf), axis=1, keepdims=True)
        second = jnp.max(jnp.where(low, -jnp.inf, part), axis=1, keepdims=True)
        parts.append(jnp.exp(part - jnp.where(low, first, second)))
    powers = jnp.concatenate(parts, axis=1)
    return powers / nn(powers.astype(bf16), ones)


def features_back(phi, upstream, ones):
    phi = phi.astype(f32)
    return phi * (upstream - segment_sum(phi * upstream, ones))


def split_of(ids, lens, row, count):
    first = ids[1] * count
    start, split = 0, count
    for n in range(lens.shape[1]):
        inside = (start >= first) & (start < first + count)
        split = jnp.where(inside, start - first, split)
        start = start + lens[row, n]
    return split


def starts_within(lens, row, low, high):
    start, found = 0, 0
    for n in range(lens.shape[1]):
        found = found | jnp.where((start >= low) & (start < high), 1, 0)
        start = start + lens[row, n]
    return found == 1


def matrix(ref):
    value = ref[...]
    return value if value.ndim == 2 else value.reshape(-1, value.shape[-1])


def with_aux(pair, head, aux):
    own = (lane(pair.shape) < HD) if head == 0 else (lane(pair.shape) >= HD)
    return jnp.where(own, pair, aux)


def pair_rows(first, second):
    top = sublane(first.shape) < HD
    return jnp.where(top, first, second)


def put_wire(ref, at, first, second, aux_rows):
    ref[0, at, 0:F, :] = pair_rows(first, second).astype(bf16)
    sums = [sum(x[a : a + 1] for a in rows) for x, rows in zip((first, second), aux_rows)]
    row = sublane((16, F))
    ref[0, at, F:WIRE, :] = jnp.where(
        row == 0, sums[0], jnp.where(row == 1, sums[1], 0.0)
    ).astype(bf16)


def arrived(refs, at):
    half = len(refs) // 2
    return sum(
        reach[0, 0] * wire[0, at].astype(f32) for wire, reach in zip(refs[:half], refs[half:])
    ).astype(bf16)


def take_wire(both):
    state, sums = both[0:F], both[F:WIRE]
    top = sublane(state.shape) < HD
    return jnp.where(top, state, sums[0:1]), jnp.where(top, sums[1:2], state)


def block_masks(split, count, flipped):
    masks = []
    for first in range(0, count, SUB):
        if flipped:
            shape = (SUB, count - first)
            i, j = lane(shape) + first, sublane(shape) + first
        else:
            shape = (SUB, first + SUB)
            i, j = sublane(shape) + first, lane(shape)
        masks.append(((i < split) | (j >= split)) & (j <= i))
    return masks


def masked(scores, mask):
    return jnp.where(mask, scores, 0.0).astype(bf16)


def keys_kernel(
    ids, lens, tok, gain, shift, wk, wv, ok, ov, maps, normed_o, turned_o, k_o, v_o, phi_o, wire_o, kept
):
    row, quad = pl.program_id(0), pl.program_id(1)

    @pl.when(quad == 0)
    def _():
        xhat, _ = normalize(tok[...].astype(f32))
        normed = (xhat * gain[...] + shift[...]).astype(bf16)
        kept[...] = normed
        normed_o[...] = normed
        turned_o[...] = normed.T

    normed = kept[...]
    keys = (nn(normed, wk[...]) + ok[...]).astype(bf16)
    values = (nn(normed, wv[...]) + ov[...]).astype(bf16)
    k_o[...] = keys
    v_o[...] = values
    count = keys.shape[0]
    split = split_of(ids, lens, row, count)
    begin = jnp.where(split < count, split, 0)
    last = sublane((count, PAIR)) >= begin
    ones = segment_ones(2 * F)
    cuts = [slice(p * PAIR, (p + 1) * PAIR) for p in range(2)]
    logits = [nn(keys[:, at], map_weight(maps[at, :], True)) for at in cuts]
    phis = [features(part, ones).astype(bf16) for part in logits]
    for p, at in enumerate(cuts):
        phi_o[:, 2 * p * F : 2 * (p + 1) * F] = phis[p]
    for p, at in enumerate(cuts):
        pair = values[:, at].astype(f32)
        sums = [
            tn(
                jnp.where(last, with_aux(pair, h, 1.0), 0.0).astype(bf16),
                phis[p][:, h * F : (h + 1) * F],
            )
            for h in range(2)
        ]
        put_wire(wire_o, p, sums[0], sums[1], ((HD,), (0,)))


def queries_kernel(normed, wq, oq, maps, q_o, phi_o):
    queries = (nn(normed[...], wq[...]) + oq[...]).astype(bf16)
    q_o[...] = queries
    ones = segment_ones(2 * F)
    cuts = [slice(p * PAIR, (p + 1) * PAIR) for p in range(2)]
    logits = [nn(queries[:, at], map_weight(maps[at, :], False)) for at in cuts]
    for p, part in enumerate(logits):
        phi_o[:, 2 * p * F : 2 * (p + 1) * F] = features(part, ones).astype(bf16)


def attention_kernel(ids, lens, phi_query, phi_key, val, num_o):
    count = val.shape[0]
    split = split_of(ids, lens, pl.program_id(0), count)
    masks = block_masks(split, count, False)
    columns = [slice(h * F, (h + 1) * F) for h in range(4)]
    blocks = [slice(first, first + SUB) for first in range(0, count, SUB)]
    scores = [
        [
            masked(nt(phi_query[rows, at], phi_key[: rows.stop, at]), mask)
            for rows, mask in zip(blocks, masks)
        ]
        for at in columns
    ]
    for h, at in enumerate(columns):
        pair = val[:, h // 2 * PAIR : (h // 2 + 1) * PAIR].astype(f32)
        extended = with_aux(pair, h % 2, 1.0).astype(bf16)
        for rows, part in zip(blocks, scores[h]):
            num_o[rows, at] = nn(part, extended[: rows.stop])


def middle_kernel(
    states, ids, lens, num, phi_query, tok, wo, bias, gain, shift, *rest
):
    wires, (att_o, rden_o, mid_o, normed_o) = rest[: 2 * states], rest[2 * states :]
    count = num.shape[0]
    carry = sublane((count, F)) < split_of(ids, lens, pl.program_id(0), count)
    low = lane((count, PAIR)) < HD
    for p in range(wires[0].shape[1]):
        sums = []
        for h, memory in enumerate(take_wire(arrived(wires, p))):
            column = slice((2 * p + h) * F, (2 * p + h + 1) * F)
            sums.append(
                num[:, column] + jnp.where(carry, nt(phi_query[:, column], memory), 0.0)
            )
        numerator = jnp.where(low, sums[0], sums[1])
        denominator = pltpu.roll(jnp.where(low, sums[1], sums[0]), HD, 1)
        inverse = 1.0 / denominator
        at = slice(p * PAIR, (p + 1) * PAIR)
        rden_o[:, at] = inverse.astype(bf16)
        att_o[:, at] = (numerator * inverse).astype(bf16)
    middle = tok[...].astype(f32) + nn(att_o[...], matrix(wo)) + bias[...]
    mid_o[...] = middle
    xhat, _ = normalize(middle)
    normed_o[...] = (xhat * gain[...] + shift[...]).astype(bf16)


def put_halves(refs, value, core, at):
    if len(refs) == 1:
        refs[0][:, at] = value
        return
    mine_o, other_o = refs
    chips, rows, _ = mine_o.shape
    parted = value.reshape(chips, 2, rows, value.shape[1])
    even, odd = parted[:, 0], parted[:, 1]
    first = core == 0
    mine_o[:, :, at] = jnp.where(first, even, odd).astype(bf16)
    other_o[:, :, at] = jnp.where(first, odd, even).astype(bf16)


def mlp_kernel(plain, ids, lens, normed, cot, ex, sh, bias, branch, mid, *rest):
    out_o, back_o, bg_o, *grads, turned, y_s, back_s, mid_s, sem = rest
    step = pl.program_id(0)
    copy = pltpu.make_async_copy(mid, mid_s, sem)

    @pl.when(step == 0)
    def _():
        copy.start()
        turned[...] = normed[...].T
        y_s[...] = jnp.zeros_like(y_s)
        back_s[...] = jnp.zeros_like(back_s)

    expand, shrink = matrix(ex), matrix(sh)
    pre = nn(normed[...], expand) + bias[...]
    square = pre * pre
    slope, cubic = 0.7978845608028654, 0.044715
    half = 0.5 * jnp.tanh(pre * (slope + slope * cubic * square)) + 0.5
    raised = pre * half
    hidden = raised.astype(bf16)
    rise = half + raised * (1.0 - half) * (2.0 * slope + 6.0 * slope * cubic * square)
    back = (nt(cot[...], shrink) * rise).astype(bf16)
    bg_o[...] = jnp.sum(back.astype(f32), axis=0, keepdims=True)
    y_s[...] += nn(hidden, shrink)
    back_s[...] += nt(back, expand)

    @pl.when(step == pl.num_programs(0) - 1)
    def _():
        copy.wait()
        out_o[...] = (mid_s[...] + y_s[...] + branch[...]).astype(bf16)
        back_o[...] = back_s[...].astype(bf16)

    shrink_grad = tn(hidden, cot[...])
    expand_grad = nn(turned[...], back)
    if plain:
        eg_o, sg_o = grads
        sg_o[...] = shrink_grad
        eg_o[...] = expand_grad
        return
    em_o, eo_o, sm_o, so_o = grads
    core = ids[1] % 2
    first = core == 0
    put_halves((em_o, eo_o), expand_grad, core, slice(None))
    chips, rows, lanes = sm_o.shape
    width = shrink_grad.shape[1]
    subs = lanes // width
    parted = shrink_grad.reshape(chips, 2, subs, rows, width)
    for sub in range(subs):
        even, odd = parted[:, 0, sub], parted[:, 1, sub]
        at = slice(sub * width, (sub + 1) * width)
        sm_o[:, :, at] = jnp.where(first, even, odd).astype(bf16)
        so_o[:, :, at] = jnp.where(first, odd, even).astype(bf16)


def column_sum(values):
    return jnp.sum(values, axis=0, keepdims=True)


def middle_back_kernel(
    parts,
    ids,
    lens,
    mid,
    back,
    cot,
    att,
    rden,
    phi_query,
    wo,
    gain,
    mb_o,
    ext_o,
    wire_o,
    small_o,
    *rest,
):
    *og_refs, og_s, sums_s = rest
    step = pl.program_id(0)
    row, part = step // parts, lax.rem(step, parts)

    @pl.when(step == 0)
    def _():
        og_s[...] = jnp.zeros_like(og_s)
        small_o[...] = jnp.zeros_like(small_o)

    middle = mid[...]
    upstream = cot[...].astype(f32)
    xhat, scale = normalize(middle)
    from_norm = back[...].astype(f32)
    middle_back = upstream + normalize_back(from_norm, xhat, scale, gain[...])
    branch_back = middle_back.astype(bf16)
    mb_o[...] = branch_back
    small_o[0:1, :] += column_sum(from_norm * xhat)
    small_o[1:2, :] += column_sum(from_norm)
    small_o[2:3, :] += column_sum(branch_back.astype(f32))
    small_o[3:4, :] += column_sum(upstream)
    og_s[...] += tn(att[...], branch_back)

    @pl.when(step == pl.num_programs(0) - 1)
    def _():
        put_halves(og_refs, og_s[...], ids[1] % 2, slice(None))

    attended_back = nt(branch_back, matrix(wo))
    count = middle.shape[0]
    carry = sublane((count, F)) < split_of(ids, lens, row, count * parts) - part * count
    ones = segment_ones(PAIR)
    spot = lane((count, PAIR))
    for p in range(wire_o.shape[1]):
        at = slice(p * PAIR, (p + 1) * PAIR)
        given = attended_back[:, at]
        inverse = rden[:, at].astype(f32)
        numerator_back = given * inverse
        denominator_back = -segment_sum(given * att[:, at].astype(f32), ones) * inverse
        aux = pltpu.roll(denominator_back, HD, 1)
        high = aux.astype(bf16).astype(f32)
        rest = aux - high
        for h in range(2):
            first = HD if h == 0 else 0
            extended = with_aux(
                numerator_back,
                h,
                jnp.where(spot == first, high, jnp.where(spot == first + 1, rest, 0.0)),
            ).astype(bf16)
            column = slice((2 * p + h) * F, (2 * p + h + 1) * F)
            ext_o[:, column] = extended
            query = jnp.where(carry, phi_query[:, column].astype(f32), 0.0).astype(bf16)
            total = tn(extended, query)
            sums_s[2 * p + h] = jnp.where(part == 0, total, sums_s[2 * p + h] + total)

    @pl.when(part == parts - 1)
    def _():
        for p in range(wire_o.shape[1]):
            put_wire(wire_o, p, sums_s[2 * p], sums_s[2 * p + 1], ((HD, HD + 1), (0, 1)))


def map_gradient(pair, logits_back):
    both = tn(pair, logits_back)
    rows = pair_rows(both[:, :F], both[:, F:])
    return rows - pltpu.roll(rows, HD, 1)


def add_by_row(out, row, value):
    @pl.when(row == 0)
    def _():
        out[...] = value

    @pl.when(row > 0)
    def _():
        out[...] += value


def local_back_kernel(
    first, states, ids, lens, phi_query, phi_key, val, ext, queries, maps, *rest
):
    wires, (pq_o, kg_o, vg_o, mg_o) = rest[: 2 * states], rest[2 * states :]
    row = pl.program_id(1) + first
    count = val.shape[0]
    split = split_of(ids, lens, row, count)
    flipped = block_masks(split, count, True)
    carry = sublane((count, F)) < split
    ones = segment_ones(2 * F)
    columns = [slice(h * F, (h + 1) * F) for h in range(4)]
    cuts = [slice(p * PAIR, (p + 1) * PAIR) for p in range(2)]
    pairs = [val[:, at].astype(f32) for at in cuts]
    extended = [with_aux(pairs[h // 2], h % 2, 1.0).astype(bf16) for h in range(4)]
    memories = [memory for p in range(2) for memory in take_wire(arrived(wires, p))]
    grads = [
        jnp.where(carry, nn(ext[:, columns[h]], memories[h]), 0.0) for h in range(4)
    ]
    blocks = [slice(first, first + SUB) for first in range(0, count, SUB)]
    heads, tops = [], []
    for h, at in enumerate(columns):
        back, scores = [], []
        for rows, mask in zip(blocks, flipped):
            on = slice(rows.start, count)
            back.append(masked(nt(extended[h][rows], ext[on, at]), mask))
            scores.append(masked(nt(phi_key[rows, at], phi_query[on, at]), mask))
        heads.append((back, scores))
    for h, at in enumerate(columns):
        back, scores = heads[h]
        value_parts = []
        for rows, given, score in zip(blocks, back, scores):
            on = slice(rows.start, count)
            kg_o[rows, at] = nn(given, phi_query[on, at]).astype(bf16)
            value_parts.append(nn(score, ext[on, at]))
        tops.append(jnp.concatenate(value_parts, axis=0))
        query_parts = []
        for i, rows in enumerate(blocks):
            part = [
                tn(given[:, rows.start - on.start : rows.stop - on.start], phi_key[on, at])
                for given, on in zip(back[: i + 1], blocks)
            ]
            query_parts.append(sum(part[1:], part[0]))
        grads[h] = grads[h] + jnp.concatenate(query_parts, axis=0)
    low = lane((count, PAIR)) < HD
    for p, at in enumerate(cuts):
        vg_o[:, at] = jnp.where(low, tops[2 * p], tops[2 * p + 1]).astype(bf16)
    logits_back = [
        features_back(
            phi_query[:, 2 * p * F : 2 * (p + 1) * F],
            jnp.concatenate(grads[2 * p : 2 * p + 2], axis=1),
            ones,
        ).astype(bf16)
        for p in range(2)
    ]
    for p, at in enumerate(cuts):
        pq_o[:, at] = nt(logits_back[p], map_weight(maps[at, :], False)).astype(bf16)
    gradient = [map_gradient(queries[:, at], logits_back[p]) for p, at in enumerate(cuts)]
    gradient = jnp.concatenate(gradient, axis=0)
    mg_o[...] = jnp.where(lane(gradient.shape) < HD, gradient, 0.0)


def keys_back_kernel(
    first, states, ids, lens, kg, vg, phi_key, val, keys, maps, *rest
):
    wires = rest[: 2 * states]
    *from_before, pk_o, pv_o, mg_o = rest[2 * states :]
    row = pl.program_id(1) + first
    count = val.shape[0]
    split = split_of(ids, lens, row, count)
    begin = jnp.where(split < count, split, 0)
    last = sublane((count, F)) >= begin
    low = lane((count, PAIR)) < HD
    ones = segment_ones(2 * F)
    cuts = [slice(p * PAIR, (p + 1) * PAIR) for p in range(2)]
    logits_back = []
    for p, at in enumerate(cuts):
        pair = val[:, at].astype(f32)
        both = arrived(wires, p)
        state = both[0:F]
        spot = sublane(state.shape)
        grads, tops = [], []
        for h, memory in enumerate(take_wire(both)):
            column = slice((2 * p + h) * F, (2 * p + h + 1) * F)
            first = HD if h == 0 else 0
            own = (spot < HD) if h == 0 else (spot >= HD)
            memory = jnp.where(own | (spot == first), memory.astype(f32), 0.0).astype(bf16)
            extended = with_aux(pair, h, 1.0).astype(bf16)
            grads.append(kg[:, column].astype(f32) + jnp.where(last, nn(extended, memory), 0.0))
            tops.append(nt(phi_key[:, column], state))
        pv_o[:, at] = (
            vg[:, at].astype(f32) + jnp.where(last, jnp.where(low, tops[0], tops[1]), 0.0)
        ).astype(bf16)
        at = slice(2 * p * F, 2 * (p + 1) * F)
        logits_back.append(
            features_back(phi_key[:, at], jnp.concatenate(grads, axis=1), ones).astype(bf16)
        )
    for p, at in enumerate(cuts):
        pk_o[:, at] = nt(logits_back[p], map_weight(maps[at, :], True)).astype(bf16)
    gradient = jnp.concatenate(
        [
            pltpu.roll(map_gradient(keys[:, at], logits_back[p]), HD, 1)
            for p, at in enumerate(cuts)
        ],
        axis=0,
    )
    before = sum(part[...] for part in from_before)
    mg_o[...] = before + jnp.where(lane(gradient.shape) < HD, 0.0, gradient)


def weight_back_kernel(ids, lens, turned, pb, *refs):
    put_halves(refs, nn(turned[...], pb[...]), ids[1] % 2, slice(None))


def key_weight_back_kernel(
    steps, devices, ids, lens, turned, pk, small_in, small_mid, hid, maps, *rest
):
    *refs, lines = rest
    step = pl.program_id(0)
    core = ids[1] % 2

    @pl.when(step < steps)
    def _():
        put_halves(refs, nn(turned[...], pk[...]), core, slice(None))

    if devices:

        @pl.when(step == steps)
        def _():
            pack(devices, core, small_in, small_mid, hid, maps, *refs, lines)


def input_back_kernel(pq, pk, pv, wq, wk, wv, tok, mb, gain, out_o, small_o):
    @pl.when(pl.program_id(0) == 0)
    def _():
        small_o[...] = jnp.zeros_like(small_o)

    from_norm = nt(pq[...], wq[...]) + nt(pk[...], wk[...]) + nt(pv[...], wv[...])
    xhat, scale = normalize(tok[...].astype(f32))
    small_o[0:1, :] += column_sum(from_norm * xhat)
    small_o[1:2, :] += column_sum(from_norm)
    for i, part in enumerate((pq, pk, pv)):
        small_o[2 + i : 3 + i, :] += column_sum(part[...].astype(f32))
    out_o[...] = (mb[...].astype(f32) + normalize_back(from_norm, xhat, scale, gain[...])).astype(bf16)


def spec(shape, index):
    return pl.BlockSpec(memory_space=pl.ANY) if shape is None else pl.BlockSpec(shape, index)


def estimate(micros):
    return pl.CostEstimate(
        flops=int(micros * PACE * 1e9), bytes_accessed=int(micros * PACE * 1e6), transcendentals=0
    )


MARKS = {}


def mark_of(array):
    return MARKS[id(array)][1] if id(array) in MARKS else array


def call(kernel, grid, ins, outs, scratch=(), scalars=0, name=None, micros=10, waits=(), into=()):
    waits = [mark_of(array) for array in waits]
    arrays = [entry[0] for entry in ins[scalars:]]
    if name not in FREE_INS:
        arrays = [pltpu.with_memory_space_constraint(array, pltpu.HBM) for array in arrays]
    arrays += [pltpu.with_memory_space_constraint(array, pltpu.HBM) for array in waits]
    arrays += into
    fetched = [entry[0] for entry in ins[:scalars]]
    read, given = len(ins), len(ins) + len(waits) + len(into)

    def body(*refs):
        refs[given + len(outs)][...] = jnp.zeros((8, F), f32)
        kernel(*refs[:read], *refs[given : given + len(outs)], *refs[given + len(outs) + 1 :])

    def shaped(shape, kind, block, index, free=False):
        return (jax.ShapeDtypeStruct if free else pltpu.HBM)(shape, kind)

    *results, mark = pl.pallas_call(
        body,
        out_shape=[shaped(*out) for out in outs] + [pltpu.HBM((8, F), f32)],
        grid_spec=pltpu.PrefetchScalarGridSpec(
            num_scalar_prefetch=scalars,
            grid=grid,
            in_specs=[spec(block, index) for _, block, index in ins[scalars:]]
            + [pl.BlockSpec(memory_space=pl.ANY)] * (given - read),
            out_specs=[spec(*out[2:4]) for out in outs]
            + [spec((8, F), lambda *i: (0, 0))],
            scratch_shapes=list(scratch),
        ),
        compiler_params=pltpu.CompilerParams(
            vmem_limit_bytes=LIMITS.get(name, LIMIT) * 1024 * 1024
        ),
        cost_estimate=estimate(micros),
        input_output_aliases={given - len(into) + i: i for i in range(len(into))},
        name=name,
    )(*fetched, *arrays)
    MARKS.update((id(result), (result, mark)) for result in results)
    return results


def tie_kernel(*refs):
    del refs


def tie(values, *waits):
    anywhere = pl.BlockSpec(memory_space=pl.ANY)
    count = len(values)
    waits = [mark_of(array) for array in waits]
    return pl.pallas_call(
        tie_kernel,
        out_shape=[jax.ShapeDtypeStruct(v.shape, v.dtype) for v in values],
        in_specs=[anywhere] * (count + len(waits)),
        out_specs=[anywhere] * count,
        input_output_aliases={i: i for i in range(count)},
        cost_estimate=estimate(0.5),
        name="tie",
    )(*values, *waits)


def gather_rows(part):
    return lax.all_gather(part, AXES, axis=0, tiled=True)


def scatter_rows(whole):
    return lax.psum_scatter(whole, AXES, scatter_dimension=0, tiled=True)


def scatter_columns(rows):
    return lax.psum_scatter(rows, AXES, scatter_dimension=1, tiled=True)


def swap(array, mask, axis="seq", name="swap"):
    size = lax.axis_size(axis)
    with jax.named_scope(name):
        return lax.ppermute(array, axis, [(i, i ^ mask) for i in range(size)])


def gather_cores(pieces, name):
    return pieces + [swap(piece, 1, name=name) for piece in pieces]


def put_piece(cuts, outs, at, piece):
    for out, first, last, sub in cuts:
        if sub is None:
            outs[out][at] = piece[:, first:last]
        else:
            outs[out][at, sub] = piece[:, first:last]


def place_kernel(cuts, ids, *refs):
    pieces, outs = refs[:8], refs[8:]

    def put(at, chips):
        for core in range(2):
            for piece, pair in zip(pieces[4 * core + at : 4 * core + at + 2], chips):
                for r, chip in enumerate(pair):
                    put_piece(cuts, outs, ids[1] ^ (2 * chip + core), piece[r, 0])

    @pl.when(pl.program_id(0) < 2)
    def _():
        put(0, ((0, 1), (2, 3)))

    @pl.when(pl.program_id(0) >= 2)
    def _():
        put(2, ((0, 2), (1, 3)))


def place(pieces, ids, cuts, shapes, name, micros, waits=()):
    rows, wide = pieces[0].shape[-2:]
    near = lambda s: jnp.minimum(s, 1)
    far = lambda s: jnp.maximum(s - 2, 0)
    ins = [
        (p.reshape(2, 2, rows, wide), (2, 1, rows, wide), lambda s, ids, at=at: (0, at(s), 0, 0))
        for p, at in zip(pieces, (near, near, far, far) * 2)
    ]

    def target(shape):
        return lambda s, ids: (ids[0] ^ s,) + (0,) * len(shape)

    return call(
        functools.partial(place_kernel, cuts),
        (4,),
        [(ids, None, None)] + ins,
        [((32, *shape), bf16, (8, *shape), target(shape), True) for shape in shapes],
        [],
        1,
        name,
        micros,
        waits,
    )


def first_sum_kernel(parts, ids, *refs):
    ins, (near_keep, near_send, far_keep, far_send) = refs[: parts * 8], refs[parts * 8 :]
    step = pl.program_id(0)

    def put(targets):
        at = 0
        for part in range(parts):
            wide = ins[part * 8].shape[-1]
            for r, (out, i) in enumerate(targets):
                mine, got = ins[(part * 4 + r) * 2 : (part * 4 + r) * 2 + 2]
                total = mine[0, 0].astype(f32) + got[0, 0].astype(f32)
                out[i, 0, :, at : at + wide] = total.astype(bf16)
            at += wide

    @pl.when(step < 2)
    def _():
        put(((near_keep, 0), (near_send, 0), (near_keep, 1), (near_send, 1)))

    @pl.when(step >= 2)
    def _():
        put(((far_keep, 0), (far_keep, 1), (far_send, 0), (far_send, 1)))


def first_sum(mines, gots, ids, name, micros=4, waits=()):
    rows = mines[0].shape[-2]
    wides = [m.shape[-1] for m in mines]
    ins = [(ids, None, None)]

    def index(r):
        return lambda k, ids: (ids[0] ^ k, (ids[1] // 2) ^ r, 0, 0)

    for mine, got, wide in zip(mines, gots, wides):
        for r in range(4):
            for array in (mine, got):
                ins.append((array.reshape(4, 4, rows, wide), (1, 1, rows, wide), index(r)))
    total, last = sum(wides), name[0] == "k"
    near = lambda k, ids: (0, jnp.minimum(k, 1), 0, 0)
    far = lambda k, ids: (0, jnp.maximum(k - 2, 0), 0, 0)
    return call(
        functools.partial(first_sum_kernel, len(mines)),
        (4,),
        ins,
        [
            ((2, 2, rows, total), bf16, (2, 1, rows, total), at, free)
            for at, free in ((near, last), (near, name[0] != "m"), (far, last), (far, True))
        ],
        [],
        1,
        name,
        micros,
        waits,
    )


def middle_sum_kernel(near_keep, near_got, far_keep, far_got, *outs):
    for at, (kept, got) in enumerate(((near_keep, near_got), (far_keep, far_got))):
        for i in range(2):
            total = kept[i].astype(f32) + got[i].astype(f32)
            outs[2 * at + i][...] = total.astype(bf16)


def middle_sum(sums, name, micros=3, waits=()):
    near_keep, near_send, far_keep, far_send = sums
    pieces = [near_keep, swap(near_send, 2, name=name + "_x1")]
    pieces += [far_keep, swap(far_send, 4, name=name + "_y1")]
    _, _, rows, wide = near_keep.shape
    tile = 1536 if wide % 1536 == 0 else wide
    near_keep, near_send, far_keep, far_send = call(
        middle_sum_kernel,
        (wide // tile,),
        [(p, (2, 2, rows, tile), lambda g: (0, 0, 0, g)) for p in pieces],
        [
            ((2, rows, wide), bf16, (2, rows, tile), lambda g: (0, 0, g), free)
            for free in (name[0] == "k", True) * 2
        ],
        [],
        0,
        name,
        micros,
        waits,
    )
    near_got, far_got = swap(near_send, 4, name=name + "_y2"), swap(far_send, 2, name=name + "_x2")
    return [near_keep, near_got, far_keep, far_got]


def second_sum_kernel(direct, near, near_got, far, far_got, *outs):
    for k in range(4):
        kept, got = (near, near_got) if k < 2 else (far, far_got)
        total = kept[k % 2].astype(f32) + got[k % 2].astype(f32)
        if direct:
            outs[k][...] = total.astype(outs[k].dtype)
        else:
            outs[k % 2][k // 2] = total.astype(outs[k % 2].dtype)


def second_sum(pieces, name, micros=3, waits=(), direct=True):
    _, rows, wide = pieces[0].shape
    tile = 1536 if wide % 1536 == 0 else wide
    if direct:
        shape, cut = (rows, wide), (rows, tile)
        outs = [(shape, bf16 if k else f32, cut, lambda g: (0, g), k > 0) for k in range(4)]
    else:
        shape, cut = (2, rows, wide), (2, rows, tile)
        outs = [(shape, bf16 if k else f32, cut, lambda g: (0, 0, g), k > 0) for k in range(2)]
    return call(
        functools.partial(second_sum_kernel, direct),
        (wide // tile,),
        [(p, (2, rows, tile), lambda g: (0, 0, g)) for p in pieces],
        outs,
        [],
        0,
        name,
        micros,
        waits,
    )


def reduce_batch(sums, name):
    got = [swap(sums[k], k, "batch", name + "_layer") for k in range(1, 4)]
    return sums[0] + sum(part.astype(f32) for part in got)


def reduce_layer1(sums, name, waits):
    (kept,) = tie(sums[:1], *waits)
    return kept + swap(sums[1], 1, "batch", name + "_layer1").astype(f32)


def reduce_layer2(pair, name, waits):
    got = swap(pair[1].astype(bf16), 2, "batch", name + "_layer2")
    (kept,) = tie([pair[0]], *waits)
    return kept + got.astype(f32)


def spots(length, each, owners):
    at = lane((F, length))
    owner = ((at.astype(f32) + 0.5) * (1.0 / each)).astype(jnp.int32)
    inside = (at - owner * each == sublane((F, length))).astype(bf16)
    at = lane((owners.shape[0], length))
    owner = ((at.astype(f32) + 0.5) * (1.0 / each)).astype(jnp.int32)
    return inside, owner == owners


def unpack_kernel(devices, block, *outs):
    rows = block.shape[0] // devices
    vectors = [(out, i) for out in outs for i in range(out.shape[0])]
    count = len(vectors)
    place_at = lane((count * devices, block.shape[0]))
    line = sublane((count * devices, block.shape[0]))
    vector = ((line.astype(f32) + 0.5) * (1.0 / devices)).astype(jnp.int32)
    picked = nn(
        (place_at == (line - vector * devices) * rows + vector).astype(bf16), block[...]
    ).astype(bf16)
    for j, (out, i) in enumerate(vectors):
        length = out.shape[1]
        owners = sublane((devices, length))
        inside, owned = spots(length, length // devices, owners)
        spread = nn(picked[j * devices : (j + 1) * devices], inside)
        out[i : i + 1, :] = column_sum(jnp.where(owned, spread, 0.0))


def shards_kernel(
    gain, shift, mix, offset, maps, out, branch, ex, hid, sh, first_o, rest_o, small
):
    rows = mix.shape[0]
    small[...] = jnp.zeros_like(small)
    for j, part in enumerate((gain, shift, branch)):
        small[2 * j : 2 * j + 2, 0:rows] = part[...].astype(f32)
    small[6:7, 0 : 3 * rows] = offset[...].astype(f32)
    small[7:8, 0 : 4 * rows] = hid[...].astype(f32)
    wide, width = mix.shape[1], sh.shape[1]
    first_o[:, 0:wide] = mix[...]
    first_o[:, wide : wide + F] = maps[...]
    first_o[:, wide + F : wide + 2 * F] = small[...].astype(bf16)
    for i in range(4):
        rest_o[i] = ex[:, i * width : (i + 1) * width]
        rest_o[4 + i] = sh[i * rows : (i + 1) * rows, :].astype(f32).astype(bf16)
    rest_o[8] = out[...]


def pack(devices, core, small_in, small_mid, hid, maps, mine_o, other_o, lines):
    offset = jnp.concatenate([small_in[i : i + 1, :] for i in range(2, 5)], axis=1)
    lines[...] = jnp.zeros_like(lines)
    vectors = [
        small_in[0:1, :],
        small_mid[0:1, :],
        small_in[1:2, :],
        small_mid[1:2, :],
        small_mid[2:3, :],
        small_mid[3:4, :],
        offset,
        hid[...],
    ]
    half = devices // 2
    for j, vector in enumerate(vectors):
        length = vector.shape[1]
        line = sublane((devices, length))
        owners = jnp.where(line < half, 2 * line + core, 2 * (line - half) + 1 - core)
        inside, owned = spots(length, length // devices, owners)
        share = jnp.where(owned, vector, 0.0).astype(bf16)
        lines[:, j, :] = nt(share, inside)
    put_halves((mine_o, other_o), maps[...], core, slice(0, F))
    mine_o[:, :, F:] = lines[:half].astype(bf16)
    other_o[:, :, F:] = lines[half:].astype(bf16)


def flags_kernel(levels, count, ids, lens, *outs):
    mine = ids[1]
    for row in range(lens.shape[0]):
        flags = []
        for reverse in (False, True):
            for level in range(levels):
                span = 1 << level
                begin = mine - lax.rem(mine, span)
                upper = lax.rem(mine // span, 2) == 1
                own_closed = starts_within(lens, row, begin * count, (begin + span) * count)
                if reverse:
                    receives = jnp.logical_not(upper)
                    closed = starts_within(lens, row, (mine + 1) * count, (begin + span) * count)
                    other = starts_within(lens, row, (begin - span) * count, begin * count)
                else:
                    receives = upper
                    closed = starts_within(lens, row, begin * count, mine * count)
                    other = starts_within(
                        lens, row, (begin + span) * count, (begin + 2 * span) * count
                    )
                flags.append(receives & jnp.logical_not(closed))
                flags.append(receives | jnp.logical_not(other))
                flags.append(jnp.logical_not(receives & own_closed))
        for out, flag in zip(outs, flags):
            out[row] = jnp.full((1, 1, F), jnp.where(flag, 1.0, 0.0), f32)


def carry(total, came, flags, level, reverse, waits=()):
    levels = len(flags) // 6
    at = 3 * (level + (levels if reverse else 0))
    reaches, keeps, joins = flags[at : at + 3]
    other = swap(total, 1 << level, name=f"state{level}")
    came = came + [(other, reaches)]
    if level == levels - 1:
        return None, came
    if len(waits):
        keeps, joins = tie([keeps, joins], *waits)
    return (keeps * total.astype(f32) + joins * other.astype(f32)).astype(bf16), came


def local(
    tokens,
    sequence_lengths,
    norm_gains,
    norm_shifts,
    mixing_weight,
    mixing_offset,
    feature_maps,
    output_weight,
    branch_offsets,
    expand_weight,
    hidden_offset,
    shrink_weight,
    cotangent,
):
    MARKS.clear()
    row_count, tok_count, width = tokens.shape
    count = row_count * tok_count
    heads = width // HD
    pairs, quads = heads // 2, heads // 4
    quad = 2 * PAIR
    hidden_width = expand_weight.shape[1]
    batch, size = lax.axis_size("batch"), lax.axis_size("seq")
    devices = batch * size
    share = width // devices
    plain = size != 8 or batch != 4 or share % 8 != 0 or hidden_width != 4 * width or 4 * share > F

    mine = lax.axis_index("seq").astype(jnp.int32)
    ids = jnp.stack([lax.axis_index("batch").astype(jnp.int32), mine])
    lens = sequence_lengths
    scalars = [(ids, None, None), (lens, None, None)]
    levels = size.bit_length() - 1
    flag = (row_count, 1, 1, F)
    flags = call(
        functools.partial(flags_kernel, levels, tok_count),
        (1,),
        scalars,
        [(flag, f32, flag, lambda i, *s: (0, 0, 0, 0))] * (6 * levels),
        [],
        2,
        "flags",
        1,
    )

    if plain:
        gains = lax.all_gather(norm_gains, AXES, axis=1, tiled=True).astype(f32)[:, None]
        shifts = lax.all_gather(norm_shifts, AXES, axis=1, tiled=True).astype(f32)[:, None]
        branches = lax.all_gather(branch_offsets, AXES, axis=1, tiled=True).astype(f32)[:, None]
        offset = gather_rows(mixing_offset).astype(f32)[None]
        hidden_bias = gather_rows(hidden_offset).astype(f32)[None]
        first_weight = jnp.concatenate(
            [gather_rows(mixing_weight), gather_rows(feature_maps)], axis=1
        )
        out_weight = gather_rows(output_weight)
        expand = gather_rows(expand_weight)
        shrink = gather_rows(shrink_weight)
    else:
        wide = 3 * width + 2 * F
        shards = (
            norm_gains,
            norm_shifts,
            mixing_weight,
            mixing_offset[None],
            feature_maps,
            output_weight,
            branch_offsets,
            expand_weight,
            hidden_offset[None],
            shrink_weight,
        )
        at = lambda i: (0, 0)
        first, rest = call(
            shards_kernel,
            (1,),
            [(array, array.shape, at) for array in shards],
            [
                ((share, wide), bf16, (share, wide), at, True),
                ((9, share, width), bf16, (9, share, width), lambda i: (0, 0, 0)),
            ],
            [pltpu.VMEM((share, F), f32)],
            0,
            "shards",
            2,
        )
        layers = [first] + [swap(first, k, "batch", "first_layer") for k in range(1, 4)]
        near, far = jnp.stack(layers[:2]), jnp.stack(layers[2:])
        rest = lax.all_gather(rest, AXES)
        near = jnp.concatenate([near, swap(near, 2, name="first_x1")])
        far = jnp.concatenate([far, swap(far, 4, name="first_y1")])
        first = [
            near,
            swap(near, 4, name="first_y2"),
            far,
            swap(far, 2, name="first_x2"),
        ]
        first = gather_cores(first, "first_core")
        (first_weight,) = place(
            first, ids, ((0, 0, wide, None),), ((share, wide),), "place_first", 5
        )
        first_weight = first_weight.reshape(width, -1)
        *rows_out, offset, hidden_bias = call(
            functools.partial(unpack_kernel, devices),
            (1,),
            [(first_weight, (width, F), lambda i: (0, 3 * width // F + 1))],
            [
                ((n, length), f32, (n, length), lambda i: (0, 0))
                for n, length in [(1, width)] * 6 + [(1, 3 * width), (1, hidden_width)]
            ],
            [],
            0,
            "unpack",
            2,
        )
        gains, shifts, branches = (rows_out[i : i + 2] for i in (0, 2, 4))

    tok = tokens.reshape(count, width)
    cot = cotangent.reshape(count, width)
    full = lambda r, q, *s: (0, 0)

    def columns(first):
        return lambda r, q, *s: (0, first + q)

    own = lambda r, q, *s: (r, 0)
    cell = lambda r, q, *s: (r, q)
    normed, turned, keys, values, phi_key, wire = call(
        keys_kernel,
        (row_count, quads),
        [
            *scalars,
            (tok, (tok_count, width), own),
            (gains[0], (1, width), full),
            (shifts[0], (1, width), full),
            (first_weight, (width, quad), columns(quads)),
            (first_weight, (width, quad), columns(2 * quads)),
            (offset, (1, quad), columns(quads)),
            (offset, (1, quad), columns(2 * quads)),
            (first_weight, (quad, F), lambda r, q, *s: (q, 3 * width // F)),
        ],
        [
            ((count, width), bf16, (tok_count, width), own),
            ((width, count), bf16, (width, tok_count), lambda r, q, *s: (0, r)),
            ((count, width), bf16, (tok_count, quad), cell),
            ((count, width), bf16, (tok_count, quad), cell),
            ((count, heads * F), bf16, (tok_count, 4 * F), cell),
            (
                (row_count, pairs, WIRE, F),
                bf16,
                (1, 2, WIRE, F),
                lambda r, q, *s: (r, q, 0, 0),
            ),
        ],
        [pltpu.VMEM((tok_count, width), bf16)],
        2,
        "keys",
        15,
        flags,
    )
    queries, phi_query = call(
        queries_kernel,
        (row_count, quads),
        [
            (normed, (tok_count, width), own),
            (first_weight, (width, quad), columns(0)),
            (offset, (1, quad), columns(0)),
            (first_weight, (quad, F), lambda r, q, *s: (q, 3 * width // F)),
        ],
        [
            ((count, width), bf16, (tok_count, quad), cell),
            ((count, heads * F), bf16, (tok_count, 4 * F), cell),
        ],
        [],
        0,
        "queries",
        8,
    )
    total, came = carry(wire, [], flags, 0, False)
    total, came = carry(total, came, flags, 1, False, (phi_query,))
    (numerator,) = call(
        attention_kernel,
        (row_count, quads),
        [
            *scalars,
            (phi_query, (tok_count, 4 * F), cell),
            (phi_key, (tok_count, 4 * F), cell),
            (values, (tok_count, quad), cell),
        ],
        [((count, heads * F), f32, (tok_count, 4 * F), cell)],
        [],
        2,
        "attention",
        12,
        (total,),
    )
    for level in range(2, levels):
        total, came = carry(total, came, flags, level, False, (numerator,))

    def states(came, pairs_of, index):
        wires = [
            (wire, (1, pairs_of, WIRE, F), lambda *i: (*index(*i), 0, 0)) for wire, _ in came
        ]
        reaches = [
            (reach, (1, 1, 1, F), lambda *i: (index(*i)[0], 0, 0, 0)) for _, reach in came
        ]
        return wires + reaches

    memories = came
    if plain:
        out_part = (out_weight, (width, width), lambda r, *s: (0, 0))
        expand_part = (expand, (width, width), lambda f, *s: (0, f))
        shrink_part = (shrink, (width, width), lambda f, *s: (f, 0))
    else:
        cut = (devices, 1, share, width)
        out_part = (rest, cut, lambda r, *s: (0, 8, 0, 0))
        expand_part = (rest, cut, lambda f, *s: (0, f, 0, 0))
        cut = (devices // 4, 4, share, width)
        shrink_part = (rest, cut, lambda f, *s: (f, 1, 0, 0))
    whole = lambda r, *s: (0, 0)
    one = lambda r, *s: (r, 0)
    attended, inverse, middle, normed_mid = call(
        functools.partial(middle_kernel, len(memories)),
        (row_count,),
        [
            *scalars,
            (numerator, (tok_count, heads * F), one),
            (phi_query, (tok_count, heads * F), one),
            (tok, (tok_count, width), one),
            out_part,
            (branches[0], (1, width), whole),
            (gains[1], (1, width), whole),
            (shifts[1], (1, width), whole),
            *states(memories, pairs, lambda r, *s: (r, 0)),
        ],
        [
            ((count, width), bf16, (tok_count, width), one),
            ((count, width), bf16, (tok_count, width), one),
            ((count, width), f32, (tok_count, width), one),
            ((count, width), bf16, (tok_count, width), one),
        ],
        [],
        2,
        "middle",
        9,
    )
    tile = width
    steps = hidden_width // tile

    def halves(wide, block, index):
        if plain:
            return [((width, wide), f32, (width, block), lambda *i: (0, index(*i)))]
        shape = (devices // 2, share, wide)
        cut = (devices // 2, share, block)
        return [(shape, bf16, cut, lambda *i: (0, 0, index(*i)), True)] * 2

    layer_output, normed_mid_back, hidden_grad, *mlp_grads = call(
        functools.partial(mlp_kernel, plain),
        (steps,),
        [
            *scalars,
            (normed_mid, (count, width), lambda f, *s: (0, 0)),
            (cot, (count, width), lambda f, *s: (0, 0)),
            expand_part,
            shrink_part,
            (hidden_bias, (1, tile), lambda f, *s: (0, f)),
            (branches[1], (1, width), whole),
            (middle, None, None),
        ],
        [
            ((count, width), bf16, (count, width), lambda f, *s: (0, 0)),
            ((count, width), bf16, (count, width), lambda f, *s: (0, 0)),
            ((1, hidden_width), f32, (1, tile), lambda f, *s: (0, f)),
            *halves(hidden_width, tile, lambda f, *s: f),
            *(
                [((hidden_width, width), f32, (tile, width), lambda f, *s: (f, 0))]
                if plain
                else [
                    (
                        (devices // 2, share, 4 * width),
                        bf16,
                        (devices // 2 // steps, share, 4 * width),
                        lambda f, *s: (f, 0, 0),
                        True,
                    )
                ]
                * 2
            ),
        ],
        [pltpu.VMEM((width, count), bf16)]
        + [pltpu.VMEM((count, width), f32)] * 3
        + [pltpu.SemaphoreType.DMA],
        2,
        "mlp",
        37,
    )
    parts = tok_count // SUB
    middle_back, extended, wire_back, small_mid, *output_grads = call(
        functools.partial(middle_back_kernel, parts),
        (count // SUB,),
        [
            *scalars,
            (middle, (SUB, width), one),
            (normed_mid_back, (SUB, width), one),
            (cot, (SUB, width), one),
            (attended, (SUB, width), one),
            (inverse, (SUB, width), one),
            (phi_query, (SUB, heads * F), one),
            out_part,
            (gains[1], (1, width), whole),
        ],
        [
            ((count, width), bf16, (SUB, width), one),
            ((count, heads * F), bf16, (SUB, heads * F), one),
            ((row_count, pairs, WIRE, F), bf16, (1, pairs, WIRE, F), lambda r, *s: (r // parts, 0, 0, 0)),
            ((8, width), f32, (8, width), whole),
            *halves(width, width, lambda r, *s: 0),
        ],
        [pltpu.VMEM((width, width), f32), pltpu.VMEM((heads, F, F), f32)],
        2,
        "middle_back",
        17,
    )
    total, came = carry(wire_back, [], flags, 0, True)
    if not plain:
        expand_mine, expand_other, shrink_mine, shrink_other = mlp_grads
        mlp_waits = first_sum(
            (expand_mine, shrink_mine),
            (swap(expand_other, 1, name="mlp_core"), swap(shrink_other, 1, name="mlp_core")),
            ids,
            "mlp_first_sum",
            7,
            (total,),
        )
    cell = lambda p, r, *s: (r, p)
    of_pair = lambda p, r, *s: (p, 0)
    from_wire = lambda p, r, *s: (r, p, 0, 0)

    def attend_back(first, into=(), waits=()):
        cell = lambda p, r, *s: (r + first, p)
        return call(
            functools.partial(local_back_kernel, first, len(memories)),
            (quads, 1),
            [
                *scalars,
                (phi_query, (tok_count, 4 * F), cell),
                (phi_key, (tok_count, 4 * F), cell),
                (values, (tok_count, quad), cell),
                (extended, (tok_count, 4 * F), cell),
                (queries, (tok_count, quad), cell),
                (first_weight, (quad, F), lambda p, r, *s: (p, 3 * width // F)),
                *states(memories, 2, lambda p, r, *s: (r + first, p)),
            ],
            [
                ((count, width), bf16, (tok_count, quad), cell),
                ((count, heads * F), bf16, (tok_count, 4 * F), cell),
                ((count, width), bf16, (tok_count, quad), cell),
                ((width, F), f32, (quad, F), of_pair),
            ],
            [],
            2,
            "local_back",
            25 / row_count,
            waits,
            into,
        )

    partial, maps_query = (), []
    for level in range(1, levels):
        if level <= row_count:
            waits = (total, *(mlp_waits[:1] if level == 1 and not plain else ()))
            *partial, map_query = attend_back(level - 1, partial, waits)
            maps_query.append(map_query)
        total, came = carry(total, came, flags, level, True, partial[:1])
        if level == 1 and not plain:
            mlp_waits = [mlp_waits[0], *tie(mlp_waits[1:2], total), *mlp_waits[2:]]
    for first in range(levels - 1, row_count):
        *partial, map_query = attend_back(first, partial)
        maps_query.append(map_query)
    queries_back, key_feat, value_feat = partial

    def weight_back(pb, waits=()):
        return call(
            weight_back_kernel,
            (quads,),
            [
                *scalars,
                (turned, (width, count), lambda q, *s: (0, 0)),
                (pb, (count, quad), lambda q, *s: (0, q)),
            ],
            halves(width, quad, lambda q, *s: q),
            [],
            2,
            "weight_back",
            5,
            waits,
        )

    query_grads = weight_back(queries_back)

    def attend_keys_back(first, map_grads, into=(), waits=()):
        cell = lambda p, r, *s: (r + first, p)
        return call(
            functools.partial(keys_back_kernel, first, len(came)),
            (quads, 1),
            [
                *scalars,
                (key_feat, (tok_count, 4 * F), cell),
                (value_feat, (tok_count, quad), cell),
                (phi_key, (tok_count, 4 * F), cell),
                (values, (tok_count, quad), cell),
                (keys, (tok_count, quad), cell),
                (first_weight, (quad, F), lambda p, r, *s: (p, 3 * width // F)),
                *states(came, 2, lambda p, r, *s: (r + first, p)),
                *[(map_grad, (quad, F), of_pair) for map_grad in map_grads],
            ],
            [
                ((count, width), bf16, (tok_count, quad), cell),
                ((count, width), bf16, (tok_count, quad), cell),
                ((width, F), f32, (quad, F), of_pair),
            ],
            [],
            2,
            "keys_back",
            13 / row_count,
            waits,
            into,
        )

    *partial, map_grad = attend_keys_back(0, maps_query, (), query_grads[:1])
    if not plain:
        mlp_sums = middle_sum(mlp_waits, "mlp_middle_sum", 4, partial[:1])
    for first in range(1, row_count):
        waits = () if plain else mlp_sums[:1]
        *partial, map_grad = attend_keys_back(first, [map_grad], partial, waits)
    keys_back, values_back = partial
    value_grads = weight_back(values_back)
    if not plain:
        mlp_sums = second_sum(mlp_sums, "mlp_second_sum", 4, value_grads[:1], False)
        query_waits = first_sum(
            (query_grads[0], output_grads[0], value_grads[0]),
            (
                swap(query_grads[1], 1, name="query_core"),
                swap(output_grads[1], 1, name="query_core"),
                swap(value_grads[1], 1, name="query_core"),
            ),
            ids,
            "query_first_sum",
            3,
            mlp_sums[:1],
        )
    row = lambda r: (r, 0)
    fixed = lambda r: (0, 0)
    input_gradient, small_in = call(
        input_back_kernel,
        (count // SUB,),
        [
            (queries_back, (SUB, width), row),
            (keys_back, (SUB, width), row),
            (values_back, (SUB, width), row),
            (first_weight, (width, width), lambda r: (0, 0)),
            (first_weight, (width, width), lambda r: (0, 1)),
            (first_weight, (width, width), lambda r: (0, 2)),
            (tok, (SUB, width), row),
            (middle_back, (SUB, width), row),
            (gains[0], (1, width), fixed),
        ],
        [
            ((count, width), bf16, (SUB, width), row),
            ((8, width), f32, (8, width), fixed),
        ],
        [],
        0,
        "input_back",
        10,
        () if plain else query_waits[:1],
    )
    if not plain:
        query_sums = middle_sum(query_waits, "query_middle_sum", 2, (input_gradient,))
    small_parts = [
        (array, array.shape, lambda q, *s: (0, 0))
        for array in (small_in, small_mid, hidden_grad, map_grad)
    ]
    key_grads = call(
        functools.partial(key_weight_back_kernel, quads, 0 if plain else devices),
        (quads + (0 if plain else 1),),
        [
            *scalars,
            (turned, (width, count), lambda q, *s: (0, 0)),
            (keys_back, (count, quad), lambda q, *s: (0, jnp.minimum(q, quads - 1))),
            *small_parts,
        ],
        halves(width + (0 if plain else quad), quad, lambda q, *s: q),
        [pltpu.VMEM((devices, share, F), f32)],
        2,
        "key_weight_back",
        10,
        () if plain else query_sums[:1],
    )
    if plain:
        mixing_grad = jnp.concatenate([query_grads[0], key_grads[0], value_grads[0]], axis=1)
        offset_grad = small_in[2:5].reshape(-1)
        grads = (
            scatter_columns(jnp.stack([small_in[0], small_mid[0]])),
            scatter_columns(jnp.stack([small_in[1], small_mid[1]])),
            scatter_rows(mixing_grad),
            scatter_rows(offset_grad),
            scatter_rows(map_grad),
            scatter_rows(output_grads[0]),
            scatter_columns(small_mid[2:4]),
            scatter_rows(mlp_grads[0]),
            scatter_rows(hidden_grad[0]),
            scatter_rows(mlp_grads[1]),
        )
    else:
        query_sums = second_sum(query_sums, "query_second_sum", 3, (key_grads[0],), False)
        mlp_pair = reduce_layer1(mlp_sums, "mlp", query_sums[:1])
        key_sums = first_sum(
            (key_grads[0],),
            (swap(key_grads[1], 1, name="key_core"),),
            ids,
            "key_first_sum",
            4,
            (mlp_pair,),
        )
        query_pair = reduce_layer1(query_sums, "query", key_sums[:1])
        key_sums = middle_sum(key_sums, "key_middle_sum", 2, (query_pair,))
        key_sums = second_sum(key_sums, "key_second_sum")
        mlp_total = reduce_layer2(mlp_pair, "mlp", key_sums[:1])
        query_total = reduce_layer2(query_pair, "query", key_sums[:1])
        key_total = reduce_batch(key_sums, "key")
        small_total = key_total[0:8, width + F :]
        mixing_grad = jnp.concatenate(
            [query_total[:, :width], key_total[:, :width], query_total[:, 2 * width :]], axis=1
        )
        shrink_grad = mlp_total[:, hidden_width:].reshape(share, 4, width)
        grads = (
            small_total[0:2, :share],
            small_total[2:4, :share],
            mixing_grad,
            small_total[6, : 3 * share],
            key_total[:, width : width + F],
            query_total[:, width : 2 * width],
            small_total[4:6, :share],
            mlp_total[:, :hidden_width],
            small_total[7, : 4 * share],
            shrink_grad.transpose(1, 0, 2).reshape(4 * share, width),
        )
    return (layer_output.reshape(tokens.shape), input_gradient.reshape(tokens.shape), *grads)


def solution(mesh):
    rows = P("batch", "seq", None)
    split_rows = P(AXES, None)
    split_columns = P(None, AXES)
    split_vector = P(AXES)
    return jax.shard_map(
        local,
        mesh=mesh,
        in_specs=(
            rows,
            P("batch", None),
            split_columns,
            split_columns,
            split_rows,
            split_vector,
            split_rows,
            split_rows,
            split_columns,
            split_rows,
            split_vector,
            split_rows,
            rows,
        ),
        out_specs=(
            rows,
            rows,
            split_columns,
            split_columns,
            split_rows,
            split_vector,
            split_rows,
            split_rows,
            split_columns,
            split_rows,
            split_vector,
            split_rows,
        ),
        check_vma=False,
    )
```

```python
import functools

import jax
import jax.numpy as jnp
from jax import lax
from jax.experimental import pallas as pl
from jax.experimental.pallas import tpu as pltpu
from jax.sharding import PartitionSpec as P

HD = 64
F = 2 * HD
PAIR = 2 * HD
SUB = 256
WIRE = F + 16
EPSILON = 1e-05
AXES = ("batch", "seq")
LIMIT = 28
LIMITS = {"mlp": 56, "attention": 32, "middle_back": 40, "local_back": 40, "middle": 40, "input_back": 32}
SUMS = {
    group + part
    for group in ("mlp", "query", "key")
    for part in ("_first_sum", "_middle_sum", "_second_sum")
}
FREE_INS = SUMS | {"place_first", "unpack", "keys", "queries", "input_back"}
PACE = 0.01
bf16 = jnp.bfloat16
f32 = jnp.float32


def dot(a, b, left, right):
    return lax.dot_general(a, b, (((left,), (right,)), ((), ())), preferred_element_type=f32)


def nn(a, b):
    return dot(a, b, 1, 0)


def nt(a, b):
    return dot(a, b, 1, 1)


def tn(a, b):
    return dot(a, b, 0, 0)


def lane(shape):
    return lax.broadcasted_iota(jnp.int32, shape, len(shape) - 1)


def sublane(shape):
    return lax.broadcasted_iota(jnp.int32, shape, len(shape) - 2)


def normalize(values):
    center = jnp.mean(values, axis=-1, keepdims=True)
    centered = values - center
    spread = jnp.mean(centered * centered, axis=-1, keepdims=True)
    scale = lax.rsqrt(spread + EPSILON)
    return centered * scale, scale


def normalize_back(upstream, xhat, scale, gain):
    entry = upstream * gain
    first = jnp.mean(entry, axis=-1, keepdims=True)
    second = jnp.mean(entry * xhat, axis=-1, keepdims=True)
    return scale * (entry - first - xhat * second)


def map_weight(rows, keys):
    rows = rows.astype(f32)
    turned = pltpu.roll(rows, HD, 1)
    low = lane(rows.shape) < HD
    signed = jnp.where(low, turned, -rows) if keys else jnp.where(low, rows, -turned)
    top = sublane(rows.shape) < HD
    return jnp.concatenate(
        [jnp.where(top, signed, 0.0), jnp.where(top, 0.0, signed)], axis=1
    ).astype(bf16)


def segment_ones(width):
    shape = (width, width)
    return (lane(shape) // HD == sublane(shape) // HD).astype(bf16)


def segment_sum(values, ones):
    high = values.astype(bf16)
    low = (values - high.astype(f32)).astype(bf16)
    return nn(high, ones) + nn(low, ones)


def features(logits, ones):
    parts = []
    for at in range(0, logits.shape[1], F):
        part = logits[:, at : at + F]
        low = lane(part.shape) < HD
        first = jnp.max(jnp.where(low, part, -jnp.inf), axis=1, keepdims=True)
        second = jnp.max(jnp.where(low, -jnp.inf, part), axis=1, keepdims=True)
        parts.append(jnp.exp(part - jnp.where(low, first, second)))
    powers = jnp.concatenate(parts, axis=1)
    return powers / nn(powers.astype(bf16), ones)


def features_back(phi, upstream, ones):
    phi = phi.astype(f32)
    return phi * (upstream - segment_sum(phi * upstream, ones))


def split_of(ids, lens, row, count):
    first = ids[1] * count
    start, split = 0, count
    for n in range(lens.shape[1]):
        inside = (start >= first) & (start < first + count)
        split = jnp.where(inside, start - first, split)
        start = start + lens[row, n]
    return split


def starts_within(lens, row, low, high):
    start, found = 0, 0
    for n in range(lens.shape[1]):
        found = found | jnp.where((start >= low) & (start < high), 1, 0)
        start = start + lens[row, n]
    return found == 1


def matrix(ref):
    value = ref[...]
    return value if value.ndim == 2 else value.reshape(-1, value.shape[-1])


def with_aux(pair, head, aux):
    own = (lane(pair.shape) < HD) if head == 0 else (lane(pair.shape) >= HD)
    return jnp.where(own, pair, aux)


def pair_rows(first, second):
    top = sublane(first.shape) < HD
    return jnp.where(top, first, second)


def put_wire(ref, at, first, second, aux_rows):
    ref[0, at, 0:F, :] = pair_rows(first, second).astype(bf16)
    sums = [sum(x[a : a + 1] for a in rows) for x, rows in zip((first, second), aux_rows)]
    row = sublane((16, F))
    ref[0, at, F:WIRE, :] = jnp.where(
        row == 0, sums[0], jnp.where(row == 1, sums[1], 0.0)
    ).astype(bf16)


def arrived(refs, at):
    half = len(refs) // 2
    return sum(
        reach[0, 0] * wire[0, at].astype(f32) for wire, reach in zip(refs[:half], refs[half:])
    ).astype(bf16)


def take_wire(both):
    state, sums = both[0:F], both[F:WIRE]
    top = sublane(state.shape) < HD
    return jnp.where(top, state, sums[0:1]), jnp.where(top, sums[1:2], state)


def block_masks(split, count, flipped):
    masks = []
    for first in range(0, count, SUB):
        if flipped:
            shape = (SUB, count - first)
            i, j = lane(shape) + first, sublane(shape) + first
        else:
            shape = (SUB, first + SUB)
            i, j = sublane(shape) + first, lane(shape)
        masks.append(((i < split) | (j >= split)) & (j <= i))
    return masks


def masked(scores, mask):
    return jnp.where(mask, scores, 0.0).astype(bf16)


def keys_kernel(
    ids, lens, tok, gain, shift, wk, wv, ok, ov, maps, normed_o, turned_o, k_o, v_o, phi_o, wire_o, kept
):
    row, quad = pl.program_id(0), pl.program_id(1)

    @pl.when(quad == 0)
    def _():
        xhat, _ = normalize(tok[...].astype(f32))
        normed = (xhat * gain[...] + shift[...]).astype(bf16)
        kept[...] = normed
        normed_o[...] = normed
        turned_o[...] = normed.T

    normed = kept[...]
    keys = (nn(normed, wk[...]) + ok[...]).astype(bf16)
    values = (nn(normed, wv[...]) + ov[...]).astype(bf16)
    k_o[...] = keys
    v_o[...] = values
    count = keys.shape[0]
    split = split_of(ids, lens, row, count)
    begin = jnp.where(split < count, split, 0)
    last = sublane((count, PAIR)) >= begin
    ones = segment_ones(2 * F)
    cuts = [slice(p * PAIR, (p + 1) * PAIR) for p in range(2)]
    logits = [nn(keys[:, at], map_weight(maps[at, :], True)) for at in cuts]
    phis = [features(part, ones).astype(bf16) for part in logits]
    for p, at in enumerate(cuts):
        phi_o[:, 2 * p * F : 2 * (p + 1) * F] = phis[p]
    for p, at in enumerate(cuts):
        pair = values[:, at].astype(f32)
        sums = [
            tn(
                jnp.where(last, with_aux(pair, h, 1.0), 0.0).astype(bf16),
                phis[p][:, h * F : (h + 1) * F],
            )
            for h in range(2)
        ]
        put_wire(wire_o, p, sums[0], sums[1], ((HD,), (0,)))


def queries_kernel(normed, wq, oq, maps, q_o, phi_o):
    queries = (nn(normed[...], wq[...]) + oq[...]).astype(bf16)
    q_o[...] = queries
    ones = segment_ones(2 * F)
    cuts = [slice(p * PAIR, (p + 1) * PAIR) for p in range(2)]
    logits = [nn(queries[:, at], map_weight(maps[at, :], False)) for at in cuts]
    for p, part in enumerate(logits):
        phi_o[:, 2 * p * F : 2 * (p + 1) * F] = features(part, ones).astype(bf16)


def attention_kernel(ids, lens, phi_query, phi_key, val, num_o):
    count = val.shape[0]
    split = split_of(ids, lens, pl.program_id(0), count)
    masks = block_masks(split, count, False)
    columns = [slice(h * F, (h + 1) * F) for h in range(4)]
    blocks = [slice(first, first + SUB) for first in range(0, count, SUB)]
    scores = [
        [
            masked(nt(phi_query[rows, at], phi_key[: rows.stop, at]), mask)
            for rows, mask in zip(blocks, masks)
        ]
        for at in columns
    ]
    for h, at in enumerate(columns):
        pair = val[:, h // 2 * PAIR : (h // 2 + 1) * PAIR].astype(f32)
        extended = with_aux(pair, h % 2, 1.0).astype(bf16)
        for rows, part in zip(blocks, scores[h]):
            num_o[rows, at] = nn(part, extended[: rows.stop])


def middle_kernel(
    states, ids, lens, num, phi_query, tok, wo, bias, gain, shift, *rest
):
    wires, (att_o, rden_o, mid_o, normed_o) = rest[: 2 * states], rest[2 * states :]
    count = num.shape[0]
    carry = sublane((count, F)) < split_of(ids, lens, pl.program_id(0), count)
    low = lane((count, PAIR)) < HD
    for p in range(wires[0].shape[1]):
        sums = []
        for h, memory in enumerate(take_wire(arrived(wires, p))):
            column = slice((2 * p + h) * F, (2 * p + h + 1) * F)
            sums.append(
                num[:, column] + jnp.where(carry, nt(phi_query[:, column], memory), 0.0)
            )
        numerator = jnp.where(low, sums[0], sums[1])
        denominator = pltpu.roll(jnp.where(low, sums[1], sums[0]), HD, 1)
        inverse = 1.0 / denominator
        at = slice(p * PAIR, (p + 1) * PAIR)
        rden_o[:, at] = inverse.astype(bf16)
        att_o[:, at] = (numerator * inverse).astype(bf16)
    middle = tok[...].astype(f32) + nn(att_o[...], matrix(wo)) + bias[...]
    mid_o[...] = middle
    xhat, _ = normalize(middle)
    normed_o[...] = (xhat * gain[...] + shift[...]).astype(bf16)


def put_halves(refs, value, core, at):
    if len(refs) == 1:
        refs[0][:, at] = value
        return
    mine_o, other_o = refs
    chips, rows, _ = mine_o.shape
    parted = value.reshape(chips, 2, rows, value.shape[1])
    even, odd = parted[:, 0], parted[:, 1]
    first = core == 0
    mine_o[:, :, at] = jnp.where(first, even, odd).astype(bf16)
    other_o[:, :, at] = jnp.where(first, odd, even).astype(bf16)


def mlp_kernel(plain, ids, lens, normed, cot, ex, sh, bias, branch, mid, *rest):
    out_o, back_o, bg_o, *grads, turned, y_s, back_s, mid_s, sem = rest
    step = pl.program_id(0)
    copy = pltpu.make_async_copy(mid, mid_s, sem)

    @pl.when(step == 0)
    def _():
        copy.start()
        turned[...] = normed[...].T
        y_s[...] = jnp.zeros_like(y_s)
        back_s[...] = jnp.zeros_like(back_s)

    expand, shrink = matrix(ex), matrix(sh)
    pre = nn(normed[...], expand) + bias[...]
    square = pre * pre
    slope, cubic = 0.7978845608028654, 0.044715
    half = 0.5 * jnp.tanh(pre * (slope + slope * cubic * square)) + 0.5
    raised = pre * half
    hidden = raised.astype(bf16)
    rise = half + raised * (1.0 - half) * (2.0 * slope + 6.0 * slope * cubic * square)
    back = (nt(cot[...], shrink) * rise).astype(bf16)
    bg_o[...] = jnp.sum(back.astype(f32), axis=0, keepdims=True)
    y_s[...] += nn(hidden, shrink)
    back_s[...] += nt(back, expand)

    @pl.when(step == pl.num_programs(0) - 1)
    def _():
        copy.wait()
        out_o[...] = (mid_s[...] + y_s[...] + branch[...]).astype(bf16)
        back_o[...] = back_s[...].astype(bf16)

    shrink_grad = tn(hidden, cot[...])
    expand_grad = nn(turned[...], back)
    if plain:
        eg_o, sg_o = grads
        sg_o[...] = shrink_grad
        eg_o[...] = expand_grad
        return
    em_o, eo_o, sm_o, so_o = grads
    core = ids[1] % 2
    first = core == 0
    put_halves((em_o, eo_o), expand_grad, core, slice(None))
    chips, rows, lanes = sm_o.shape
    width = shrink_grad.shape[1]
    subs = lanes // width
    parted = shrink_grad.reshape(chips, 2, subs, rows, width)
    for sub in range(subs):
        even, odd = parted[:, 0, sub], parted[:, 1, sub]
        at = slice(sub * width, (sub + 1) * width)
        sm_o[:, :, at] = jnp.where(first, even, odd).astype(bf16)
        so_o[:, :, at] = jnp.where(first, odd, even).astype(bf16)


def column_sum(values):
    return jnp.sum(values, axis=0, keepdims=True)


def middle_back_kernel(
    parts,
    ids,
    lens,
    mid,
    back,
    cot,
    att,
    rden,
    phi_query,
    wo,
    gain,
    mb_o,
    ext_o,
    wire_o,
    small_o,
    *rest,
):
    *og_refs, og_s, sums_s = rest
    step = pl.program_id(0)
    row, part = step // parts, lax.rem(step, parts)

    @pl.when(step == 0)
    def _():
        og_s[...] = jnp.zeros_like(og_s)
        small_o[...] = jnp.zeros_like(small_o)

    middle = mid[...]
    upstream = cot[...].astype(f32)
    xhat, scale = normalize(middle)
    from_norm = back[...].astype(f32)
    middle_back = upstream + normalize_back(from_norm, xhat, scale, gain[...])
    branch_back = middle_back.astype(bf16)
    mb_o[...] = branch_back
    small_o[0:1, :] += column_sum(from_norm * xhat)
    small_o[1:2, :] += column_sum(from_norm)
    small_o[2:3, :] += column_sum(branch_back.astype(f32))
    small_o[3:4, :] += column_sum(upstream)
    og_s[...] += tn(att[...], branch_back)

    @pl.when(step == pl.num_programs(0) - 1)
    def _():
        put_halves(og_refs, og_s[...], ids[1] % 2, slice(None))

    attended_back = nt(branch_back, matrix(wo))
    count = middle.shape[0]
    carry = sublane((count, F)) < split_of(ids, lens, row, count * parts) - part * count
    ones = segment_ones(PAIR)
    spot = lane((count, PAIR))
    for p in range(wire_o.shape[1]):
        at = slice(p * PAIR, (p + 1) * PAIR)
        given = attended_back[:, at]
        inverse = rden[:, at].astype(f32)
        numerator_back = given * inverse
        denominator_back = -segment_sum(given * att[:, at].astype(f32), ones) * inverse
        aux = pltpu.roll(denominator_back, HD, 1)
        high = aux.astype(bf16).astype(f32)
        rest = aux - high
        for h in range(2):
            first = HD if h == 0 else 0
            extended = with_aux(
                numerator_back,
                h,
                jnp.where(spot == first, high, jnp.where(spot == first + 1, rest, 0.0)),
            ).astype(bf16)
            column = slice((2 * p + h) * F, (2 * p + h + 1) * F)
            ext_o[:, column] = extended
            query = jnp.where(carry, phi_query[:, column].astype(f32), 0.0).astype(bf16)
            total = tn(extended, query)
            sums_s[2 * p + h] = jnp.where(part == 0, total, sums_s[2 * p + h] + total)

    @pl.when(part == parts - 1)
    def _():
        for p in range(wire_o.shape[1]):
            put_wire(wire_o, p, sums_s[2 * p], sums_s[2 * p + 1], ((HD, HD + 1), (0, 1)))


def map_gradient(pair, logits_back):
    both = tn(pair, logits_back)
    rows = pair_rows(both[:, :F], both[:, F:])
    return rows - pltpu.roll(rows, HD, 1)


def add_by_row(out, row, value):
    @pl.when(row == 0)
    def _():
        out[...] = value

    @pl.when(row > 0)
    def _():
        out[...] += value


def local_back_kernel(
    first, states, ids, lens, phi_query, phi_key, val, ext, queries, maps, *rest
):
    wires, (pq_o, kg_o, vg_o, mg_o) = rest[: 2 * states], rest[2 * states :]
    row = pl.program_id(1) + first
    count = val.shape[0]
    split = split_of(ids, lens, row, count)
    flipped = block_masks(split, count, True)
    carry = sublane((count, F)) < split
    ones = segment_ones(2 * F)
    columns = [slice(h * F, (h + 1) * F) for h in range(4)]
    cuts = [slice(p * PAIR, (p + 1) * PAIR) for p in range(2)]
    pairs = [val[:, at].astype(f32) for at in cuts]
    extended = [with_aux(pairs[h // 2], h % 2, 1.0).astype(bf16) for h in range(4)]
    memories = [memory for p in range(2) for memory in take_wire(arrived(wires, p))]
    grads = [
        jnp.where(carry, nn(ext[:, columns[h]], memories[h]), 0.0) for h in range(4)
    ]
    blocks = [slice(first, first + SUB) for first in range(0, count, SUB)]
    heads, tops = [], []
    for h, at in enumerate(columns):
        back, scores = [], []
        for rows, mask in zip(blocks, flipped):
            on = slice(rows.start, count)
            back.append(masked(nt(extended[h][rows], ext[on, at]), mask))
            scores.append(masked(nt(phi_key[rows, at], phi_query[on, at]), mask))
        heads.append((back, scores))
    for h, at in enumerate(columns):
        back, scores = heads[h]
        value_parts = []
        for rows, given, score in zip(blocks, back, scores):
            on = slice(rows.start, count)
            kg_o[rows, at] = nn(given, phi_query[on, at]).astype(bf16)
            value_parts.append(nn(score, ext[on, at]))
        tops.append(jnp.concatenate(value_parts, axis=0))
        query_parts = []
        for i, rows in enumerate(blocks):
            part = [
                tn(given[:, rows.start - on.start : rows.stop - on.start], phi_key[on, at])
                for given, on in zip(back[: i + 1], blocks)
            ]
            query_parts.append(sum(part[1:], part[0]))
        grads[h] = grads[h] + jnp.concatenate(query_parts, axis=0)
    low = lane((count, PAIR)) < HD
    for p, at in enumerate(cuts):
        vg_o[:, at] = jnp.where(low, tops[2 * p], tops[2 * p + 1]).astype(bf16)
    logits_back = [
        features_back(
            phi_query[:, 2 * p * F : 2 * (p + 1) * F],
            jnp.concatenate(grads[2 * p : 2 * p + 2], axis=1),
            ones,
        ).astype(bf16)
        for p in range(2)
    ]
    for p, at in enumerate(cuts):
        pq_o[:, at] = nt(logits_back[p], map_weight(maps[at, :], False)).astype(bf16)
    gradient = [map_gradient(queries[:, at], logits_back[p]) for p, at in enumerate(cuts)]
    gradient = jnp.concatenate(gradient, axis=0)
    mg_o[...] = jnp.where(lane(gradient.shape) < HD, gradient, 0.0)


def keys_back_kernel(
    first, states, ids, lens, kg, vg, phi_key, val, keys, maps, *rest
):
    wires = rest[: 2 * states]
    *from_before, pk_o, pv_o, mg_o = rest[2 * states :]
    row = pl.program_id(1) + first
    count = val.shape[0]
    split = split_of(ids, lens, row, count)
    begin = jnp.where(split < count, split, 0)
    last = sublane((count, F)) >= begin
    low = lane((count, PAIR)) < HD
    ones = segment_ones(2 * F)
    cuts = [slice(p * PAIR, (p + 1) * PAIR) for p in range(2)]
    logits_back = []
    for p, at in enumerate(cuts):
        pair = val[:, at].astype(f32)
        both = arrived(wires, p)
        state = both[0:F]
        spot = sublane(state.shape)
        grads, tops = [], []
        for h, memory in enumerate(take_wire(both)):
            column = slice((2 * p + h) * F, (2 * p + h + 1) * F)
            first = HD if h == 0 else 0
            own = (spot < HD) if h == 0 else (spot >= HD)
            memory = jnp.where(own | (spot == first), memory.astype(f32), 0.0).astype(bf16)
            extended = with_aux(pair, h, 1.0).astype(bf16)
            grads.append(kg[:, column].astype(f32) + jnp.where(last, nn(extended, memory), 0.0))
            tops.append(nt(phi_key[:, column], state))
        pv_o[:, at] = (
            vg[:, at].astype(f32) + jnp.where(last, jnp.where(low, tops[0], tops[1]), 0.0)
        ).astype(bf16)
        at = slice(2 * p * F, 2 * (p + 1) * F)
        logits_back.append(
            features_back(phi_key[:, at], jnp.concatenate(grads, axis=1), ones).astype(bf16)
        )
    for p, at in enumerate(cuts):
        pk_o[:, at] = nt(logits_back[p], map_weight(maps[at, :], True)).astype(bf16)
    gradient = jnp.concatenate(
        [
            pltpu.roll(map_gradient(keys[:, at], logits_back[p]), HD, 1)
            for p, at in enumerate(cuts)
        ],
        axis=0,
    )
    before = sum(part[...] for part in from_before)
    mg_o[...] = before + jnp.where(lane(gradient.shape) < HD, 0.0, gradient)


def weight_back_kernel(ids, lens, turned, pb, *refs):
    put_halves(refs, nn(turned[...], pb[...]), ids[1] % 2, slice(None))


def key_weight_back_kernel(
    steps, devices, ids, lens, turned, pk, small_in, small_mid, hid, maps, *rest
):
    *refs, lines = rest
    step = pl.program_id(0)
    core = ids[1] % 2

    @pl.when(step < steps)
    def _():
        put_halves(refs, nn(turned[...], pk[...]), core, slice(None))

    if devices:

        @pl.when(step == steps)
        def _():
            pack(devices, core, small_in, small_mid, hid, maps, *refs, lines)


def input_back_kernel(pq, pk, pv, wq, wk, wv, tok, mb, gain, out_o, small_o):
    @pl.when(pl.program_id(0) == 0)
    def _():
        small_o[...] = jnp.zeros_like(small_o)

    from_norm = nt(pq[...], wq[...]) + nt(pk[...], wk[...]) + nt(pv[...], wv[...])
    xhat, scale = normalize(tok[...].astype(f32))
    small_o[0:1, :] += column_sum(from_norm * xhat)
    small_o[1:2, :] += column_sum(from_norm)
    for i, part in enumerate((pq, pk, pv)):
        small_o[2 + i : 3 + i, :] += column_sum(part[...].astype(f32))
    out_o[...] = (mb[...].astype(f32) + normalize_back(from_norm, xhat, scale, gain[...])).astype(bf16)


def spec(shape, index):
    return pl.BlockSpec(memory_space=pl.ANY) if shape is None else pl.BlockSpec(shape, index)


def estimate(micros):
    return pl.CostEstimate(
        flops=int(micros * PACE * 1e9), bytes_accessed=int(micros * PACE * 1e6), transcendentals=0
    )


MARKS = {}


def mark_of(array):
    return MARKS[id(array)][1] if id(array) in MARKS else array


def call(kernel, grid, ins, outs, scratch=(), scalars=0, name=None, micros=10, waits=(), into=()):
    waits = [mark_of(array) for array in waits]
    arrays = [entry[0] for entry in ins[scalars:]]
    if name not in FREE_INS:
        arrays = [pltpu.with_memory_space_constraint(array, pltpu.HBM) for array in arrays]
    arrays += [pltpu.with_memory_space_constraint(array, pltpu.HBM) for array in waits]
    arrays += into
    fetched = [entry[0] for entry in ins[:scalars]]
    read, given = len(ins), len(ins) + len(waits) + len(into)

    def body(*refs):
        refs[given + len(outs)][...] = jnp.zeros((8, F), f32)
        kernel(*refs[:read], *refs[given : given + len(outs)], *refs[given + len(outs) + 1 :])

    def shaped(shape, kind, block, index, free=False):
        return (jax.ShapeDtypeStruct if free else pltpu.HBM)(shape, kind)

    *results, mark = pl.pallas_call(
        body,
        out_shape=[shaped(*out) for out in outs] + [pltpu.HBM((8, F), f32)],
        grid_spec=pltpu.PrefetchScalarGridSpec(
            num_scalar_prefetch=scalars,
            grid=grid,
            in_specs=[spec(block, index) for _, block, index in ins[scalars:]]
            + [pl.BlockSpec(memory_space=pl.ANY)] * (given - read),
            out_specs=[spec(*out[2:4]) for out in outs]
            + [spec((8, F), lambda *i: (0, 0))],
            scratch_shapes=list(scratch),
        ),
        compiler_params=pltpu.CompilerParams(
            vmem_limit_bytes=LIMITS.get(name, LIMIT) * 1024 * 1024
        ),
        cost_estimate=estimate(micros),
        input_output_aliases={given - len(into) + i: i for i in range(len(into))},
        name=name,
    )(*fetched, *arrays)
    MARKS.update((id(result), (result, mark)) for result in results)
    return results


def tie_kernel(*refs):
    del refs


def tie(values, *waits):
    anywhere = pl.BlockSpec(memory_space=pl.ANY)
    count = len(values)
    waits = [mark_of(array) for array in waits]
    return pl.pallas_call(
        tie_kernel,
        out_shape=[jax.ShapeDtypeStruct(v.shape, v.dtype) for v in values],
        in_specs=[anywhere] * (count + len(waits)),
        out_specs=[anywhere] * count,
        input_output_aliases={i: i for i in range(count)},
        cost_estimate=estimate(0.5),
        name="tie",
    )(*values, *waits)


def gather_rows(part):
    return lax.all_gather(part, AXES, axis=0, tiled=True)


def scatter_rows(whole):
    return lax.psum_scatter(whole, AXES, scatter_dimension=0, tiled=True)


def scatter_columns(rows):
    return lax.psum_scatter(rows, AXES, scatter_dimension=1, tiled=True)


def swap(array, mask, axis="seq", name="swap"):
    size = lax.axis_size(axis)
    with jax.named_scope(name):
        return lax.ppermute(array, axis, [(i, i ^ mask) for i in range(size)])


def gather_cores(pieces, name):
    return pieces + [swap(piece, 1, name=name) for piece in pieces]


def put_piece(cuts, outs, at, piece):
    for out, first, last, sub in cuts:
        if sub is None:
            outs[out][at] = piece[:, first:last]
        else:
            outs[out][at, sub] = piece[:, first:last]


def place_kernel(cuts, ids, *refs):
    pieces, outs = refs[:8], refs[8:]

    def put(at, chips):
        for core in range(2):
            for piece, pair in zip(pieces[4 * core + at : 4 * core + at + 2], chips):
                for r, chip in enumerate(pair):
                    put_piece(cuts, outs, ids[1] ^ (2 * chip + core), piece[r, 0])

    @pl.when(pl.program_id(0) < 2)
    def _():
        put(0, ((0, 1), (2, 3)))

    @pl.when(pl.program_id(0) >= 2)
    def _():
        put(2, ((0, 2), (1, 3)))


def place(pieces, ids, cuts, shapes, name, micros, waits=()):
    rows, wide = pieces[0].shape[-2:]
    near = lambda s: jnp.minimum(s, 1)
    far = lambda s: jnp.maximum(s - 2, 0)
    ins = [
        (p.reshape(2, 2, rows, wide), (2, 1, rows, wide), lambda s, ids, at=at: (0, at(s), 0, 0))
        for p, at in zip(pieces, (near, near, far, far) * 2)
    ]

    def target(shape):
        return lambda s, ids: (ids[0] ^ s,) + (0,) * len(shape)

    return call(
        functools.partial(place_kernel, cuts),
        (4,),
        [(ids, None, None)] + ins,
        [((32, *shape), bf16, (8, *shape), target(shape), True) for shape in shapes],
        [],
        1,
        name,
        micros,
        waits,
    )


def first_sum_kernel(parts, ids, *refs):
    ins, (near_keep, near_send, far_keep, far_send) = refs[: parts * 8], refs[parts * 8 :]
    step = pl.program_id(0)

    def put(targets):
        at = 0
        for part in range(parts):
            wide = ins[part * 8].shape[-1]
            for r, (out, i) in enumerate(targets):
                mine, got = ins[(part * 4 + r) * 2 : (part * 4 + r) * 2 + 2]
                total = mine[0, 0].astype(f32) + got[0, 0].astype(f32)
                out[i, 0, :, at : at + wide] = total.astype(bf16)
            at += wide

    @pl.when(step < 2)
    def _():
        put(((near_keep, 0), (near_send, 0), (near_keep, 1), (near_send, 1)))

    @pl.when(step >= 2)
    def _():
        put(((far_keep, 0), (far_keep, 1), (far_send, 0), (far_send, 1)))


def first_sum(mines, gots, ids, name, micros=4, waits=()):
    rows = mines[0].shape[-2]
    wides = [m.shape[-1] for m in mines]
    ins = [(ids, None, None)]

    def index(r):
        return lambda k, ids: (ids[0] ^ k, (ids[1] // 2) ^ r, 0, 0)

    for mine, got, wide in zip(mines, gots, wides):
        for r in range(4):
            for array in (mine, got):
                ins.append((array.reshape(4, 4, rows, wide), (1, 1, rows, wide), index(r)))
    total, last = sum(wides), name[0] == "k"
    near = lambda k, ids: (0, jnp.minimum(k, 1), 0, 0)
    far = lambda k, ids: (0, jnp.maximum(k - 2, 0), 0, 0)
    return call(
        functools.partial(first_sum_kernel, len(mines)),
        (4,),
        ins,
        [
            ((2, 2, rows, total), bf16, (2, 1, rows, total), at, free)
            for at, free in ((near, last), (near, name[0] != "m"), (far, last), (far, True))
        ],
        [],
        1,
        name,
        micros,
        waits,
    )


def middle_sum_kernel(near_keep, near_got, far_keep, far_got, *outs):
    for at, (kept, got) in enumerate(((near_keep, near_got), (far_keep, far_got))):
        for i in range(2):
            total = kept[i].astype(f32) + got[i].astype(f32)
            outs[2 * at + i][...] = total.astype(bf16)


def middle_sum(sums, name, micros=3, waits=()):
    near_keep, near_send, far_keep, far_send = sums
    pieces = [near_keep, swap(near_send, 2, name=name + "_x1")]
    pieces += [far_keep, swap(far_send, 4, name=name + "_y1")]
    _, _, rows, wide = near_keep.shape
    tile = 1536 if wide % 1536 == 0 else wide
    near_keep, near_send, far_keep, far_send = call(
        middle_sum_kernel,
        (wide // tile,),
        [(p, (2, 2, rows, tile), lambda g: (0, 0, 0, g)) for p in pieces],
        [
            ((2, rows, wide), bf16, (2, rows, tile), lambda g: (0, 0, g), free)
            for free in (name[0] == "k", True) * 2
        ],
        [],
        0,
        name,
        micros,
        waits,
    )
    near_got, far_got = swap(near_send, 4, name=name + "_y2"), swap(far_send, 2, name=name + "_x2")
    return [near_keep, near_got, far_keep, far_got]


def second_sum_kernel(direct, near, near_got, far, far_got, *outs):
    for k in range(4):
        kept, got = (near, near_got) if k < 2 else (far, far_got)
        total = kept[k % 2].astype(f32) + got[k % 2].astype(f32)
        if direct:
            outs[k][...] = total.astype(outs[k].dtype)
        else:
            outs[k % 2][k // 2] = total.astype(outs[k % 2].dtype)


def second_sum(pieces, name, micros=3, waits=(), direct=True):
    _, rows, wide = pieces[0].shape
    tile = 1536 if wide % 1536 == 0 else wide
    if direct:
        shape, cut = (rows, wide), (rows, tile)
        outs = [(shape, bf16 if k else f32, cut, lambda g: (0, g), k > 0) for k in range(4)]
    else:
        shape, cut = (2, rows, wide), (2, rows, tile)
        outs = [(shape, bf16 if k else f32, cut, lambda g: (0, 0, g), k > 0) for k in range(2)]
    return call(
        functools.partial(second_sum_kernel, direct),
        (wide // tile,),
        [(p, (2, rows, tile), lambda g: (0, 0, g)) for p in pieces],
        outs,
        [],
        0,
        name,
        micros,
        waits,
    )


def reduce_batch(sums, name):
    got = [swap(sums[k], k, "batch", name + "_layer") for k in range(1, 4)]
    return sums[0] + sum(part.astype(f32) for part in got)


def reduce_layer1(sums, name, waits):
    (kept,) = tie(sums[:1], *waits)
    return kept + swap(sums[1], 1, "batch", name + "_layer1").astype(f32)


def reduce_layer2(pair, name, waits):
    got = swap(pair[1].astype(bf16), 2, "batch", name + "_layer2")
    (kept,) = tie([pair[0]], *waits)
    return kept + got.astype(f32)


def spots(length, each, owners):
    at = lane((F, length))
    owner = ((at.astype(f32) + 0.5) * (1.0 / each)).astype(jnp.int32)
    inside = (at - owner * each == sublane((F, length))).astype(bf16)
    at = lane((owners.shape[0], length))
    owner = ((at.astype(f32) + 0.5) * (1.0 / each)).astype(jnp.int32)
    return inside, owner == owners


def unpack_kernel(devices, block, *outs):
    rows = block.shape[0] // devices
    vectors = [(out, i) for out in outs for i in range(out.shape[0])]
    count = len(vectors)
    place_at = lane((count * devices, block.shape[0]))
    line = sublane((count * devices, block.shape[0]))
    vector = ((line.astype(f32) + 0.5) * (1.0 / devices)).astype(jnp.int32)
    picked = nn(
        (place_at == (line - vector * devices) * rows + vector).astype(bf16), block[...]
    ).astype(bf16)
    for j, (out, i) in enumerate(vectors):
        length = out.shape[1]
        owners = sublane((devices, length))
        inside, owned = spots(length, length // devices, owners)
        spread = nn(picked[j * devices : (j + 1) * devices], inside)
        out[i : i + 1, :] = column_sum(jnp.where(owned, spread, 0.0))


def shards_kernel(
    gain, shift, mix, offset, maps, out, branch, ex, hid, sh, first_o, rest_o, small
):
    rows = mix.shape[0]
    small[...] = jnp.zeros_like(small)
    for j, part in enumerate((gain, shift, branch)):
        small[2 * j : 2 * j + 2, 0:rows] = part[...].astype(f32)
    small[6:7, 0 : 3 * rows] = offset[...].astype(f32)
    small[7:8, 0 : 4 * rows] = hid[...].astype(f32)
    wide, width = mix.shape[1], sh.shape[1]
    first_o[:, 0:wide] = mix[...]
    first_o[:, wide : wide + F] = maps[...]
    first_o[:, wide + F : wide + 2 * F] = small[...].astype(bf16)
    for i in range(4):
        rest_o[i] = ex[:, i * width : (i + 1) * width]
        rest_o[4 + i] = sh[i * rows : (i + 1) * rows, :].astype(f32).astype(bf16)
    rest_o[8] = out[...]


def pack(devices, core, small_in, small_mid, hid, maps, mine_o, other_o, lines):
    offset = jnp.concatenate([small_in[i : i + 1, :] for i in range(2, 5)], axis=1)
    lines[...] = jnp.zeros_like(lines)
    vectors = [
        small_in[0:1, :],
        small_mid[0:1, :],
        small_in[1:2, :],
        small_mid[1:2, :],
        small_mid[2:3, :],
        small_mid[3:4, :],
        offset,
        hid[...],
    ]
    half = devices // 2
    for j, vector in enumerate(vectors):
        length = vector.shape[1]
        line = sublane((devices, length))
        owners = jnp.where(line < half, 2 * line + core, 2 * (line - half) + 1 - core)
        inside, owned = spots(length, length // devices, owners)
        share = jnp.where(owned, vector, 0.0).astype(bf16)
        lines[:, j, :] = nt(share, inside)
    put_halves((mine_o, other_o), maps[...], core, slice(0, F))
    mine_o[:, :, F:] = lines[:half].astype(bf16)
    other_o[:, :, F:] = lines[half:].astype(bf16)


def flags_kernel(levels, count, ids, lens, *outs):
    mine = ids[1]
    for row in range(lens.shape[0]):
        flags = []
        for reverse in (False, True):
            for level in range(levels):
                span = 1 << level
                begin = mine - lax.rem(mine, span)
                upper = lax.rem(mine // span, 2) == 1
                own_closed = starts_within(lens, row, begin * count, (begin + span) * count)
                if reverse:
                    receives = jnp.logical_not(upper)
                    closed = starts_within(lens, row, (mine + 1) * count, (begin + span) * count)
                    other = starts_within(lens, row, (begin - span) * count, begin * count)
                else:
                    receives = upper
                    closed = starts_within(lens, row, begin * count, mine * count)
                    other = starts_within(
                        lens, row, (begin + span) * count, (begin + 2 * span) * count
                    )
                flags.append(receives & jnp.logical_not(closed))
                flags.append(receives | jnp.logical_not(other))
                flags.append(jnp.logical_not(receives & own_closed))
        for out, flag in zip(outs, flags):
            out[row] = jnp.full((1, 1, F), jnp.where(flag, 1.0, 0.0), f32)


def carry(total, came, flags, level, reverse, waits=()):
    levels = len(flags) // 6
    at = 3 * (level + (levels if reverse else 0))
    reaches, keeps, joins = flags[at : at + 3]
    other = swap(total, 1 << level, name=f"state{level}")
    came = came + [(other, reaches)]
    if level == levels - 1:
        return None, came
    if len(waits):
        keeps, joins = tie([keeps, joins], *waits)
    return (keeps * total.astype(f32) + joins * other.astype(f32)).astype(bf16), came


def local(
    tokens,
    sequence_lengths,
    norm_gains,
    norm_shifts,
    mixing_weight,
    mixing_offset,
    feature_maps,
    output_weight,
    branch_offsets,
    expand_weight,
    hidden_offset,
    shrink_weight,
    cotangent,
):
    MARKS.clear()
    row_count, tok_count, width = tokens.shape
    count = row_count * tok_count
    heads = width // HD
    pairs, quads = heads // 2, heads // 4
    quad = 2 * PAIR
    hidden_width = expand_weight.shape[1]
    batch, size = lax.axis_size("batch"), lax.axis_size("seq")
    devices = batch * size
    share = width // devices
    plain = size != 8 or batch != 4 or share % 8 != 0 or hidden_width != 4 * width or 4 * share > F

    mine = lax.axis_index("seq").astype(jnp.int32)
    ids = jnp.stack([lax.axis_index("batch").astype(jnp.int32), mine])
    lens = sequence_lengths
    scalars = [(ids, None, None), (lens, None, None)]
    levels = size.bit_length() - 1
    flag = (row_count, 1, 1, F)
    flags = call(
        functools.partial(flags_kernel, levels, tok_count),
        (1,),
        scalars,
        [(flag, f32, flag, lambda i, *s: (0, 0, 0, 0))] * (6 * levels),
        [],
        2,
        "flags",
        1,
    )

    if plain:
        gains = lax.all_gather(norm_gains, AXES, axis=1, tiled=True).astype(f32)[:, None]
        shifts = lax.all_gather(norm_shifts, AXES, axis=1, tiled=True).astype(f32)[:, None]
        branches = lax.all_gather(branch_offsets, AXES, axis=1, tiled=True).astype(f32)[:, None]
        offset = gather_rows(mixing_offset).astype(f32)[None]
        hidden_bias = gather_rows(hidden_offset).astype(f32)[None]
        first_weight = jnp.concatenate(
            [gather_rows(mixing_weight), gather_rows(feature_maps)], axis=1
        )
        out_weight = gather_rows(output_weight)
        expand = gather_rows(expand_weight)
        shrink = gather_rows(shrink_weight)
    else:
        wide = 3 * width + 2 * F
        shards = (
            norm_gains,
            norm_shifts,
            mixing_weight,
            mixing_offset[None],
            feature_maps,
            output_weight,
            branch_offsets,
            expand_weight,
            hidden_offset[None],
            shrink_weight,
        )
        at = lambda i: (0, 0)
        first, rest = call(
            shards_kernel,
            (1,),
            [(array, array.shape, at) for array in shards],
            [
                ((share, wide), bf16, (share, wide), at, True),
                ((9, share, width), bf16, (9, share, width), lambda i: (0, 0, 0)),
            ],
            [pltpu.VMEM((share, F), f32)],
            0,
            "shards",
            2,
        )
        layers = [first] + [swap(first, k, "batch", "first_layer") for k in range(1, 4)]
        near, far = jnp.stack(layers[:2]), jnp.stack(layers[2:])
        rest = lax.all_gather(rest, AXES)
        near = jnp.concatenate([near, swap(near, 2, name="first_x1")])
        far = jnp.concatenate([far, swap(far, 4, name="first_y1")])
        first = [
            near,
            swap(near, 4, name="first_y2"),
            far,
            swap(far, 2, name="first_x2"),
        ]
        first = gather_cores(first, "first_core")
        (first_weight,) = place(
            first, ids, ((0, 0, wide, None),), ((share, wide),), "place_first", 5
        )
        first_weight = first_weight.reshape(width, -1)
        *rows_out, offset, hidden_bias = call(
            functools.partial(unpack_kernel, devices),
            (1,),
            [(first_weight, (width, F), lambda i: (0, 3 * width // F + 1))],
            [
                ((n, length), f32, (n, length), lambda i: (0, 0))
                for n, length in [(1, width)] * 6 + [(1, 3 * width), (1, hidden_width)]
            ],
            [],
            0,
            "unpack",
            2,
        )
        gains, shifts, branches = (rows_out[i : i + 2] for i in (0, 2, 4))

    tok = tokens.reshape(count, width)
    cot = cotangent.reshape(count, width)
    full = lambda r, q, *s: (0, 0)

    def columns(first):
        return lambda r, q, *s: (0, first + q)

    own = lambda r, q, *s: (r, 0)
    cell = lambda r, q, *s: (r, q)
    normed, turned, keys, values, phi_key, wire = call(
        keys_kernel,
        (row_count, quads),
        [
            *scalars,
            (tok, (tok_count, width), own),
            (gains[0], (1, width), full),
            (shifts[0], (1, width), full),
            (first_weight, (width, quad), columns(quads)),
            (first_weight, (width, quad), columns(2 * quads)),
            (offset, (1, quad), columns(quads)),
            (offset, (1, quad), columns(2 * quads)),
            (first_weight, (quad, F), lambda r, q, *s: (q, 3 * width // F)),
        ],
        [
            ((count, width), bf16, (tok_count, width), own),
            ((width, count), bf16, (width, tok_count), lambda r, q, *s: (0, r)),
            ((count, width), bf16, (tok_count, quad), cell),
            ((count, width), bf16, (tok_count, quad), cell),
            ((count, heads * F), bf16, (tok_count, 4 * F), cell),
            (
                (row_count, pairs, WIRE, F),
                bf16,
                (1, 2, WIRE, F),
                lambda r, q, *s: (r, q, 0, 0),
            ),
        ],
        [pltpu.VMEM((tok_count, width), bf16)],
        2,
        "keys",
        15,
        flags,
    )
    queries, phi_query = call(
        queries_kernel,
        (row_count, quads),
        [
            (normed, (tok_count, width), own),
            (first_weight, (width, quad), columns(0)),
            (offset, (1, quad), columns(0)),
            (first_weight, (quad, F), lambda r, q, *s: (q, 3 * width // F)),
        ],
        [
            ((count, width), bf16, (tok_count, quad), cell),
            ((count, heads * F), bf16, (tok_count, 4 * F), cell),
        ],
        [],
        0,
        "queries",
        8,
    )
    total, came = carry(wire, [], flags, 0, False)
    total, came = carry(total, came, flags, 1, False, (phi_query,))
    (numerator,) = call(
        attention_kernel,
        (row_count, quads),
        [
            *scalars,
            (phi_query, (tok_count, 4 * F), cell),
            (phi_key, (tok_count, 4 * F), cell),
            (values, (tok_count, quad), cell),
        ],
        [((count, heads * F), f32, (tok_count, 4 * F), cell)],
        [],
        2,
        "attention",
        12,
        (total,),
    )
    for level in range(2, levels):
        total, came = carry(total, came, flags, level, False, (numerator,))

    def states(came, pairs_of, index):
        wires = [
            (wire, (1, pairs_of, WIRE, F), lambda *i: (*index(*i), 0, 0)) for wire, _ in came
        ]
        reaches = [
            (reach, (1, 1, 1, F), lambda *i: (index(*i)[0], 0, 0, 0)) for _, reach in came
        ]
        return wires + reaches

    memories = came
    if plain:
        out_part = (out_weight, (width, width), lambda r, *s: (0, 0))
        expand_part = (expand, (width, width), lambda f, *s: (0, f))
        shrink_part = (shrink, (width, width), lambda f, *s: (f, 0))
    else:
        cut = (devices, 1, share, width)
        out_part = (rest, cut, lambda r, *s: (0, 8, 0, 0))
        expand_part = (rest, cut, lambda f, *s: (0, f, 0, 0))
        cut = (devices // 4, 4, share, width)
        shrink_part = (rest, cut, lambda f, *s: (f, 1, 0, 0))
    whole = lambda r, *s: (0, 0)
    one = lambda r, *s: (r, 0)
    attended, inverse, middle, normed_mid = call(
        functools.partial(middle_kernel, len(memories)),
        (row_count,),
        [
            *scalars,
            (numerator, (tok_count, heads * F), one),
            (phi_query, (tok_count, heads * F), one),
            (tok, (tok_count, width), one),
            out_part,
            (branches[0], (1, width), whole),
            (gains[1], (1, width), whole),
            (shifts[1], (1, width), whole),
            *states(memories, pairs, lambda r, *s: (r, 0)),
        ],
        [
            ((count, width), bf16, (tok_count, width), one),
            ((count, width), bf16, (tok_count, width), one),
            ((count, width), f32, (tok_count, width), one),
            ((count, width), bf16, (tok_count, width), one),
        ],
        [],
        2,
        "middle",
        9,
    )
    tile = width
    steps = hidden_width // tile

    def halves(wide, block, index):
        if plain:
            return [((width, wide), f32, (width, block), lambda *i: (0, index(*i)))]
        shape = (devices // 2, share, wide)
        cut = (devices // 2, share, block)
        return [(shape, bf16, cut, lambda *i: (0, 0, index(*i)), True)] * 2

    layer_output, normed_mid_back, hidden_grad, *mlp_grads = call(
        functools.partial(mlp_kernel, plain),
        (steps,),
        [
            *scalars,
            (normed_mid, (count, width), lambda f, *s: (0, 0)),
            (cot, (count, width), lambda f, *s: (0, 0)),
            expand_part,
            shrink_part,
            (hidden_bias, (1, tile), lambda f, *s: (0, f)),
            (branches[1], (1, width), whole),
            (middle, None, None),
        ],
        [
            ((count, width), bf16, (count, width), lambda f, *s: (0, 0)),
            ((count, width), bf16, (count, width), lambda f, *s: (0, 0)),
            ((1, hidden_width), f32, (1, tile), lambda f, *s: (0, f)),
            *halves(hidden_width, tile, lambda f, *s: f),
            *(
                [((hidden_width, width), f32, (tile, width), lambda f, *s: (f, 0))]
                if plain
                else [
                    (
                        (devices // 2, share, 4 * width),
                        bf16,
                        (devices // 2 // steps, share, 4 * width),
                        lambda f, *s: (f, 0, 0),
                        True,
                    )
                ]
                * 2
            ),
        ],
        [pltpu.VMEM((width, count), bf16)]
        + [pltpu.VMEM((count, width), f32)] * 3
        + [pltpu.SemaphoreType.DMA],
        2,
        "mlp",
        37,
    )
    middle_back, extended, wire_back, small_mid, *output_grads = call(
        functools.partial(middle_back_kernel, 1),
        (row_count,),
        [
            *scalars,
            (middle, (tok_count, width), one),
            (normed_mid_back, (tok_count, width), one),
            (cot, (tok_count, width), one),
            (attended, (tok_count, width), one),
            (inverse, (tok_count, width), one),
            (phi_query, (tok_count, heads * F), one),
            out_part,
            (gains[1], (1, width), whole),
        ],
        [
            ((count, width), bf16, (tok_count, width), one),
            ((count, heads * F), bf16, (tok_count, heads * F), one),
            ((row_count, pairs, WIRE, F), bf16, (1, pairs, WIRE, F), lambda r, *s: (r, 0, 0, 0)),
            ((8, width), f32, (8, width), whole),
            *halves(width, width, lambda r, *s: 0),
        ],
        [pltpu.VMEM((width, width), f32), pltpu.VMEM((heads, F, F), f32)],
        2,
        "middle_back",
        17,
    )
    total, came = carry(wire_back, [], flags, 0, True)
    if not plain:
        expand_mine, expand_other, shrink_mine, shrink_other = mlp_grads
        mlp_waits = first_sum(
            (expand_mine, shrink_mine),
            (swap(expand_other, 1, name="mlp_core"), swap(shrink_other, 1, name="mlp_core")),
            ids,
            "mlp_first_sum",
            7,
            (wire_back,),
        )
    cell = lambda p, r, *s: (r, p)
    of_pair = lambda p, r, *s: (p, 0)
    from_wire = lambda p, r, *s: (r, p, 0, 0)

    def attend_back(first, into=(), waits=()):
        cell = lambda p, r, *s: (r + first, p)
        return call(
            functools.partial(local_back_kernel, first, len(memories)),
            (quads, 1),
            [
                *scalars,
                (phi_query, (tok_count, 4 * F), cell),
                (phi_key, (tok_count, 4 * F), cell),
                (values, (tok_count, quad), cell),
                (extended, (tok_count, 4 * F), cell),
                (queries, (tok_count, quad), cell),
                (first_weight, (quad, F), lambda p, r, *s: (p, 3 * width // F)),
                *states(memories, 2, lambda p, r, *s: (r + first, p)),
            ],
            [
                ((count, width), bf16, (tok_count, quad), cell),
                ((count, heads * F), bf16, (tok_count, 4 * F), cell),
                ((count, width), bf16, (tok_count, quad), cell),
                ((width, F), f32, (quad, F), of_pair),
            ],
            [],
            2,
            "local_back",
            25 / row_count,
            waits,
            into,
        )

    partial, maps_query = (), []
    for level in range(1, levels):
        if level <= row_count:
            waits = (total, *(mlp_waits[:1] if level == 1 and not plain else ()))
            *partial, map_query = attend_back(level - 1, partial, waits)
            maps_query.append(map_query)
        total, came = carry(total, came, flags, level, True, partial[:1])
        if level == 1 and not plain:
            mlp_waits = [mlp_waits[0], *tie(mlp_waits[1:2], total), *mlp_waits[2:]]
    for first in range(levels - 1, row_count):
        *partial, map_query = attend_back(first, partial)
        maps_query.append(map_query)
    queries_back, key_feat, value_feat = partial

    def weight_back(pb, waits=()):
        return call(
            weight_back_kernel,
            (quads,),
            [
                *scalars,
                (turned, (width, count), lambda q, *s: (0, 0)),
                (pb, (count, quad), lambda q, *s: (0, q)),
            ],
            halves(width, quad, lambda q, *s: q),
            [],
            2,
            "weight_back",
            5,
            waits,
        )

    query_grads = weight_back(queries_back)

    def attend_keys_back(first, map_grads, into=(), waits=()):
        cell = lambda p, r, *s: (r + first, p)
        return call(
            functools.partial(keys_back_kernel, first, len(came)),
            (quads, 1),
            [
                *scalars,
                (key_feat, (tok_count, 4 * F), cell),
                (value_feat, (tok_count, quad), cell),
                (phi_key, (tok_count, 4 * F), cell),
                (values, (tok_count, quad), cell),
                (keys, (tok_count, quad), cell),
                (first_weight, (quad, F), lambda p, r, *s: (p, 3 * width // F)),
                *states(came, 2, lambda p, r, *s: (r + first, p)),
                *[(map_grad, (quad, F), of_pair) for map_grad in map_grads],
            ],
            [
                ((count, width), bf16, (tok_count, quad), cell),
                ((count, width), bf16, (tok_count, quad), cell),
                ((width, F), f32, (quad, F), of_pair),
            ],
            [],
            2,
            "keys_back",
            13 / row_count,
            waits,
            into,
        )

    *partial, map_grad = attend_keys_back(0, maps_query, (), query_grads[:1])
    if not plain:
        mlp_sums = middle_sum(mlp_waits, "mlp_middle_sum", 4, partial[:1])
    for first in range(1, row_count):
        waits = () if plain else mlp_sums[:1]
        *partial, map_grad = attend_keys_back(first, [map_grad], partial, waits)
    keys_back, values_back = partial
    value_grads = weight_back(values_back)
    if not plain:
        mlp_sums = second_sum(mlp_sums, "mlp_second_sum", 4, value_grads[:1], False)
        query_waits = first_sum(
            (query_grads[0], output_grads[0], value_grads[0]),
            (
                swap(query_grads[1], 1, name="query_core"),
                swap(output_grads[1], 1, name="query_core"),
                swap(value_grads[1], 1, name="query_core"),
            ),
            ids,
            "query_first_sum",
            3,
            mlp_sums[:1],
        )
    row = lambda r: (r, 0)
    fixed = lambda r: (0, 0)
    input_gradient, small_in = call(
        input_back_kernel,
        (count // SUB,),
        [
            (queries_back, (SUB, width), row),
            (keys_back, (SUB, width), row),
            (values_back, (SUB, width), row),
            (first_weight, (width, width), lambda r: (0, 0)),
            (first_weight, (width, width), lambda r: (0, 1)),
            (first_weight, (width, width), lambda r: (0, 2)),
            (tok, (SUB, width), row),
            (middle_back, (SUB, width), row),
            (gains[0], (1, width), fixed),
        ],
        [
            ((count, width), bf16, (SUB, width), row),
            ((8, width), f32, (8, width), fixed),
        ],
        [],
        0,
        "input_back",
        10,
        () if plain else query_waits[:1],
    )
    if not plain:
        query_sums = middle_sum(query_waits, "query_middle_sum", 2, (input_gradient,))
    small_parts = [
        (array, array.shape, lambda q, *s: (0, 0))
        for array in (small_in, small_mid, hidden_grad, map_grad)
    ]
    key_grads = call(
        functools.partial(key_weight_back_kernel, quads, 0 if plain else devices),
        (quads + (0 if plain else 1),),
        [
            *scalars,
            (turned, (width, count), lambda q, *s: (0, 0)),
            (keys_back, (count, quad), lambda q, *s: (0, jnp.minimum(q, quads - 1))),
            *small_parts,
        ],
        halves(width + (0 if plain else quad), quad, lambda q, *s: q),
        [pltpu.VMEM((devices, share, F), f32)],
        2,
        "key_weight_back",
        10,
        () if plain else query_sums[:1],
    )
    if plain:
        mixing_grad = jnp.concatenate([query_grads[0], key_grads[0], value_grads[0]], axis=1)
        offset_grad = small_in[2:5].reshape(-1)
        grads = (
            scatter_columns(jnp.stack([small_in[0], small_mid[0]])),
            scatter_columns(jnp.stack([small_in[1], small_mid[1]])),
            scatter_rows(mixing_grad),
            scatter_rows(offset_grad),
            scatter_rows(map_grad),
            scatter_rows(output_grads[0]),
            scatter_columns(small_mid[2:4]),
            scatter_rows(mlp_grads[0]),
            scatter_rows(hidden_grad[0]),
            scatter_rows(mlp_grads[1]),
        )
    else:
        query_sums = second_sum(query_sums, "query_second_sum", 3, (key_grads[0],), False)
        mlp_pair = reduce_layer1(mlp_sums, "mlp", query_sums[:1])
        key_sums = first_sum(
            (key_grads[0],),
            (swap(key_grads[1], 1, name="key_core"),),
            ids,
            "key_first_sum",
            4,
            (mlp_pair,),
        )
        query_pair = reduce_layer1(query_sums, "query", key_sums[:1])
        key_sums = middle_sum(key_sums, "key_middle_sum", 2, (query_pair,))
        key_sums = second_sum(key_sums, "key_second_sum")
        mlp_total = reduce_layer2(mlp_pair, "mlp", key_sums[:1])
        query_total = reduce_layer2(query_pair, "query", key_sums[:1])
        key_total = reduce_batch(key_sums, "key")
        small_total = key_total[0:8, width + F :]
        mixing_grad = jnp.concatenate(
            [query_total[:, :width], key_total[:, :width], query_total[:, 2 * width :]], axis=1
        )
        shrink_grad = mlp_total[:, hidden_width:].reshape(share, 4, width)
        grads = (
            small_total[0:2, :share],
            small_total[2:4, :share],
            mixing_grad,
            small_total[6, : 3 * share],
            key_total[:, width : width + F],
            query_total[:, width : 2 * width],
            small_total[4:6, :share],
            mlp_total[:, :hidden_width],
            small_total[7, : 4 * share],
            shrink_grad.transpose(1, 0, 2).reshape(4 * share, width),
        )
    return (layer_output.reshape(tokens.shape), input_gradient.reshape(tokens.shape), *grads)


def solution(mesh):
    rows = P("batch", "seq", None)
    split_rows = P(AXES, None)
    split_columns = P(None, AXES)
    split_vector = P(AXES)
    return jax.shard_map(
        local,
        mesh=mesh,
        in_specs=(
            rows,
            P("batch", None),
            split_columns,
            split_columns,
            split_rows,
            split_vector,
            split_rows,
            split_rows,
            split_columns,
            split_rows,
            split_vector,
            split_rows,
            rows,
        ),
        out_specs=(
            rows,
            rows,
            split_columns,
            split_columns,
            split_rows,
            split_vector,
            split_rows,
            split_rows,
            split_columns,
            split_rows,
            split_vector,
            split_rows,
        ),
        check_vma=False,
    )
```

```python
import functools

import jax
import jax.numpy as jnp
from jax import lax
from jax.experimental import pallas as pl
from jax.experimental.pallas import tpu as pltpu
from jax.sharding import PartitionSpec as P

HD = 64
F = 2 * HD
PAIR = 2 * HD
SUB = 256
WIRE = F + 16
EPSILON = 1e-05
AXES = ("batch", "seq")
LIMIT = 28
LIMITS = {"mlp": 56, "attention": 32, "middle_back": 40, "local_back": 40, "middle": 40, "input_back": 32}
SUMS = {
    group + part
    for group in ("mlp", "query", "key")
    for part in ("_first_sum", "_middle_sum", "_second_sum")
}
FREE_INS = SUMS | {"place_first", "unpack", "keys", "queries", "input_back"}
PACE = 0.01
bf16 = jnp.bfloat16
f32 = jnp.float32


def dot(a, b, left, right):
    return lax.dot_general(a, b, (((left,), (right,)), ((), ())), preferred_element_type=f32)


def nn(a, b):
    return dot(a, b, 1, 0)


def nt(a, b):
    return dot(a, b, 1, 1)


def tn(a, b):
    return dot(a, b, 0, 0)


def lane(shape):
    return lax.broadcasted_iota(jnp.int32, shape, len(shape) - 1)


def sublane(shape):
    return lax.broadcasted_iota(jnp.int32, shape, len(shape) - 2)


def normalize(values):
    center = jnp.mean(values, axis=-1, keepdims=True)
    centered = values - center
    spread = jnp.mean(centered * centered, axis=-1, keepdims=True)
    scale = lax.rsqrt(spread + EPSILON)
    return centered * scale, scale


def normalize_back(upstream, xhat, scale, gain):
    entry = upstream * gain
    first = jnp.mean(entry, axis=-1, keepdims=True)
    second = jnp.mean(entry * xhat, axis=-1, keepdims=True)
    return scale * (entry - first - xhat * second)


def map_weight(rows, keys):
    rows = rows.astype(f32)
    turned = pltpu.roll(rows, HD, 1)
    low = lane(rows.shape) < HD
    signed = jnp.where(low, turned, -rows) if keys else jnp.where(low, rows, -turned)
    top = sublane(rows.shape) < HD
    return jnp.concatenate(
        [jnp.where(top, signed, 0.0), jnp.where(top, 0.0, signed)], axis=1
    ).astype(bf16)


def segment_ones(width):
    shape = (width, width)
    return (lane(shape) // HD == sublane(shape) // HD).astype(bf16)


def segment_sum(values, ones):
    high = values.astype(bf16)
    low = (values - high.astype(f32)).astype(bf16)
    return nn(high, ones) + nn(low, ones)


def features(logits, ones):
    parts = []
    for at in range(0, logits.shape[1], F):
        part = logits[:, at : at + F]
        low = lane(part.shape) < HD
        first = jnp.max(jnp.where(low, part, -jnp.inf), axis=1, keepdims=True)
        second = jnp.max(jnp.where(low, -jnp.inf, part), axis=1, keepdims=True)
        parts.append(jnp.exp(part - jnp.where(low, first, second)))
    powers = jnp.concatenate(parts, axis=1)
    return powers / nn(powers.astype(bf16), ones)


def features_back(phi, upstream, ones):
    phi = phi.astype(f32)
    return phi * (upstream - segment_sum(phi * upstream, ones))


def split_of(ids, lens, row, count):
    first = ids[1] * count
    start, split = 0, count
    for n in range(lens.shape[1]):
        inside = (start >= first) & (start < first + count)
        split = jnp.where(inside, start - first, split)
        start = start + lens[row, n]
    return split


def starts_within(lens, row, low, high):
    start, found = 0, 0
    for n in range(lens.shape[1]):
        found = found | jnp.where((start >= low) & (start < high), 1, 0)
        start = start + lens[row, n]
    return found == 1


def matrix(ref):
    value = ref[...]
    return value if value.ndim == 2 else value.reshape(-1, value.shape[-1])


def with_aux(pair, head, aux):
    own = (lane(pair.shape) < HD) if head == 0 else (lane(pair.shape) >= HD)
    return jnp.where(own, pair, aux)


def pair_rows(first, second):
    top = sublane(first.shape) < HD
    return jnp.where(top, first, second)


def put_wire(ref, at, first, second, aux_rows):
    ref[0, at, 0:F, :] = pair_rows(first, second).astype(bf16)
    sums = [sum(x[a : a + 1] for a in rows) for x, rows in zip((first, second), aux_rows)]
    row = sublane((16, F))
    ref[0, at, F:WIRE, :] = jnp.where(
        row == 0, sums[0], jnp.where(row == 1, sums[1], 0.0)
    ).astype(bf16)


def arrived(refs, at):
    half = len(refs) // 2
    return sum(
        reach[0, 0] * wire[0, at].astype(f32) for wire, reach in zip(refs[:half], refs[half:])
    ).astype(bf16)


def take_wire(both):
    state, sums = both[0:F], both[F:WIRE]
    top = sublane(state.shape) < HD
    return jnp.where(top, state, sums[0:1]), jnp.where(top, sums[1:2], state)


def block_masks(split, count, flipped):
    masks = []
    for first in range(0, count, SUB):
        if flipped:
            shape = (SUB, count - first)
            i, j = lane(shape) + first, sublane(shape) + first
        else:
            shape = (SUB, first + SUB)
            i, j = sublane(shape) + first, lane(shape)
        masks.append(((i < split) | (j >= split)) & (j <= i))
    return masks


def masked(scores, mask):
    return jnp.where(mask, scores, 0.0).astype(bf16)


def keys_kernel(
    ids, lens, tok, gain, shift, wk, wv, ok, ov, maps, normed_o, turned_o, k_o, v_o, phi_o, wire_o, kept
):
    row, quad = pl.program_id(0), pl.program_id(1)

    @pl.when(quad == 0)
    def _():
        xhat, _ = normalize(tok[...].astype(f32))
        normed = (xhat * gain[...] + shift[...]).astype(bf16)
        kept[...] = normed
        normed_o[...] = normed
        turned_o[...] = normed.T

    normed = kept[...]
    keys = (nn(normed, wk[...]) + ok[...]).astype(bf16)
    values = (nn(normed, wv[...]) + ov[...]).astype(bf16)
    k_o[...] = keys
    v_o[...] = values
    count = keys.shape[0]
    split = split_of(ids, lens, row, count)
    begin = jnp.where(split < count, split, 0)
    last = sublane((count, PAIR)) >= begin
    ones = segment_ones(2 * F)
    cuts = [slice(p * PAIR, (p + 1) * PAIR) for p in range(2)]
    logits = [nn(keys[:, at], map_weight(maps[at, :], True)) for at in cuts]
    phis = [features(part, ones).astype(bf16) for part in logits]
    for p, at in enumerate(cuts):
        phi_o[:, 2 * p * F : 2 * (p + 1) * F] = phis[p]
    for p, at in enumerate(cuts):
        pair = values[:, at].astype(f32)
        sums = [
            tn(
                jnp.where(last, with_aux(pair, h, 1.0), 0.0).astype(bf16),
                phis[p][:, h * F : (h + 1) * F],
            )
            for h in range(2)
        ]
        put_wire(wire_o, p, sums[0], sums[1], ((HD,), (0,)))


def queries_kernel(normed, wq, oq, maps, q_o, phi_o):
    queries = (nn(normed[...], wq[...]) + oq[...]).astype(bf16)
    q_o[...] = queries
    ones = segment_ones(2 * F)
    cuts = [slice(p * PAIR, (p + 1) * PAIR) for p in range(2)]
    logits = [nn(queries[:, at], map_weight(maps[at, :], False)) for at in cuts]
    for p, part in enumerate(logits):
        phi_o[:, 2 * p * F : 2 * (p + 1) * F] = features(part, ones).astype(bf16)


def attention_kernel(ids, lens, phi_query, phi_key, val, num_o):
    count = val.shape[0]
    split = split_of(ids, lens, pl.program_id(0), count)
    masks = block_masks(split, count, False)
    columns = [slice(h * F, (h + 1) * F) for h in range(4)]
    blocks = [slice(first, first + SUB) for first in range(0, count, SUB)]
    scores = [
        [
            masked(nt(phi_query[rows, at], phi_key[: rows.stop, at]), mask)
            for rows, mask in zip(blocks, masks)
        ]
        for at in columns
    ]
    for h, at in enumerate(columns):
        pair = val[:, h // 2 * PAIR : (h // 2 + 1) * PAIR].astype(f32)
        extended = with_aux(pair, h % 2, 1.0).astype(bf16)
        for rows, part in zip(blocks, scores[h]):
            num_o[rows, at] = nn(part, extended[: rows.stop])


def middle_kernel(
    states, ids, lens, num, phi_query, tok, wo, bias, gain, shift, *rest
):
    wires, (att_o, rden_o, mid_o, normed_o) = rest[: 2 * states], rest[2 * states :]
    count = num.shape[0]
    carry = sublane((count, F)) < split_of(ids, lens, pl.program_id(0), count)
    low = lane((count, PAIR)) < HD
    for p in range(wires[0].shape[1]):
        sums = []
        for h, memory in enumerate(take_wire(arrived(wires, p))):
            column = slice((2 * p + h) * F, (2 * p + h + 1) * F)
            sums.append(
                num[:, column] + jnp.where(carry, nt(phi_query[:, column], memory), 0.0)
            )
        numerator = jnp.where(low, sums[0], sums[1])
        denominator = pltpu.roll(jnp.where(low, sums[1], sums[0]), HD, 1)
        inverse = 1.0 / denominator
        at = slice(p * PAIR, (p + 1) * PAIR)
        rden_o[:, at] = inverse.astype(bf16)
        att_o[:, at] = (numerator * inverse).astype(bf16)
    middle = tok[...].astype(f32) + nn(att_o[...], matrix(wo)) + bias[...]
    mid_o[...] = middle
    xhat, _ = normalize(middle)
    normed_o[...] = (xhat * gain[...] + shift[...]).astype(bf16)


def put_halves(refs, value, core, at):
    if len(refs) == 1:
        refs[0][:, at] = value
        return
    mine_o, other_o = refs
    chips, rows, _ = mine_o.shape
    parted = value.reshape(chips, 2, rows, value.shape[1])
    even, odd = parted[:, 0], parted[:, 1]
    first = core == 0
    mine_o[:, :, at] = jnp.where(first, even, odd).astype(bf16)
    other_o[:, :, at] = jnp.where(first, odd, even).astype(bf16)


def mlp_kernel(plain, ids, lens, normed, cot, ex, sh, bias, branch, mid, *rest):
    out_o, back_o, bg_o, *grads, turned, y_s, back_s, mid_s, sem = rest
    step = pl.program_id(0)
    copy = pltpu.make_async_copy(mid, mid_s, sem)

    @pl.when(step == 0)
    def _():
        copy.start()
        turned[...] = normed[...].T
        y_s[...] = jnp.zeros_like(y_s)
        back_s[...] = jnp.zeros_like(back_s)

    expand, shrink = matrix(ex), matrix(sh)
    pre = nn(normed[...], expand) + bias[...]
    square = pre * pre
    slope, cubic = 0.7978845608028654, 0.044715
    half = 0.5 * jnp.tanh(pre * (slope + slope * cubic * square)) + 0.5
    raised = pre * half
    hidden = raised.astype(bf16)
    rise = half + raised * (1.0 - half) * (2.0 * slope + 6.0 * slope * cubic * square)
    back = (nt(cot[...], shrink) * rise).astype(bf16)
    bg_o[...] = jnp.sum(back.astype(f32), axis=0, keepdims=True)
    y_s[...] += nn(hidden, shrink)
    back_s[...] += nt(back, expand)

    @pl.when(step == pl.num_programs(0) - 1)
    def _():
        copy.wait()
        out_o[...] = (mid_s[...] + y_s[...] + branch[...]).astype(bf16)
        back_o[...] = back_s[...].astype(bf16)

    shrink_grad = tn(hidden, cot[...])
    expand_grad = nn(turned[...], back)
    if plain:
        eg_o, sg_o = grads
        sg_o[...] = shrink_grad
        eg_o[...] = expand_grad
        return
    em_o, eo_o, sm_o, so_o = grads
    core = ids[1] % 2
    first = core == 0
    put_halves((em_o, eo_o), expand_grad, core, slice(None))
    chips, rows, lanes = sm_o.shape
    width = shrink_grad.shape[1]
    subs = lanes // width
    parted = shrink_grad.reshape(chips, 2, subs, rows, width)
    for sub in range(subs):
        even, odd = parted[:, 0, sub], parted[:, 1, sub]
        at = slice(sub * width, (sub + 1) * width)
        sm_o[:, :, at] = jnp.where(first, even, odd).astype(bf16)
        so_o[:, :, at] = jnp.where(first, odd, even).astype(bf16)


def column_sum(values):
    return jnp.sum(values, axis=0, keepdims=True)


def middle_back_kernel(
    parts,
    ids,
    lens,
    mid,
    back,
    cot,
    att,
    rden,
    phi_query,
    wo,
    gain,
    mb_o,
    ext_o,
    wire_o,
    small_o,
    *rest,
):
    *og_refs, og_s, sums_s = rest
    step = pl.program_id(0)
    row, part = step // parts, lax.rem(step, parts)

    @pl.when(step == 0)
    def _():
        og_s[...] = jnp.zeros_like(og_s)
        small_o[...] = jnp.zeros_like(small_o)

    middle = mid[...]
    upstream = cot[...].astype(f32)
    xhat, scale = normalize(middle)
    from_norm = back[...].astype(f32)
    middle_back = upstream + normalize_back(from_norm, xhat, scale, gain[...])
    branch_back = middle_back.astype(bf16)
    mb_o[...] = branch_back
    small_o[0:1, :] += column_sum(from_norm * xhat)
    small_o[1:2, :] += column_sum(from_norm)
    small_o[2:3, :] += column_sum(branch_back.astype(f32))
    small_o[3:4, :] += column_sum(upstream)
    og_s[...] += tn(att[...], branch_back)

    @pl.when(step == pl.num_programs(0) - 1)
    def _():
        put_halves(og_refs, og_s[...], ids[1] % 2, slice(None))

    attended_back = nt(branch_back, matrix(wo))
    count = middle.shape[0]
    carry = sublane((count, F)) < split_of(ids, lens, row, count * parts) - part * count
    ones = segment_ones(PAIR)
    spot = lane((count, PAIR))
    for p in range(wire_o.shape[1]):
        at = slice(p * PAIR, (p + 1) * PAIR)
        given = attended_back[:, at]
        inverse = rden[:, at].astype(f32)
        numerator_back = given * inverse
        denominator_back = -segment_sum(given * att[:, at].astype(f32), ones) * inverse
        aux = pltpu.roll(denominator_back, HD, 1)
        high = aux.astype(bf16).astype(f32)
        rest = aux - high
        for h in range(2):
            first = HD if h == 0 else 0
            extended = with_aux(
                numerator_back,
                h,
                jnp.where(spot == first, high, jnp.where(spot == first + 1, rest, 0.0)),
            ).astype(bf16)
            column = slice((2 * p + h) * F, (2 * p + h + 1) * F)
            ext_o[:, column] = extended
            query = jnp.where(carry, phi_query[:, column].astype(f32), 0.0).astype(bf16)
            total = tn(extended, query)
            sums_s[2 * p + h] = jnp.where(part == 0, total, sums_s[2 * p + h] + total)

    @pl.when(part == parts - 1)
    def _():
        for p in range(wire_o.shape[1]):
            put_wire(wire_o, p, sums_s[2 * p], sums_s[2 * p + 1], ((HD, HD + 1), (0, 1)))


def map_gradient(pair, logits_back):
    both = tn(pair, logits_back)
    rows = pair_rows(both[:, :F], both[:, F:])
    return rows - pltpu.roll(rows, HD, 1)


def add_by_row(out, row, value):
    @pl.when(row == 0)
    def _():
        out[...] = value

    @pl.when(row > 0)
    def _():
        out[...] += value


def local_back_kernel(
    first, states, ids, lens, phi_query, phi_key, val, ext, queries, maps, *rest
):
    wires, (pq_o, kg_o, vg_o, mg_o) = rest[: 2 * states], rest[2 * states :]
    row = pl.program_id(1) + first
    count = val.shape[0]
    split = split_of(ids, lens, row, count)
    flipped = block_masks(split, count, True)
    carry = sublane((count, F)) < split
    ones = segment_ones(2 * F)
    columns = [slice(h * F, (h + 1) * F) for h in range(4)]
    cuts = [slice(p * PAIR, (p + 1) * PAIR) for p in range(2)]
    pairs = [val[:, at].astype(f32) for at in cuts]
    extended = [with_aux(pairs[h // 2], h % 2, 1.0).astype(bf16) for h in range(4)]
    memories = [memory for p in range(2) for memory in take_wire(arrived(wires, p))]
    grads = [
        jnp.where(carry, nn(ext[:, columns[h]], memories[h]), 0.0) for h in range(4)
    ]
    blocks = [slice(first, first + SUB) for first in range(0, count, SUB)]
    heads, tops = [], []
    for h, at in enumerate(columns):
        back, scores = [], []
        for rows, mask in zip(blocks, flipped):
            on = slice(rows.start, count)
            back.append(masked(nt(extended[h][rows], ext[on, at]), mask))
            scores.append(masked(nt(phi_key[rows, at], phi_query[on, at]), mask))
        heads.append((back, scores))
    for h, at in enumerate(columns):
        back, scores = heads[h]
        value_parts = []
        for rows, given, score in zip(blocks, back, scores):
            on = slice(rows.start, count)
            kg_o[rows, at] = nn(given, phi_query[on, at]).astype(bf16)
            value_parts.append(nn(score, ext[on, at]))
        tops.append(jnp.concatenate(value_parts, axis=0))
        query_parts = []
        for i, rows in enumerate(blocks):
            part = [
                tn(given[:, rows.start - on.start : rows.stop - on.start], phi_key[on, at])
                for given, on in zip(back[: i + 1], blocks)
            ]
            query_parts.append(sum(part[1:], part[0]))
        grads[h] = grads[h] + jnp.concatenate(query_parts, axis=0)
    low = lane((count, PAIR)) < HD
    for p, at in enumerate(cuts):
        vg_o[:, at] = jnp.where(low, tops[2 * p], tops[2 * p + 1]).astype(bf16)
    logits_back = [
        features_back(
            phi_query[:, 2 * p * F : 2 * (p + 1) * F],
            jnp.concatenate(grads[2 * p : 2 * p + 2], axis=1),
            ones,
        ).astype(bf16)
        for p in range(2)
    ]
    for p, at in enumerate(cuts):
        pq_o[:, at] = nt(logits_back[p], map_weight(maps[at, :], False)).astype(bf16)
    gradient = [map_gradient(queries[:, at], logits_back[p]) for p, at in enumerate(cuts)]
    gradient = jnp.concatenate(gradient, axis=0)
    mg_o[...] = jnp.where(lane(gradient.shape) < HD, gradient, 0.0)


def keys_back_kernel(
    first, states, ids, lens, kg, vg, phi_key, val, keys, maps, *rest
):
    wires = rest[: 2 * states]
    *from_before, pk_o, pv_o, mg_o = rest[2 * states :]
    row = pl.program_id(1) + first
    count = val.shape[0]
    split = split_of(ids, lens, row, count)
    begin = jnp.where(split < count, split, 0)
    last = sublane((count, F)) >= begin
    low = lane((count, PAIR)) < HD
    ones = segment_ones(2 * F)
    cuts = [slice(p * PAIR, (p + 1) * PAIR) for p in range(2)]
    logits_back = []
    for p, at in enumerate(cuts):
        pair = val[:, at].astype(f32)
        both = arrived(wires, p)
        state = both[0:F]
        spot = sublane(state.shape)
        grads, tops = [], []
        for h, memory in enumerate(take_wire(both)):
            column = slice((2 * p + h) * F, (2 * p + h + 1) * F)
            first = HD if h == 0 else 0
            own = (spot < HD) if h == 0 else (spot >= HD)
            memory = jnp.where(own | (spot == first), memory.astype(f32), 0.0).astype(bf16)
            extended = with_aux(pair, h, 1.0).astype(bf16)
            grads.append(kg[:, column].astype(f32) + jnp.where(last, nn(extended, memory), 0.0))
            tops.append(nt(phi_key[:, column], state))
        pv_o[:, at] = (
            vg[:, at].astype(f32) + jnp.where(last, jnp.where(low, tops[0], tops[1]), 0.0)
        ).astype(bf16)
        at = slice(2 * p * F, 2 * (p + 1) * F)
        logits_back.append(
            features_back(phi_key[:, at], jnp.concatenate(grads, axis=1), ones).astype(bf16)
        )
    for p, at in enumerate(cuts):
        pk_o[:, at] = nt(logits_back[p], map_weight(maps[at, :], True)).astype(bf16)
    gradient = jnp.concatenate(
        [
            pltpu.roll(map_gradient(keys[:, at], logits_back[p]), HD, 1)
            for p, at in enumerate(cuts)
        ],
        axis=0,
    )
    before = sum(part[...] for part in from_before)
    mg_o[...] = before + jnp.where(lane(gradient.shape) < HD, 0.0, gradient)


def weight_back_kernel(ids, lens, turned, pb, *refs):
    put_halves(refs, nn(turned[...], pb[...]), ids[1] % 2, slice(None))


def key_weight_back_kernel(
    steps, devices, ids, lens, turned, pk, small_in, small_mid, hid, maps, *rest
):
    *refs, lines = rest
    step = pl.program_id(0)
    core = ids[1] % 2

    @pl.when(step < steps)
    def _():
        put_halves(refs, nn(turned[...], pk[...]), core, slice(None))

    if devices:

        @pl.when(step == steps)
        def _():
            pack(devices, core, small_in, small_mid, hid, maps, *refs, lines)


def input_back_kernel(pq, pk, pv, wq, wk, wv, tok, mb, gain, out_o, small_o):
    @pl.when(pl.program_id(0) == 0)
    def _():
        small_o[...] = jnp.zeros_like(small_o)

    from_norm = nt(pq[...], wq[...]) + nt(pk[...], wk[...]) + nt(pv[...], wv[...])
    xhat, scale = normalize(tok[...].astype(f32))
    small_o[0:1, :] += column_sum(from_norm * xhat)
    small_o[1:2, :] += column_sum(from_norm)
    for i, part in enumerate((pq, pk, pv)):
        small_o[2 + i : 3 + i, :] += column_sum(part[...].astype(f32))
    out_o[...] = (mb[...].astype(f32) + normalize_back(from_norm, xhat, scale, gain[...])).astype(bf16)


def spec(shape, index):
    return pl.BlockSpec(memory_space=pl.ANY) if shape is None else pl.BlockSpec(shape, index)


def estimate(micros):
    return pl.CostEstimate(
        flops=int(micros * PACE * 1e9), bytes_accessed=int(micros * PACE * 1e6), transcendentals=0
    )


MARKS = {}


def mark_of(array):
    return MARKS[id(array)][1] if id(array) in MARKS else array


def call(kernel, grid, ins, outs, scratch=(), scalars=0, name=None, micros=10, waits=(), into=()):
    waits = [mark_of(array) for array in waits]
    arrays = [entry[0] for entry in ins[scalars:]]
    if name not in FREE_INS:
        arrays = [pltpu.with_memory_space_constraint(array, pltpu.HBM) for array in arrays]
    arrays += [pltpu.with_memory_space_constraint(array, pltpu.HBM) for array in waits]
    arrays += into
    fetched = [entry[0] for entry in ins[:scalars]]
    read, given = len(ins), len(ins) + len(waits) + len(into)

    def body(*refs):
        refs[given + len(outs)][...] = jnp.zeros((8, F), f32)
        kernel(*refs[:read], *refs[given : given + len(outs)], *refs[given + len(outs) + 1 :])

    def shaped(shape, kind, block, index, free=False):
        return (jax.ShapeDtypeStruct if free else pltpu.HBM)(shape, kind)

    *results, mark = pl.pallas_call(
        body,
        out_shape=[shaped(*out) for out in outs] + [pltpu.HBM((8, F), f32)],
        grid_spec=pltpu.PrefetchScalarGridSpec(
            num_scalar_prefetch=scalars,
            grid=grid,
            in_specs=[spec(block, index) for _, block, index in ins[scalars:]]
            + [pl.BlockSpec(memory_space=pl.ANY)] * (given - read),
            out_specs=[spec(*out[2:4]) for out in outs]
            + [spec((8, F), lambda *i: (0, 0))],
            scratch_shapes=list(scratch),
        ),
        compiler_params=pltpu.CompilerParams(
            vmem_limit_bytes=LIMITS.get(name, LIMIT) * 1024 * 1024
        ),
        cost_estimate=estimate(micros),
        input_output_aliases={given - len(into) + i: i for i in range(len(into))},
        name=name,
    )(*fetched, *arrays)
    MARKS.update((id(result), (result, mark)) for result in results)
    return results


def tie_kernel(*refs):
    del refs


def tie(values, *waits):
    anywhere = pl.BlockSpec(memory_space=pl.ANY)
    count = len(values)
    waits = [mark_of(array) for array in waits]
    return pl.pallas_call(
        tie_kernel,
        out_shape=[jax.ShapeDtypeStruct(v.shape, v.dtype) for v in values],
        in_specs=[anywhere] * (count + len(waits)),
        out_specs=[anywhere] * count,
        input_output_aliases={i: i for i in range(count)},
        cost_estimate=estimate(0.5),
        name="tie",
    )(*values, *waits)


def gather_rows(part):
    return lax.all_gather(part, AXES, axis=0, tiled=True)


def scatter_rows(whole):
    return lax.psum_scatter(whole, AXES, scatter_dimension=0, tiled=True)


def scatter_columns(rows):
    return lax.psum_scatter(rows, AXES, scatter_dimension=1, tiled=True)


def swap(array, mask, axis="seq", name="swap"):
    size = lax.axis_size(axis)
    with jax.named_scope(name):
        return lax.ppermute(array, axis, [(i, i ^ mask) for i in range(size)])


def gather_cores(pieces, name):
    return pieces + [swap(piece, 1, name=name) for piece in pieces]


def put_piece(cuts, outs, at, piece):
    for out, first, last, sub in cuts:
        if sub is None:
            outs[out][at] = piece[:, first:last]
        else:
            outs[out][at, sub] = piece[:, first:last]


def place_kernel(cuts, ids, *refs):
    pieces, outs = refs[:8], refs[8:]

    def put(at, chips):
        for core in range(2):
            for piece, pair in zip(pieces[4 * core + at : 4 * core + at + 2], chips):
                for r, chip in enumerate(pair):
                    put_piece(cuts, outs, ids[1] ^ (2 * chip + core), piece[r, 0])

    @pl.when(pl.program_id(0) < 2)
    def _():
        put(0, ((0, 1), (2, 3)))

    @pl.when(pl.program_id(0) >= 2)
    def _():
        put(2, ((0, 2), (1, 3)))


def place(pieces, ids, cuts, shapes, name, micros, waits=()):
    rows, wide = pieces[0].shape[-2:]
    near = lambda s: jnp.minimum(s, 1)
    far = lambda s: jnp.maximum(s - 2, 0)
    ins = [
        (p.reshape(2, 2, rows, wide), (2, 1, rows, wide), lambda s, ids, at=at: (0, at(s), 0, 0))
        for p, at in zip(pieces, (near, near, far, far) * 2)
    ]

    def target(shape):
        return lambda s, ids: (ids[0] ^ s,) + (0,) * len(shape)

    return call(
        functools.partial(place_kernel, cuts),
        (4,),
        [(ids, None, None)] + ins,
        [((32, *shape), bf16, (8, *shape), target(shape), True) for shape in shapes],
        [],
        1,
        name,
        micros,
        waits,
    )


def first_sum_kernel(parts, ids, *refs):
    ins, (near_keep, near_send, far_keep, far_send) = refs[: parts * 8], refs[parts * 8 :]
    step = pl.program_id(0)

    def put(targets):
        at = 0
        for part in range(parts):
            wide = ins[part * 8].shape[-1]
            for r, (out, i) in enumerate(targets):
                mine, got = ins[(part * 4 + r) * 2 : (part * 4 + r) * 2 + 2]
                total = mine[0, 0].astype(f32) + got[0, 0].astype(f32)
                out[i, 0, :, at : at + wide] = total.astype(bf16)
            at += wide

    @pl.when(step < 2)
    def _():
        put(((near_keep, 0), (near_send, 0), (near_keep, 1), (near_send, 1)))

    @pl.when(step >= 2)
    def _():
        put(((far_keep, 0), (far_keep, 1), (far_send, 0), (far_send, 1)))


def first_sum(mines, gots, ids, name, micros=4, waits=()):
    rows = mines[0].shape[-2]
    wides = [m.shape[-1] for m in mines]
    ins = [(ids, None, None)]

    def index(r):
        return lambda k, ids: (ids[0] ^ k, (ids[1] // 2) ^ r, 0, 0)

    for mine, got, wide in zip(mines, gots, wides):
        for r in range(4):
            for array in (mine, got):
                ins.append((array.reshape(4, 4, rows, wide), (1, 1, rows, wide), index(r)))
    total, last = sum(wides), name[0] in "kq"
    near = lambda k, ids: (0, jnp.minimum(k, 1), 0, 0)
    far = lambda k, ids: (0, jnp.maximum(k - 2, 0), 0, 0)
    return call(
        functools.partial(first_sum_kernel, len(mines)),
        (4,),
        ins,
        [
            ((2, 2, rows, total), bf16, (2, 1, rows, total), at, free)
            for at, free in ((near, last), (near, name[0] != "m"), (far, last), (far, True))
        ],
        [],
        1,
        name,
        micros,
        waits,
    )


def middle_sum_kernel(near_keep, near_got, far_keep, far_got, *outs):
    for at, (kept, got) in enumerate(((near_keep, near_got), (far_keep, far_got))):
        for i in range(2):
            total = kept[i].astype(f32) + got[i].astype(f32)
            outs[2 * at + i][...] = total.astype(bf16)


def middle_sum(sums, name, micros=3, waits=()):
    near_keep, near_send, far_keep, far_send = sums
    pieces = [near_keep, swap(near_send, 2, name=name + "_x1")]
    pieces += [far_keep, swap(far_send, 4, name=name + "_y1")]
    _, _, rows, wide = near_keep.shape
    tile = 1536 if wide % 1536 == 0 else wide
    near_keep, near_send, far_keep, far_send = call(
        middle_sum_kernel,
        (wide // tile,),
        [(p, (2, 2, rows, tile), lambda g: (0, 0, 0, g)) for p in pieces],
        [
            ((2, rows, wide), bf16, (2, rows, tile), lambda g: (0, 0, g), free)
            for free in (name[0] in "kq", True) * 2
        ],
        [],
        0,
        name,
        micros,
        waits,
    )
    near_got, far_got = swap(near_send, 4, name=name + "_y2"), swap(far_send, 2, name=name + "_x2")
    return [near_keep, near_got, far_keep, far_got]


def second_sum_kernel(direct, near, near_got, far, far_got, *outs):
    for k in range(4):
        kept, got = (near, near_got) if k < 2 else (far, far_got)
        total = kept[k % 2].astype(f32) + got[k % 2].astype(f32)
        if direct:
            outs[k][...] = total.astype(outs[k].dtype)
        else:
            outs[k % 2][k // 2] = total.astype(outs[k % 2].dtype)


def second_sum(pieces, name, micros=3, waits=(), direct=True):
    _, rows, wide = pieces[0].shape
    tile = 1536 if wide % 1536 == 0 else wide
    if direct:
        shape, cut = (rows, wide), (rows, tile)
        outs = [(shape, bf16 if k else f32, cut, lambda g: (0, g), k > 0) for k in range(4)]
    else:
        shape, cut = (2, rows, wide), (2, rows, tile)
        outs = [(shape, bf16 if k else f32, cut, lambda g: (0, 0, g), k > 0) for k in range(2)]
    return call(
        functools.partial(second_sum_kernel, direct),
        (wide // tile,),
        [(p, (2, rows, tile), lambda g: (0, 0, g)) for p in pieces],
        outs,
        [],
        0,
        name,
        micros,
        waits,
    )


def reduce_batch(sums, name):
    got = [swap(sums[k], k, "batch", name + "_layer") for k in range(1, 4)]
    return sums[0] + sum(part.astype(f32) for part in got)


def reduce_layer1(sums, name, waits):
    (kept,) = tie(sums[:1], *waits)
    return kept + swap(sums[1], 1, "batch", name + "_layer1").astype(f32)


def reduce_layer2(pair, name, waits):
    got = swap(pair[1].astype(bf16), 2, "batch", name + "_layer2")
    (kept,) = tie([pair[0]], *waits)
    return kept + got.astype(f32)


def spots(length, each, owners):
    at = lane((F, length))
    owner = ((at.astype(f32) + 0.5) * (1.0 / each)).astype(jnp.int32)
    inside = (at - owner * each == sublane((F, length))).astype(bf16)
    at = lane((owners.shape[0], length))
    owner = ((at.astype(f32) + 0.5) * (1.0 / each)).astype(jnp.int32)
    return inside, owner == owners


def unpack_kernel(devices, block, *outs):
    rows = block.shape[0] // devices
    vectors = [(out, i) for out in outs for i in range(out.shape[0])]
    count = len(vectors)
    place_at = lane((count * devices, block.shape[0]))
    line = sublane((count * devices, block.shape[0]))
    vector = ((line.astype(f32) + 0.5) * (1.0 / devices)).astype(jnp.int32)
    picked = nn(
        (place_at == (line - vector * devices) * rows + vector).astype(bf16), block[...]
    ).astype(bf16)
    for j, (out, i) in enumerate(vectors):
        length = out.shape[1]
        owners = sublane((devices, length))
        inside, owned = spots(length, length // devices, owners)
        spread = nn(picked[j * devices : (j + 1) * devices], inside)
        out[i : i + 1, :] = column_sum(jnp.where(owned, spread, 0.0))


def shards_kernel(
    gain, shift, mix, offset, maps, out, branch, ex, hid, sh, first_o, rest_o, small
):
    rows = mix.shape[0]
    small[...] = jnp.zeros_like(small)
    for j, part in enumerate((gain, shift, branch)):
        small[2 * j : 2 * j + 2, 0:rows] = part[...].astype(f32)
    small[6:7, 0 : 3 * rows] = offset[...].astype(f32)
    small[7:8, 0 : 4 * rows] = hid[...].astype(f32)
    wide, width = mix.shape[1], sh.shape[1]
    first_o[:, 0:wide] = mix[...]
    first_o[:, wide : wide + F] = maps[...]
    first_o[:, wide + F : wide + 2 * F] = small[...].astype(bf16)
    for i in range(4):
        rest_o[i] = ex[:, i * width : (i + 1) * width]
        rest_o[4 + i] = sh[i * rows : (i + 1) * rows, :].astype(f32).astype(bf16)
    rest_o[8] = out[...]


def pack(devices, core, small_in, small_mid, hid, maps, mine_o, other_o, lines):
    offset = jnp.concatenate([small_in[i : i + 1, :] for i in range(2, 5)], axis=1)
    lines[...] = jnp.zeros_like(lines)
    vectors = [
        small_in[0:1, :],
        small_mid[0:1, :],
        small_in[1:2, :],
        small_mid[1:2, :],
        small_mid[2:3, :],
        small_mid[3:4, :],
        offset,
        hid[...],
    ]
    half = devices // 2
    for j, vector in enumerate(vectors):
        length = vector.shape[1]
        line = sublane((devices, length))
        owners = jnp.where(line < half, 2 * line + core, 2 * (line - half) + 1 - core)
        inside, owned = spots(length, length // devices, owners)
        share = jnp.where(owned, vector, 0.0).astype(bf16)
        lines[:, j, :] = nt(share, inside)
    put_halves((mine_o, other_o), maps[...], core, slice(0, F))
    mine_o[:, :, F:] = lines[:half].astype(bf16)
    other_o[:, :, F:] = lines[half:].astype(bf16)


def flags_kernel(levels, count, ids, lens, *outs):
    mine = ids[1]
    for row in range(lens.shape[0]):
        flags = []
        for reverse in (False, True):
            for level in range(levels):
                span = 1 << level
                begin = mine - lax.rem(mine, span)
                upper = lax.rem(mine // span, 2) == 1
                own_closed = starts_within(lens, row, begin * count, (begin + span) * count)
                if reverse:
                    receives = jnp.logical_not(upper)
                    closed = starts_within(lens, row, (mine + 1) * count, (begin + span) * count)
                    other = starts_within(lens, row, (begin - span) * count, begin * count)
                else:
                    receives = upper
                    closed = starts_within(lens, row, begin * count, mine * count)
                    other = starts_within(
                        lens, row, (begin + span) * count, (begin + 2 * span) * count
                    )
                flags.append(receives & jnp.logical_not(closed))
                flags.append(receives | jnp.logical_not(other))
                flags.append(jnp.logical_not(receives & own_closed))
        for out, flag in zip(outs, flags):
            out[row] = jnp.full((1, 1, F), jnp.where(flag, 1.0, 0.0), f32)


def carry(total, came, flags, level, reverse, waits=()):
    levels = len(flags) // 6
    at = 3 * (level + (levels if reverse else 0))
    reaches, keeps, joins = flags[at : at + 3]
    other = swap(total, 1 << level, name=f"state{level}")
    came = came + [(other, reaches)]
    if level == levels - 1:
        return None, came
    if len(waits):
        keeps, joins = tie([keeps, joins], *waits)
    return (keeps * total.astype(f32) + joins * other.astype(f32)).astype(bf16), came


def local(
    tokens,
    sequence_lengths,
    norm_gains,
    norm_shifts,
    mixing_weight,
    mixing_offset,
    feature_maps,
    output_weight,
    branch_offsets,
    expand_weight,
    hidden_offset,
    shrink_weight,
    cotangent,
):
    MARKS.clear()
    row_count, tok_count, width = tokens.shape
    count = row_count * tok_count
    heads = width // HD
    pairs, quads = heads // 2, heads // 4
    quad = 2 * PAIR
    hidden_width = expand_weight.shape[1]
    batch, size = lax.axis_size("batch"), lax.axis_size("seq")
    devices = batch * size
    share = width // devices
    plain = size != 8 or batch != 4 or share % 8 != 0 or hidden_width != 4 * width or 4 * share > F

    mine = lax.axis_index("seq").astype(jnp.int32)
    ids = jnp.stack([lax.axis_index("batch").astype(jnp.int32), mine])
    lens = sequence_lengths
    scalars = [(ids, None, None), (lens, None, None)]
    levels = size.bit_length() - 1
    flag = (row_count, 1, 1, F)
    flags = call(
        functools.partial(flags_kernel, levels, tok_count),
        (1,),
        scalars,
        [(flag, f32, flag, lambda i, *s: (0, 0, 0, 0))] * (6 * levels),
        [],
        2,
        "flags",
        1,
    )

    if plain:
        gains = lax.all_gather(norm_gains, AXES, axis=1, tiled=True).astype(f32)[:, None]
        shifts = lax.all_gather(norm_shifts, AXES, axis=1, tiled=True).astype(f32)[:, None]
        branches = lax.all_gather(branch_offsets, AXES, axis=1, tiled=True).astype(f32)[:, None]
        offset = gather_rows(mixing_offset).astype(f32)[None]
        hidden_bias = gather_rows(hidden_offset).astype(f32)[None]
        first_weight = jnp.concatenate(
            [gather_rows(mixing_weight), gather_rows(feature_maps)], axis=1
        )
        out_weight = gather_rows(output_weight)
        expand = gather_rows(expand_weight)
        shrink = gather_rows(shrink_weight)
    else:
        wide = 3 * width + 2 * F
        shards = (
            norm_gains,
            norm_shifts,
            mixing_weight,
            mixing_offset[None],
            feature_maps,
            output_weight,
            branch_offsets,
            expand_weight,
            hidden_offset[None],
            shrink_weight,
        )
        at = lambda i: (0, 0)
        first, rest = call(
            shards_kernel,
            (1,),
            [(array, array.shape, at) for array in shards],
            [
                ((share, wide), bf16, (share, wide), at, True),
                ((9, share, width), bf16, (9, share, width), lambda i: (0, 0, 0)),
            ],
            [pltpu.VMEM((share, F), f32)],
            0,
            "shards",
            2,
        )
        layers = [first] + [swap(first, k, "batch", "first_layer") for k in range(1, 4)]
        near, far = jnp.stack(layers[:2]), jnp.stack(layers[2:])
        rest = lax.all_gather(rest, AXES)
        near = jnp.concatenate([near, swap(near, 2, name="first_x1")])
        far = jnp.concatenate([far, swap(far, 4, name="first_y1")])
        first = [
            near,
            swap(near, 4, name="first_y2"),
            far,
            swap(far, 2, name="first_x2"),
        ]
        first = gather_cores(first, "first_core")
        (first_weight,) = place(
            first, ids, ((0, 0, wide, None),), ((share, wide),), "place_first", 5
        )
        first_weight = first_weight.reshape(width, -1)
        *rows_out, offset, hidden_bias = call(
            functools.partial(unpack_kernel, devices),
            (1,),
            [(first_weight, (width, F), lambda i: (0, 3 * width // F + 1))],
            [
                ((n, length), f32, (n, length), lambda i: (0, 0))
                for n, length in [(1, width)] * 6 + [(1, 3 * width), (1, hidden_width)]
            ],
            [],
            0,
            "unpack",
            2,
        )
        gains, shifts, branches = (rows_out[i : i + 2] for i in (0, 2, 4))

    tok = tokens.reshape(count, width)
    cot = cotangent.reshape(count, width)
    full = lambda r, q, *s: (0, 0)

    def columns(first):
        return lambda r, q, *s: (0, first + q)

    own = lambda r, q, *s: (r, 0)
    cell = lambda r, q, *s: (r, q)
    normed, turned, keys, values, phi_key, wire = call(
        keys_kernel,
        (row_count, quads),
        [
            *scalars,
            (tok, (tok_count, width), own),
            (gains[0], (1, width), full),
            (shifts[0], (1, width), full),
            (first_weight, (width, quad), columns(quads)),
            (first_weight, (width, quad), columns(2 * quads)),
            (offset, (1, quad), columns(quads)),
            (offset, (1, quad), columns(2 * quads)),
            (first_weight, (quad, F), lambda r, q, *s: (q, 3 * width // F)),
        ],
        [
            ((count, width), bf16, (tok_count, width), own),
            ((width, count), bf16, (width, tok_count), lambda r, q, *s: (0, r)),
            ((count, width), bf16, (tok_count, quad), cell),
            ((count, width), bf16, (tok_count, quad), cell),
            ((count, heads * F), bf16, (tok_count, 4 * F), cell),
            (
                (row_count, pairs, WIRE, F),
                bf16,
                (1, 2, WIRE, F),
                lambda r, q, *s: (r, q, 0, 0),
            ),
        ],
        [pltpu.VMEM((tok_count, width), bf16)],
        2,
        "keys",
        15,
        flags,
    )
    queries, phi_query = call(
        queries_kernel,
        (row_count, quads),
        [
            (normed, (tok_count, width), own),
            (first_weight, (width, quad), columns(0)),
            (offset, (1, quad), columns(0)),
            (first_weight, (quad, F), lambda r, q, *s: (q, 3 * width // F)),
        ],
        [
            ((count, width), bf16, (tok_count, quad), cell),
            ((count, heads * F), bf16, (tok_count, 4 * F), cell),
        ],
        [],
        0,
        "queries",
        8,
    )
    total, came = carry(wire, [], flags, 0, False)
    total, came = carry(total, came, flags, 1, False, (phi_query,))
    (numerator,) = call(
        attention_kernel,
        (row_count, quads),
        [
            *scalars,
            (phi_query, (tok_count, 4 * F), cell),
            (phi_key, (tok_count, 4 * F), cell),
            (values, (tok_count, quad), cell),
        ],
        [((count, heads * F), f32, (tok_count, 4 * F), cell)],
        [],
        2,
        "attention",
        12,
        (total,),
    )
    for level in range(2, levels):
        total, came = carry(total, came, flags, level, False, (numerator,))

    def states(came, pairs_of, index):
        wires = [
            (wire, (1, pairs_of, WIRE, F), lambda *i: (*index(*i), 0, 0)) for wire, _ in came
        ]
        reaches = [
            (reach, (1, 1, 1, F), lambda *i: (index(*i)[0], 0, 0, 0)) for _, reach in came
        ]
        return wires + reaches

    memories = came
    if plain:
        out_part = (out_weight, (width, width), lambda r, *s: (0, 0))
        expand_part = (expand, (width, width), lambda f, *s: (0, f))
        shrink_part = (shrink, (width, width), lambda f, *s: (f, 0))
    else:
        cut = (devices, 1, share, width)
        out_part = (rest, cut, lambda r, *s: (0, 8, 0, 0))
        expand_part = (rest, cut, lambda f, *s: (0, f, 0, 0))
        cut = (devices // 4, 4, share, width)
        shrink_part = (rest, cut, lambda f, *s: (f, 1, 0, 0))
    whole = lambda r, *s: (0, 0)
    one = lambda r, *s: (r, 0)
    attended, inverse, middle, normed_mid = call(
        functools.partial(middle_kernel, len(memories)),
        (row_count,),
        [
            *scalars,
            (numerator, (tok_count, heads * F), one),
            (phi_query, (tok_count, heads * F), one),
            (tok, (tok_count, width), one),
            out_part,
            (branches[0], (1, width), whole),
            (gains[1], (1, width), whole),
            (shifts[1], (1, width), whole),
            *states(memories, pairs, lambda r, *s: (r, 0)),
        ],
        [
            ((count, width), bf16, (tok_count, width), one),
            ((count, width), bf16, (tok_count, width), one),
            ((count, width), f32, (tok_count, width), one),
            ((count, width), bf16, (tok_count, width), one),
        ],
        [],
        2,
        "middle",
        9,
    )
    tile = width
    steps = hidden_width // tile

    def halves(wide, block, index):
        if plain:
            return [((width, wide), f32, (width, block), lambda *i: (0, index(*i)))]
        shape = (devices // 2, share, wide)
        cut = (devices // 2, share, block)
        return [(shape, bf16, cut, lambda *i: (0, 0, index(*i)), True)] * 2

    layer_output, normed_mid_back, hidden_grad, *mlp_grads = call(
        functools.partial(mlp_kernel, plain),
        (steps,),
        [
            *scalars,
            (normed_mid, (count, width), lambda f, *s: (0, 0)),
            (cot, (count, width), lambda f, *s: (0, 0)),
            expand_part,
            shrink_part,
            (hidden_bias, (1, tile), lambda f, *s: (0, f)),
            (branches[1], (1, width), whole),
            (middle, None, None),
        ],
        [
            ((count, width), bf16, (count, width), lambda f, *s: (0, 0)),
            ((count, width), bf16, (count, width), lambda f, *s: (0, 0)),
            ((1, hidden_width), f32, (1, tile), lambda f, *s: (0, f)),
            *halves(hidden_width, tile, lambda f, *s: f),
            *(
                [((hidden_width, width), f32, (tile, width), lambda f, *s: (f, 0))]
                if plain
                else [
                    (
                        (devices // 2, share, 4 * width),
                        bf16,
                        (devices // 2 // steps, share, 4 * width),
                        lambda f, *s: (f, 0, 0),
                        True,
                    )
                ]
                * 2
            ),
        ],
        [pltpu.VMEM((width, count), bf16)]
        + [pltpu.VMEM((count, width), f32)] * 3
        + [pltpu.SemaphoreType.DMA],
        2,
        "mlp",
        37,
    )
    middle_back, extended, wire_back, small_mid, *output_grads = call(
        functools.partial(middle_back_kernel, 1),
        (row_count,),
        [
            *scalars,
            (middle, (tok_count, width), one),
            (normed_mid_back, (tok_count, width), one),
            (cot, (tok_count, width), one),
            (attended, (tok_count, width), one),
            (inverse, (tok_count, width), one),
            (phi_query, (tok_count, heads * F), one),
            out_part,
            (gains[1], (1, width), whole),
        ],
        [
            ((count, width), bf16, (tok_count, width), one),
            ((count, heads * F), bf16, (tok_count, heads * F), one),
            ((row_count, pairs, WIRE, F), bf16, (1, pairs, WIRE, F), lambda r, *s: (r, 0, 0, 0)),
            ((8, width), f32, (8, width), whole),
            *halves(width, width, lambda r, *s: 0),
        ],
        [pltpu.VMEM((width, width), f32), pltpu.VMEM((heads, F, F), f32)],
        2,
        "middle_back",
        17,
    )
    total, came = carry(wire_back, [], flags, 0, True)
    if not plain:
        expand_mine, expand_other, shrink_mine, shrink_other = mlp_grads
        mlp_waits = first_sum(
            (expand_mine, shrink_mine),
            (swap(expand_other, 1, name="mlp_core"), swap(shrink_other, 1, name="mlp_core")),
            ids,
            "mlp_first_sum",
            7,
            (wire_back,),
        )
    cell = lambda p, r, *s: (r, p)
    of_pair = lambda p, r, *s: (p, 0)
    from_wire = lambda p, r, *s: (r, p, 0, 0)

    def attend_back(first, into=(), waits=()):
        cell = lambda p, r, *s: (r + first, p)
        return call(
            functools.partial(local_back_kernel, first, len(memories)),
            (quads, 1),
            [
                *scalars,
                (phi_query, (tok_count, 4 * F), cell),
                (phi_key, (tok_count, 4 * F), cell),
                (values, (tok_count, quad), cell),
                (extended, (tok_count, 4 * F), cell),
                (queries, (tok_count, quad), cell),
                (first_weight, (quad, F), lambda p, r, *s: (p, 3 * width // F)),
                *states(memories, 2, lambda p, r, *s: (r + first, p)),
            ],
            [
                ((count, width), bf16, (tok_count, quad), cell),
                ((count, heads * F), bf16, (tok_count, 4 * F), cell),
                ((count, width), bf16, (tok_count, quad), cell),
                ((width, F), f32, (quad, F), of_pair),
            ],
            [],
            2,
            "local_back",
            25 / row_count,
            waits,
            into,
        )

    partial, maps_query = (), []
    for level in range(1, levels):
        if level <= row_count:
            waits = (total, *(mlp_waits[:1] if level == 1 and not plain else ()))
            *partial, map_query = attend_back(level - 1, partial, waits)
            maps_query.append(map_query)
        total, came = carry(total, came, flags, level, True, partial[:1])
        if level == 1 and not plain:
            mlp_waits = [mlp_waits[0], *tie(mlp_waits[1:2], total), *mlp_waits[2:]]
    for first in range(levels - 1, row_count):
        *partial, map_query = attend_back(first, partial)
        maps_query.append(map_query)
    queries_back, key_feat, value_feat = partial

    def weight_back(pb, waits=()):
        return call(
            weight_back_kernel,
            (quads,),
            [
                *scalars,
                (turned, (width, count), lambda q, *s: (0, 0)),
                (pb, (count, quad), lambda q, *s: (0, q)),
            ],
            halves(width, quad, lambda q, *s: q),
            [],
            2,
            "weight_back",
            5,
            waits,
        )

    query_grads = weight_back(queries_back)

    def attend_keys_back(first, map_grads, into=(), waits=()):
        cell = lambda p, r, *s: (r + first, p)
        return call(
            functools.partial(keys_back_kernel, first, len(came)),
            (quads, 1),
            [
                *scalars,
                (key_feat, (tok_count, 4 * F), cell),
                (value_feat, (tok_count, quad), cell),
                (phi_key, (tok_count, 4 * F), cell),
                (values, (tok_count, quad), cell),
                (keys, (tok_count, quad), cell),
                (first_weight, (quad, F), lambda p, r, *s: (p, 3 * width // F)),
                *states(came, 2, lambda p, r, *s: (r + first, p)),
                *[(map_grad, (quad, F), of_pair) for map_grad in map_grads],
            ],
            [
                ((count, width), bf16, (tok_count, quad), cell),
                ((count, width), bf16, (tok_count, quad), cell),
                ((width, F), f32, (quad, F), of_pair),
            ],
            [],
            2,
            "keys_back",
            13 / row_count,
            waits,
            into,
        )

    *partial, map_grad = attend_keys_back(0, maps_query, (), query_grads[:1])
    if not plain:
        mlp_sums = middle_sum(mlp_waits, "mlp_middle_sum", 4, partial[:1])
    for first in range(1, row_count):
        waits = () if plain else mlp_sums[:1]
        *partial, map_grad = attend_keys_back(first, [map_grad], partial, waits)
    keys_back, values_back = partial
    value_grads = weight_back(values_back)
    if not plain:
        mlp_sums = second_sum(mlp_sums, "mlp_second_sum", 4, value_grads[:1], False)
        query_waits = first_sum(
            (query_grads[0], output_grads[0], value_grads[0]),
            (
                swap(query_grads[1], 1, name="query_core"),
                swap(output_grads[1], 1, name="query_core"),
                swap(value_grads[1], 1, name="query_core"),
            ),
            ids,
            "query_first_sum",
            3,
            mlp_sums[:1],
        )
    row = lambda r: (r, 0)
    fixed = lambda r: (0, 0)
    input_gradient, small_in = call(
        input_back_kernel,
        (count // SUB,),
        [
            (queries_back, (SUB, width), row),
            (keys_back, (SUB, width), row),
            (values_back, (SUB, width), row),
            (first_weight, (width, width), lambda r: (0, 0)),
            (first_weight, (width, width), lambda r: (0, 1)),
            (first_weight, (width, width), lambda r: (0, 2)),
            (tok, (SUB, width), row),
            (middle_back, (SUB, width), row),
            (gains[0], (1, width), fixed),
        ],
        [
            ((count, width), bf16, (SUB, width), row),
            ((8, width), f32, (8, width), fixed),
        ],
        [],
        0,
        "input_back",
        10,
        () if plain else query_waits[:1],
    )
    if not plain:
        query_sums = middle_sum(query_waits, "query_middle_sum", 2, (input_gradient,))
    small_parts = [
        (array, array.shape, lambda q, *s: (0, 0))
        for array in (small_in, small_mid, hidden_grad, map_grad)
    ]
    key_grads = call(
        functools.partial(key_weight_back_kernel, quads, 0 if plain else devices),
        (quads + (0 if plain else 1),),
        [
            *scalars,
            (turned, (width, count), lambda q, *s: (0, 0)),
            (keys_back, (count, quad), lambda q, *s: (0, jnp.minimum(q, quads - 1))),
            *small_parts,
        ],
        halves(width + (0 if plain else quad), quad, lambda q, *s: q),
        [pltpu.VMEM((devices, share, F), f32)],
        2,
        "key_weight_back",
        10,
        () if plain else query_sums[:1],
    )
    if plain:
        mixing_grad = jnp.concatenate([query_grads[0], key_grads[0], value_grads[0]], axis=1)
        offset_grad = small_in[2:5].reshape(-1)
        grads = (
            scatter_columns(jnp.stack([small_in[0], small_mid[0]])),
            scatter_columns(jnp.stack([small_in[1], small_mid[1]])),
            scatter_rows(mixing_grad),
            scatter_rows(offset_grad),
            scatter_rows(map_grad),
            scatter_rows(output_grads[0]),
            scatter_columns(small_mid[2:4]),
            scatter_rows(mlp_grads[0]),
            scatter_rows(hidden_grad[0]),
            scatter_rows(mlp_grads[1]),
        )
    else:
        query_sums = second_sum(query_sums, "query_second_sum", 3, (key_grads[0],), False)
        mlp_pair = reduce_layer1(mlp_sums, "mlp", query_sums[:1])
        key_sums = first_sum(
            (key_grads[0],),
            (swap(key_grads[1], 1, name="key_core"),),
            ids,
            "key_first_sum",
            4,
            (mlp_pair,),
        )
        query_pair = reduce_layer1(query_sums, "query", key_sums[:1])
        key_sums = middle_sum(key_sums, "key_middle_sum", 2, (query_pair,))
        key_sums = second_sum(key_sums, "key_second_sum")
        mlp_total = reduce_layer2(mlp_pair, "mlp", key_sums[:1])
        query_total = reduce_layer2(query_pair, "query", key_sums[:1])
        key_total = reduce_batch(key_sums, "key")
        small_total = key_total[0:8, width + F :]
        mixing_grad = jnp.concatenate(
            [query_total[:, :width], key_total[:, :width], query_total[:, 2 * width :]], axis=1
        )
        shrink_grad = mlp_total[:, hidden_width:].reshape(share, 4, width)
        grads = (
            small_total[0:2, :share],
            small_total[2:4, :share],
            mixing_grad,
            small_total[6, : 3 * share],
            key_total[:, width : width + F],
            query_total[:, width : 2 * width],
            small_total[4:6, :share],
            mlp_total[:, :hidden_width],
            small_total[7, : 4 * share],
            shrink_grad.transpose(1, 0, 2).reshape(4 * share, width),
        )
    return (layer_output.reshape(tokens.shape), input_gradient.reshape(tokens.shape), *grads)


def solution(mesh):
    rows = P("batch", "seq", None)
    split_rows = P(AXES, None)
    split_columns = P(None, AXES)
    split_vector = P(AXES)
    return jax.shard_map(
        local,
        mesh=mesh,
        in_specs=(
            rows,
            P("batch", None),
            split_columns,
            split_columns,
            split_rows,
            split_vector,
            split_rows,
            split_rows,
            split_columns,
            split_rows,
            split_vector,
            split_rows,
            rows,
        ),
        out_specs=(
            rows,
            rows,
            split_columns,
            split_columns,
            split_rows,
            split_vector,
            split_rows,
            split_rows,
            split_columns,
            split_rows,
            split_vector,
            split_rows,
        ),
        check_vma=False,
    )
```
